32 devices in a mesh: tm: 8 (over z, x), space: 4 (over y, core).
Axes of the slice: x: 2, y: 2, z: 4, core: 2. Of those that a mesh axis runs over, the one named last changes fastest.
Arguments:
- start_block: float32 [8, 2, 3, 32, 32, 256], P('tm', None, None, None, 'space'), may hold values from -6 to 6
- gauge_links: float32 [8, 3, 2, 3, 3, 32, 256], P('tm', None, None, None, None, 'space'), may hold values from -1 to 1, as said below
- stored_vectors: bfloat16 [8, 448, 2, 3, 32, 256], P('tm', None, None, None, 'space'), may hold values from -0.02734375 to 0.02734375
Outputs:
- correlations: float32 [8, 448, 64], P('tm', 'space')
- solver_blocks: bfloat16 [8, 32, 256, 192], P('space', None, 'tm')
The draws below stay inside these ranges and needn't reach their ends.
Inputs may be any that keep to these rules, and one draw needn't show every extreme that they name: Every link matrix gauge_links[t, mu, 0] + i gauge_links[t, mu, 1] at a site is special unitary, drawn independently at every site and direction.
All inputs are finite; a program needn't handle non-finite values.
Results may differ from the reference program's by a relative error of at most 0.0029.
Values may be sent and summed in bfloat16 or wider, within the bound.
No kernel may reach another device: no remote copies, remote signals or barrier semaphores. Data moves between devices by JAX's collectives and lax.ppermute only.
A program may use at most 128 MiB of HBM per device.

```python
import jax
import jax.numpy as jnp
from jax import lax

NVEC = 32
NSTORE = 448
DEGREE = 4
LY = 16
LZ = 16
NX = 32
LYZ = 256
NT = 8


def draw_gauge_links(key, part):
    keys = jax.random.split(jax.random.fold_in(key, 17), 2)
    shape = (3, 3, NT, 3, NX, LY * LZ)
    real_part = jax.random.uniform(keys[0], shape, jnp.float32, -1.0, 1.0)
    imag_part = jax.random.uniform(keys[1], shape, jnp.float32, -1.0, 1.0)
    real_part = real_part + 3.0 * jnp.eye(3, dtype=jnp.float32)[:, :, None, None, None, None]
    first_re, first_im = (real_part[0], imag_part[0])
    second_re, second_im = (real_part[1], imag_part[1])
    first_scale = lax.rsqrt(jnp.sum(first_re * first_re + first_im * first_im, axis=0) + 1e-12)
    first_re = first_re * first_scale
    first_im = first_im * first_scale
    proj_re = jnp.sum(first_re * second_re + first_im * second_im, axis=0)
    proj_im = jnp.sum(first_re * second_im - first_im * second_re, axis=0)
    second_re = second_re - (proj_re * first_re - proj_im * first_im)
    second_im = second_im - (proj_re * first_im + proj_im * first_re)
    second_scale = lax.rsqrt(jnp.sum(second_re * second_re + second_im * second_im, axis=0) + 1e-12)
    second_re = second_re * second_scale
    second_im = second_im * second_scale

    def product_re(col_a, col_b):
        return first_re[col_a] * second_re[col_b] - first_im[col_a] * second_im[col_b]

    def product_im(col_a, col_b):
        return first_re[col_a] * second_im[col_b] + first_im[col_a] * second_re[col_b]
    third_re = jnp.stack([product_re(1, 2) - product_re(2, 1), product_re(2, 0) - product_re(0, 2), product_re(0, 1) - product_re(1, 0)], axis=0)
    third_im = -jnp.stack([product_im(1, 2) - product_im(2, 1), product_im(2, 0) - product_im(0, 2), product_im(0, 1) - product_im(1, 0)], axis=0)
    rows_re = jnp.stack([first_re, second_re, third_re], axis=0)
    rows_im = jnp.stack([first_im, second_im, third_im], axis=0)
    stacked = jnp.stack([rows_re, rows_im], axis=0)
    return jnp.transpose(stacked, (3, 4, 0, 1, 2, 5, 6)).astype(jnp.float32)


def steps_of(rng, extent, cuts, low, largest):
    def one(axis_at, shards_of):
        draws = jax.random.uniform(jax.random.fold_in(jax.random.fold_in(rng, 6), axis_at), (shards_of,), jnp.float32, low / len(cuts), largest / len(cuts))
        return jnp.repeat(jnp.exp(draws), extent[axis_at] // shards_of).reshape((-1,) + (1,) * (len(extent) - axis_at - 1))

    factor_of = one(*cuts[0])
    for cut in cuts[1:]:
        factor_of = factor_of * one(*cut)
    return factor_of


def normal_values(rng, extent, scale, limit, shards=(), kind=jnp.bfloat16):
    loudness = steps_of(rng, extent, shards, -0.22, 0.18) if shards else 1.0
    entries = jax.random.normal(rng, extent, jnp.float32) * scale * loudness
    return jnp.minimum(jnp.maximum(entries, -limit), limit).astype(kind)


def setup_inputs(seed: int = 0) -> dict:
    streams_of = jax.random.split(jax.random.key(seed), 4)
    start_block = normal_values(streams_of[0], (NT, 2, 3, NVEC, NX, LYZ), 1.0, 6.0, ((0, 8), (4, 4)), jnp.float32)
    gauge_links = draw_gauge_links(jax.random.fold_in(streams_of[3], 71), 0)
    stored_vectors = normal_values(streams_of[2], (NT, NSTORE, 2, 3, NX, LYZ), (6 * NX * LYZ) ** -0.5, 0.02734375, ((0, 8), (4, 4)))
    return {"start_block": start_block, "gauge_links": gauge_links, "stored_vectors": stored_vectors}


lower_edge = 0.5
upper_edge = 12.5


def contract(matrix, vector):
    return jnp.sum(matrix[:, :, :, None] * vector[:, None], axis=2)


def complex_apply(link, source):
    link_re, link_im = link[:, 0], link[:, 1]
    src_re, src_im = source[:, 0], source[:, 1]
    out_re = contract(link_re, src_re) - contract(link_im, src_im)
    out_im = contract(link_re, src_im) + contract(link_im, src_re)
    return jnp.stack([out_re, out_im], axis=1)


def dagger(link):
    return jnp.stack([jnp.swapaxes(link[:, 0], 1, 2), -jnp.swapaxes(link[:, 1], 1, 2)], axis=1)


def z_forward(values):
    along_z = lax.broadcasted_iota(jnp.int32, values.shape, values.ndim - 1) % LZ
    return jnp.where(along_z == LZ - 1, jnp.roll(values, LZ - 1, axis=-1), jnp.roll(values, -1, axis=-1))


def z_backward(values):
    along_z = lax.broadcasted_iota(jnp.int32, values.shape, values.ndim - 1) % LZ
    return jnp.where(along_z == 0, jnp.roll(values, -(LZ - 1), axis=-1), jnp.roll(values, 1, axis=-1))


def laplace_interior(source, links):
    center = source[..., 1:-1, :]
    inner_links = links[..., 1:-1, :]
    link_y = inner_links[:, 1]
    link_z = inner_links[:, 2]
    hopping = complex_apply(inner_links[:, 0], source[..., 2:, :])
    hopping = hopping + complex_apply(dagger(links[:, 0, ..., :-2, :]), source[..., :-2, :])
    hopping = hopping + complex_apply(link_y, jnp.roll(center, -LZ, axis=-1))
    hopping = hopping + complex_apply(dagger(jnp.roll(link_y, LZ, axis=-1)), jnp.roll(center, LZ, axis=-1))
    hopping = hopping + complex_apply(link_z, z_forward(center))
    hopping = hopping + complex_apply(dagger(z_backward(link_z)), z_backward(center))
    return 6.0 * center - hopping


def cheb_apply(source, links):
    scale_term = 2.0 / (upper_edge - lower_edge)
    offset_term = (upper_edge + lower_edge) / (upper_edge - lower_edge)
    return scale_term * laplace_interior(source, links) - offset_term * source[..., 1:-1, :]


def wrap_pad(values):
    return jnp.concatenate([values[..., -1:, :], values, values[..., :1, :]], axis=-2)


def filter_slice(inputs):
    block_slice, link_slice = inputs
    link_pad = wrap_pad(link_slice[None])
    prev_term = block_slice[None]
    this_term = cheb_apply(wrap_pad(prev_term), link_pad)
    for level in range(1, DEGREE):
        next_term = 2.0 * cheb_apply(wrap_pad(this_term), link_pad) - prev_term
        prev_term, this_term = this_term, next_term
    return this_term[0]


def correlation_slice(inputs):
    stored_slice, half_slice = inputs
    vectors = half_slice.astype(jnp.float32)
    turned = jnp.stack([vectors[1], -vectors[0]], axis=0)
    stacked = jnp.stack([vectors, turned], axis=0)
    result = jnp.einsum("srcxy,prcvxy->spv", stored_slice.astype(jnp.float32), stacked, precision=lax.Precision.HIGHEST)
    return result.reshape(NSTORE, 2 * NVEC)


def reference(start_block, gauge_links, stored_vectors):
    filtered = lax.map(filter_slice, (start_block, gauge_links))
    filtered_half = filtered.astype(jnp.bfloat16)
    correlations = lax.map(correlation_slice, (stored_vectors, filtered_half))
    solver_blocks = jnp.transpose(filtered_half, (0, 4, 5, 1, 2, 3)).reshape(NT, NX, LYZ, 6 * NVEC)
    return correlations, solver_blocks
```

```python
import functools

import jax
import jax.numpy as jnp
from jax import lax
from jax.experimental import pallas as pl
from jax.experimental.pallas import tpu as pltpu
from jax.sharding import PartitionSpec as P

DEGREE = 4
LZ = 16
LANES = 128
VB = 16

lower_edge = 0.5
upper_edge = 12.5
SCALE = 2.0 / (upper_edge - lower_edge)
OFFSET = (upper_edge + lower_edge) / (upper_edge - lower_edge)

VMEM_LIMIT = 60 * 2**20
LINK_ROWS = 54
LINK_PAD = 56
TABLE_ROWS = 112
GAUGE_ROWS = 24
GROUPS = ((0,), (1,))


def params():
    return pltpu.CompilerParams(vmem_limit_bytes=VMEM_LIMIT)


def pack_kernel(start_ref, halo_ref, *, layers, comps, tiles):
    for x in range(layers):
        for k in range(comps):
            for t in range(tiles):
                halo_ref[x, k, :, t * LANES : (t + 1) * LANES] = start_ref[
                    k, pl.ds(t * layers + x, VB, stride=tiles * layers), :
                ].astype(jnp.bfloat16)


def pack_halo(start2, layers, tiles):
    comps, rows, _ = start2.shape
    cells = VB * layers * tiles
    groups = rows // cells
    planes = tiles * LANES
    return pl.pallas_call(
        functools.partial(pack_kernel, layers=layers, comps=comps, tiles=tiles),
        grid=(groups,),
        in_specs=[pl.BlockSpec((comps, cells, LANES), lambda g: (0, g, 0))],
        out_specs=pl.BlockSpec(
            (layers, pl.Squeezed(), comps, VB, planes), lambda g: (0, g, 0, 0, 0)
        ),
        out_shape=jax.ShapeDtypeStruct((layers, groups, comps, VB, planes), jnp.bfloat16),
        compiler_params=params(),
        name="pack_halo",
    )(start2)


def pack_links_kernel(links_ref, own_ref, half_ref, *, layers, tiles):
    for x in range(layers):
        for t in range(tiles):
            rows = links_ref[pl.ds(t * layers + x, LINK_ROWS, stride=tiles * layers), :]
            own_ref[x, :, t * LANES : (t + 1) * LANES] = rows
            half_ref[x, :, t * LANES : (t + 1) * LANES] = rows.astype(jnp.bfloat16)


def pack_links(links2, layers, tiles):
    planes = tiles * LANES
    return pl.pallas_call(
        functools.partial(pack_links_kernel, layers=layers, tiles=tiles),
        out_shape=(
            jax.ShapeDtypeStruct((layers, LINK_ROWS, planes), jnp.float32),
            jax.ShapeDtypeStruct((layers, LINK_ROWS, planes), jnp.bfloat16),
        ),
        compiler_params=params(),
        name="pack_links",
    )(links2)


def mat_mul(a, b, conj_b=False):
    out_re, out_im = [], []
    for i in range(3):
        for j in range(3):
            re = im = None
            for k in range(3):
                ar, ai = a[0][3 * i + k], a[1][3 * i + k]
                if conj_b:
                    br, bi = b[0][3 * j + k], b[1][3 * j + k]
                    r = ar * br + ai * bi
                    m = ai * br - ar * bi
                else:
                    br, bi = b[0][3 * k + j], b[1][3 * k + j]
                    r = ar * br - ai * bi
                    m = ar * bi + ai * br
                re = r if re is None else re + r
                im = m if im is None else im + m
            out_re.append(re)
            out_im.append(im)
    return out_re, out_im


def rot(v, steps):
    return pltpu.roll(v, steps % LANES, 1)


def shifts(value, masks):
    z_last, z_first, y_low, y_high = masks
    tiles = len(value)
    up = [rot(v, LZ) for v in value]
    down = [rot(v, -LZ) for v in value]
    return (
        [jnp.where(y_low, down[t], down[(t + 1) % tiles]) for t in range(tiles)],
        [jnp.where(y_high, up[t], up[(t - 1) % tiles]) for t in range(tiles)],
        [rot(jnp.where(z_first, up[t], value[t]), -1) for t in range(tiles)],
        [rot(jnp.where(z_last, down[t], value[t]), 1) for t in range(tiles)],
    )


def lane_masks(rows):
    lane = lax.broadcasted_iota(jnp.int32, (rows, LANES), 1)
    return lane % LZ == LZ - 1, lane % LZ == 0, lane < LANES - LZ, lane >= LZ


def gauge_kernel(own_ref, lo_ref, hi_ref, table_ref, gauge_ref, ext_ref, g_ref, t_ref, *, layers):
    total = layers + 2 * DEGREE
    tiles = own_ref.shape[-1] // LANES

    def cols(t):
        return slice(t * LANES, (t + 1) * LANES)

    for t in range(tiles):
        for x in range(total):
            if x < DEGREE:
                rows = lo_ref[x, :, cols(t)].astype(jnp.float32)
            elif x < DEGREE + layers:
                rows = own_ref[x - DEGREE, :, cols(t)]
            else:
                rows = hi_ref[x - DEGREE - layers, :, cols(t)].astype(jnp.float32)
            ext_ref[t, pl.ds(x * LINK_PAD, LINK_ROWS), :] = rows

    one = jnp.ones((1, LANES), jnp.float32)
    zero = jnp.zeros((1, LANES), jnp.float32)
    unit = ([one if k % 4 == 0 else zero for k in range(9)], [zero] * 9)
    for t in range(tiles):

        def link_row(x):
            return (
                [ext_ref[t, pl.ds(x * LINK_PAD + k, 1), :] for k in range(9)],
                [ext_ref[t, pl.ds(x * LINK_PAD + 9 + k, 1), :] for k in range(9)],
            )

        def put_gauge(x, g):
            for k in range(9):
                g_ref[t, pl.ds(x * GAUGE_ROWS + k, 1), :] = g[0][k]
                g_ref[t, pl.ds(x * GAUGE_ROWS + 9 + k, 1), :] = g[1][k]

        put_gauge(DEGREE, unit)
        g = unit
        for x in range(DEGREE, total - 1):
            g = mat_mul(g, link_row(x))
            put_gauge(x + 1, g)
        g = unit
        for x in range(DEGREE - 1, -1, -1):
            g = mat_mul(g, link_row(x), conj_b=True)
            put_gauge(x, g)
        for x in range(total):
            gauge_ref[x, 0:18, cols(t)] = g_ref[t, pl.ds(x * GAUGE_ROWS, 18), :]

    masks = lane_masks(total)

    def column(ref, k, stride):
        return [ref[t, pl.ds(k, total, stride=stride), :] for t in range(tiles)]

    gauge = [column(g_ref, k, GAUGE_ROWS) for k in range(18)]
    for d in (1, 2):
        link = [column(ext_ref, 18 * d + k, LINK_PAD) for k in range(18)]
        ahead = [shifts(v, masks)[2 * (d - 1)] for v in gauge]
        turned = []
        for t in range(tiles):
            here, there, mid = (
                ([v[t] for v in field[:9]], [v[t] for v in field[9:]])
                for field in (gauge, ahead, link)
            )
            turned.append(mat_mul(mat_mul(here, mid), there, conj_b=True))
        base = 54 * (d - 1)
        for k in range(9):
            re, im = [turned[t][0][k] for t in range(tiles)], [turned[t][1][k] for t in range(tiles)]
            back_re, back_im = shifts(re, masks)[2 * d - 1], shifts(im, masks)[2 * d - 1]
            for t in range(tiles):
                for at, value in (
                    (0, re[t]),
                    (9, re[t] + im[t]),
                    (18, im[t] - re[t]),
                    (27, back_re[t]),
                    (36, back_re[t] + back_im[t]),
                    (45, back_im[t] - back_re[t]),
                ):
                    t_ref[t, pl.ds(base + at + k, total, stride=TABLE_ROWS), :] = value
    for x in range(total):
        for t in range(tiles):
            table_ref[x, 0:108, cols(t)] = t_ref[t, pl.ds(x * TABLE_ROWS, 108), :]


def gauge_tables(own, lo, hi):
    layers, _, planes = own.shape
    total = layers + 2 * DEGREE
    tiles = planes // LANES
    return pl.pallas_call(
        functools.partial(gauge_kernel, layers=layers),
        out_shape=(
            jax.ShapeDtypeStruct((total, TABLE_ROWS, planes), jnp.float32),
            jax.ShapeDtypeStruct((total, GAUGE_ROWS, planes), jnp.float32),
        ),
        scratch_shapes=[
            pltpu.VMEM((tiles, total * LINK_PAD, LANES), jnp.float32),
            pltpu.VMEM((tiles, total * GAUGE_ROWS, LANES), jnp.float32),
            pltpu.VMEM((tiles, total * TABLE_ROWS, LANES), jnp.float32),
        ],
        compiler_params=params(),
        name="gauge_tables",
    )(own, lo, hi)


def filter_kernel(
    place_ref, start_ref, lo_ref, hi_ref, table_ref, gauge_ref,
    half_ref, keep_ref, give_ref, a_ref, b_ref, pack_ref, *, layers, parts
):
    total = layers + 2 * DEGREE
    planes = table_ref.shape[-1]
    tiles = planes // LANES
    z_last, z_first, y_low, y_high = lane_masks(VB)

    def cols(t):
        return slice(t * LANES, (t + 1) * LANES)

    def turn(x, source, adjoint):
        out = {}
        for t in range(tiles):
            v = [source(k, t) for k in range(6)]
            for i in range(3):
                re = im = None
                for j in range(3):
                    k = 3 * j + i if adjoint else 3 * i + j
                    a = gauge_ref[x, pl.ds(k, 1), cols(t)]
                    b = gauge_ref[x, pl.ds(9 + k, 1), cols(t)]
                    if adjoint:
                        r, m = a * v[j] + b * v[3 + j], a * v[3 + j] - b * v[j]
                    else:
                        r, m = a * v[j] - b * v[3 + j], a * v[3 + j] + b * v[j]
                    re = r if re is None else re + r
                    im = m if im is None else im + m
                out[i, t], out[3 + i, t] = re, im
        return out

    def own_init(x, _):
        def source(k, t):
            return start_ref[k, pl.ds(t * layers + x, VB, stride=tiles * layers), :]

        out = turn(x + DEGREE, source, False)
        for (k, t), value in out.items():
            a_ref[x + DEGREE, k, :, cols(t)] = value
        return 0

    lax.fori_loop(0, layers, own_init, 0)

    def lo_init(x, _):
        out = turn(x, lambda k, t: lo_ref[x, k, :, cols(t)].astype(jnp.float32), False)
        for (k, t), value in out.items():
            a_ref[x, k, :, cols(t)] = value
        return 0

    lax.fori_loop(0, DEGREE, lo_init, 0)

    def hi_init(x, _):
        at = x + DEGREE + layers
        out = turn(at, lambda k, t: hi_ref[x, k, :, cols(t)].astype(jnp.float32), False)
        for (k, t), value in out.items():
            a_ref[at, k, :, cols(t)] = value
        return 0

    lax.fori_loop(0, DEGREE, hi_init, 0)

    def layer(x, src, prev, first):
        sums = {}

        def add(key, value, minus=False):
            have = sums.get(key)
            if have is None:
                sums[key] = -value if minus else value
            else:
                sums[key] = have - value if minus else have + value

        def hop(t, base, v, adjoint):
            both = [v[j] + v[3 + j] for j in range(3)]
            for j in range(3):
                for i in range(3):
                    k = base + (3 * j + i if adjoint else 3 * i + j)
                    a = table_ref[x, pl.ds(k, 1), cols(t)]
                    p = table_ref[x, pl.ds(k + 9, 1), cols(t)]
                    q = table_ref[x, pl.ds(k + 18, 1), cols(t)]
                    add((t, 0, i), a * both[j])
                    if adjoint:
                        add((t, 1, i), q * v[3 + j], True)
                        add((t, 2, i), p * v[j], True)
                    else:
                        add((t, 1, i), p * v[3 + j])
                        add((t, 2, i), q * v[j])

        c = {(k, t): src[x, k, :, cols(t)] for k in range(6) for t in range(tiles)}
        up = {key: rot(v, LZ) for key, v in c.items()}
        down = {key: rot(v, -LZ) for key, v in c.items()}
        out = {}
        for t in range(tiles):
            after, before = (t + 1) % tiles, (t - 1) % tiles
            hop(t, 0, [jnp.where(y_low, down[k, t], down[k, after]) for k in range(6)], False)
            hop(t, 27, [jnp.where(y_high, up[k, t], up[k, before]) for k in range(6)], True)
            hop(t, 54, [rot(jnp.where(z_first, up[k, t], c[k, t]), -1) for k in range(6)], False)
            hop(t, 81, [rot(jnp.where(z_last, down[k, t], c[k, t]), 1) for k in range(6)], True)
            for i in range(3):
                re = sums[t, 0, i] - sums[t, 1, i]
                im = sums[t, 0, i] + sums[t, 2, i]
                for k, h in ((i, re), (3 + i, im)):
                    h = h + src[x + 1, k, :, cols(t)] + src[x - 1, k, :, cols(t)]
                    if first:
                        out[k, t] = (6.0 * SCALE - OFFSET) * c[k, t] - SCALE * h
                    else:
                        out[k, t] = (
                            (12.0 * SCALE - 2.0 * OFFSET) * c[k, t]
                            - (2.0 * SCALE) * h
                            - prev[x, k, :, cols(t)]
                        )
        return out

    def apply(level, src, dst):
        def body(x, _):
            for (k, t), value in layer(x, src, dst, level == 1).items():
                dst[x, k, :, cols(t)] = value
            return 0

        lax.fori_loop(level, total - level, body, 0)

    for level in range(1, DEGREE):
        apply(level, a_ref if level % 2 else b_ref, b_ref if level % 2 else a_ref)
    src, prev = (a_ref, b_ref) if DEGREE % 2 else (b_ref, a_ref)

    def last(x, _):
        value = layer(x + DEGREE, src, prev, False)
        value = turn(x + DEGREE, lambda k, t: value[k, t], True)
        for (k, t), v in value.items():
            rounded = v.astype(jnp.bfloat16)
            half_ref[x, k, :, cols(t)] = rounded
            pack_ref[k, pl.ds(pl.multiple_of(x * VB, VB), VB), cols(t)] = rounded.astype(
                jnp.float32
            )
        return 0

    lax.fori_loop(0, layers, last, 0)

    me, shift = place_ref[0], place_ref[1]
    pairs = parts // 2
    width = planes // parts
    for k in range(6):
        turned = jnp.concatenate(
            [pack_ref[k, :, cols(t)].T for t in range(tiles)], axis=0
        )
        for m in range(pairs):
            even = turned[2 * m * width : (2 * m + 1) * width].astype(jnp.bfloat16)
            odd = turned[(2 * m + 1) * width : (2 * m + 2) * width].astype(jnp.bfloat16)
            at = lax.rem(m - shift + pairs, pairs)
            keep_ref[at, k] = jnp.where(me == 0, even, odd)
            give_ref[at, k] = jnp.where(me == 0, odd, even)


def run_filter(place, start2, lo, hi, table, gauge, first_group, count, layers, parts):
    comps = start2.shape[0]
    planes = table.shape[-1]
    total = layers + 2 * DEGREE
    width = planes // parts
    cells = layers * VB

    def out(*dims):
        return jax.ShapeDtypeStruct(dims, jnp.bfloat16)

    grid_spec = pltpu.PrefetchScalarGridSpec(
        num_scalar_prefetch=1,
        grid=(count,),
        in_specs=[
            pl.BlockSpec(
                (comps, cells * planes // LANES, LANES), lambda g, s: (0, first_group + g, 0)
            ),
            pl.BlockSpec((DEGREE, pl.Squeezed(), comps, VB, planes), lambda g, s: (0, g, 0, 0, 0)),
            pl.BlockSpec((DEGREE, pl.Squeezed(), comps, VB, planes), lambda g, s: (0, g, 0, 0, 0)),
            pl.BlockSpec((total, TABLE_ROWS, planes), lambda g, s: (0, 0, 0)),
            pl.BlockSpec((total, GAUGE_ROWS, planes), lambda g, s: (0, 0, 0)),
        ],
        out_specs=[
            pl.BlockSpec((pl.Squeezed(), layers, comps, VB, planes), lambda g, s: (g, 0, 0, 0, 0)),
            pl.BlockSpec((parts // 2, pl.Squeezed(), comps, width, cells), lambda g, s: (0, g, 0, 0, 0)),
            pl.BlockSpec((parts // 2, pl.Squeezed(), comps, width, cells), lambda g, s: (0, g, 0, 0, 0)),
        ],
        scratch_shapes=[
            pltpu.VMEM((total, comps, VB, planes), jnp.float32),
            pltpu.VMEM((total, comps, VB, planes), jnp.float32),
            pltpu.VMEM((comps, cells, planes), jnp.float32),
        ],
    )
    return pl.pallas_call(
        functools.partial(filter_kernel, layers=layers, parts=parts),
        grid_spec=grid_spec,
        out_shape=[
            out(count, layers, comps, VB, planes),
            out(parts // 2, count, comps, width, cells),
            out(parts // 2, count, comps, width, cells),
        ],
        compiler_params=params(),
        cost_estimate=pl.CostEstimate(
            flops=30_000_000 * count, bytes_accessed=3_000_000 * count, transcendentals=0
        ),
        name="chebyshev",
    )(place, start2, lo, hi, table, gauge)


def corr_kernel(place_ref, stored_ref, *refs, layers, groups):
    half_refs, out_ref, weight_ref = refs[:groups], refs[groups], refs[groups + 1]
    planes = stored_ref.shape[-1]
    vectors = VB * sum(r.shape[0] for r in half_refs)
    block = stored_ref.shape[0]

    @pl.when(pl.program_id(0) == 0)
    def _():
        at = 0
        for ref in half_refs:
            for g in range(ref.shape[0]):
                for x in range(layers):
                    for part in range(2):
                        for c in range(3):
                            for p in range(2):
                                value = ref[g, x, (part ^ p) * 3 + c]
                                if p == 1 and part == 1:
                                    value = -value
                                weight_ref[
                                    pl.ds((x * 2 + p) * vectors + at, VB),
                                    pl.ds((part * 3 + c) * planes, planes),
                                ] = value
                at += VB

    rows = jnp.concatenate(
        [stored_ref[:, k].reshape(block * layers, planes) for k in range(6)], axis=1
    )
    full = lax.dot_general(
        rows, weight_ref[...], (((1,), (1,)), ((), ())), preferred_element_type=jnp.float32
    )
    span = 2 * vectors
    layer_of_row = lax.broadcasted_iota(jnp.int32, (block * layers, span), 0) % layers
    kept = jnp.zeros((block * layers, span), jnp.float32)
    for x in range(layers):
        kept = jnp.where(layer_of_row == x, full[:, x * span : (x + 1) * span], kept)
    out_ref[...] = jnp.sum(kept.reshape(block, layers, span), axis=1).T


def run_corr(place, stored, halves, owners):
    count, comps, layers, planes = stored.shape
    block = count // owners
    vectors = VB * sum(h.shape[0] for h in halves)
    grid_spec = pltpu.PrefetchScalarGridSpec(
        num_scalar_prefetch=1,
        grid=(owners,),
        in_specs=[pl.BlockSpec((block, comps, layers, planes), lambda g, s: (g, 0, 0, 0))]
        + [pl.BlockSpec(h.shape, lambda g, s: (0, 0, 0, 0, 0)) for h in halves],
        out_specs=pl.BlockSpec(
            (pl.Squeezed(), 2 * vectors, block),
            lambda g, s: (lax.rem(g - s[2] + owners, owners), 0, 0),
        ),
        scratch_shapes=[pltpu.VMEM((layers * 2 * vectors, comps * planes), jnp.bfloat16)],
    )
    return pl.pallas_call(
        functools.partial(corr_kernel, layers=layers, groups=len(halves)),
        grid_spec=grid_spec,
        out_shape=jax.ShapeDtypeStruct((owners, 2 * vectors, block), jnp.float32),
        compiler_params=params(),
        cost_estimate=pl.CostEstimate(
            flops=6_000_000_000, bytes_accessed=12_000_000, transcendentals=0
        ),
        name="correlate",
    )(place, stored, *halves)


def gather_kernel(place_ref, *refs, layers, pairs, near, groups):
    out_ref = refs[-1]
    width = out_ref.shape[2]
    total_groups = sum(refs[g].shape[1] for g in range(groups))
    vectors = total_groups * VB
    cells = layers * VB
    depth = 2 * total_groups * cells
    row = lax.broadcasted_iota(jnp.int32, (depth, depth), 0)
    col = lax.broadcasted_iota(jnp.int32, (depth, depth), 1)
    bit, rest = row // (total_groups * cells), row % (total_groups * cells)
    group, cell = rest // cells, rest % cells
    wanted = ((cell // VB) * 2 + bit) * vectors + group * VB + cell % VB
    order = (wanted == col).astype(jnp.bfloat16)
    mine, side = place_ref[3], place_ref[4]
    for step in range(pairs):
        source = lax.rem(mine - step + pairs, pairs)
        slice_at = source // near
        chip = lax.rem(source, near)
        for h in range(2):
            core = side if h == 0 else 1 - side
            first = (chip * 2 + core) * layers
            pieces = []
            for pair in range(3):
                lanes = []
                for bit_at in range(2):
                    for g in range(groups):
                        ref = refs[step * groups + g]
                        for n in range(ref.shape[1]):
                            lanes.append(ref[h, n, 2 * pair + bit_at])
                pieces.append(jnp.concatenate(lanes, axis=1))
            rows = jnp.concatenate(pieces, axis=0)
            moved = jnp.dot(rows, order, preferred_element_type=jnp.float32)
            for x in range(layers):
                out_ref[slice_at, first + x] = jnp.concatenate(
                    [
                        moved[p * width : (p + 1) * width, x * 2 * vectors : (x + 1) * 2 * vectors]
                        for p in range(3)
                    ],
                    axis=1,
                ).astype(jnp.bfloat16)


def run_gather(place, blocks, slices, layers, near, groups):
    pairs = len(blocks) // groups
    _, _, comps, width, _ = blocks[0].shape
    vectors = VB * sum(blocks[g].shape[1] for g in range(groups))
    grid_spec = pltpu.PrefetchScalarGridSpec(
        num_scalar_prefetch=1,
        grid=(1,),
        in_specs=[pl.BlockSpec(b.shape, lambda g, s: (0, 0, 0, 0, 0)) for b in blocks],
        out_specs=pl.BlockSpec((slices, 2 * near * layers, width, comps * vectors), lambda g, s: (0, 0, 0, 0)),
    )
    return pl.pallas_call(
        functools.partial(gather_kernel, layers=layers, pairs=pairs, near=near, groups=groups),
        grid_spec=grid_spec,
        out_shape=jax.ShapeDtypeStruct((slices, 2 * near * layers, width, comps * vectors), jnp.bfloat16),
        compiler_params=params(),
        name="arrange",
    )(place, *blocks)


def shards(start_block, gauge_links, stored_vectors, *, n_tm, n_space):
    _, parts, colours, vectors, layers, planes = start_block.shape
    comps = parts * colours
    tm, space = lax.axis_index("tm"), lax.axis_index("space")
    per = n_tm // n_space
    near = n_space // 2
    pairs = n_tm // 2
    core = lax.rem(space, 2)
    place = jnp.stack(
        [core, lax.rem(tm, per) * near + space // 2, space, tm // 2, lax.rem(tm, 2)]
    ).astype(jnp.int32)

    tiles = planes // LANES

    def by_tile(value, *lead):
        value = value.reshape(-1, layers, tiles, LANES)
        return jnp.transpose(value, (0, 2, 1, 3)).reshape(*lead, LANES)

    start2 = by_tile(start_block, comps, vectors * tiles * layers)
    links2 = by_tile(gauge_links, LINK_ROWS * tiles * layers)
    up = [(i, (i + 1) % n_space) for i in range(n_space)]
    down = [((i + 1) % n_space, i) for i in range(n_space)]

    own_links, half_links = pack_links(links2, layers, tiles)
    lo_links = lax.ppermute(half_links[layers - DEGREE :], "space", up)
    hi_links = lax.ppermute(half_links[:DEGREE], "space", down)
    halo = pack_halo(start2, layers, tiles)
    table, gauge = gauge_tables(own_links, lo_links, hi_links)

    halves, sent = [], []
    for group in GROUPS:
        first, count = group[0], len(group)
        lo = lax.ppermute(halo[layers - DEGREE :, first : first + count], "space", up)
        hi = lax.ppermute(halo[:DEGREE, first : first + count], "space", down)
        half, keep, give = run_filter(
            place, start2, lo, hi, table, gauge, first, count, layers, n_tm
        )
        halves.append(half)
        swap = [(i, i ^ 1) for i in range(n_space)]
        got = lax.ppermute(give, "space", swap)
        moved = []
        for step in range(pairs):
            block = jnp.stack([keep[step], got[step]])
            table_of = []
            for i in range(n_tm):
                for j in range(n_space):
                    m = ((i % per) * near + j // 2 + step) % pairs
                    table_of.append((i * n_space + j, (2 * m + j % 2) * n_space + i // per))
            moved.append(lax.ppermute(block, ("tm", "space"), table_of))
        sent.append(moved)

    stored = stored_vectors.reshape(stored_vectors.shape[1], comps, layers, planes)
    partial = run_corr(place, stored, halves, n_space)
    total = partial[0]
    for step in range(1, n_space):
        total = total + lax.ppermute(
            partial[step], "space", [(i, (i + step) % n_space) for i in range(n_space)]
        )
    correlations = total.T[None]

    blocks = [sent[g][step] for step in range(pairs) for g in range(len(GROUPS))]
    solver_blocks = run_gather(place, blocks, per, layers, near, len(GROUPS))
    return correlations, solver_blocks


def solution(mesh):
    in_specs = (
        P("tm", None, None, None, "space", None),
        P("tm", None, None, None, None, "space", None),
        P("tm", None, None, None, "space", None),
    )
    out_specs = (P("tm", "space", None), P("space", None, "tm", None))
    body = functools.partial(shards, n_tm=mesh.shape["tm"], n_space=mesh.shape["space"])
    return jax.shard_map(body, mesh=mesh, in_specs=in_specs, out_specs=out_specs, check_vma=False)
```

```python
import functools

import jax
import jax.numpy as jnp
from jax import lax
from jax.experimental import pallas as pl
from jax.experimental.pallas import tpu as pltpu
from jax.sharding import PartitionSpec as P

DEGREE = 4
LZ = 16
LANES = 128
VB = 16

lower_edge = 0.5
upper_edge = 12.5
SCALE = 2.0 / (upper_edge - lower_edge)
OFFSET = (upper_edge + lower_edge) / (upper_edge - lower_edge)

VMEM_LIMIT = 60 * 2**20
LINK_ROWS = 54
LINK_PAD = 56
TABLE_ROWS = 112
GAUGE_ROWS = 24


def params(limit=24 * 2**20):
    return pltpu.CompilerParams(vmem_limit_bytes=limit)


def in_vmem(count):
    return [pl.BlockSpec(memory_space=pltpu.VMEM)] * count


def in_smem():
    return pl.BlockSpec(memory_space=pltpu.SMEM)


def cost(microseconds):
    return pl.CostEstimate(
        flops=1_000_000, bytes_accessed=int(microseconds * 3_000_000), transcendentals=0
    )


def fetch(start_hbm, links_hbm, start_ref, links_ref, sems):
    comps = start_ref.shape[0]
    copies = [pltpu.make_async_copy(links_hbm, links_ref, sems.at[comps])] + [
        pltpu.make_async_copy(start_hbm.at[k], start_ref.at[k], sems.at[k]) for k in range(comps)
    ]
    for copy in copies:
        copy.start()
    return copies


def fetch_scratch(start2, links2):
    return [
        pltpu.VMEM(start2.shape, jnp.float32),
        pltpu.VMEM(links2.shape, jnp.float32),
        pltpu.SemaphoreType.DMA((start2.shape[0] + 1,)),
    ]


def pack_kernel(
    start_hbm, links_hbm, up_links_ref, down_links_ref, up_ref, down_ref,
    start_ref, links_ref, sems, *, layers, tiles
):
    comps, groups = up_ref.shape[2], up_ref.shape[1]
    cells = VB * layers * tiles
    copies = fetch(start_hbm, links_hbm, start_ref, links_ref, sems)
    copies[0].wait()
    for x in range(layers):
        for t in range(tiles):
            rows = links_ref[pl.ds(t * layers + x, LINK_ROWS, stride=tiles * layers), :]
            if x < DEGREE:
                down_links_ref[x, :, cols(t)] = rows.astype(jnp.bfloat16)
            if x >= layers - DEGREE:
                up_links_ref[x - layers + DEGREE, :, cols(t)] = rows.astype(jnp.bfloat16)
    for k in range(comps):
        copies[1 + k].wait()
        for x in range(layers):
            for t in range(tiles):
                for g in range(groups):
                    half = start_ref[
                        k, pl.ds(g * cells + t * layers + x, VB, stride=tiles * layers), :
                    ].astype(jnp.bfloat16)
                    if x < DEGREE:
                        down_ref[x, g, k, :, cols(t)] = half
                    if x >= layers - DEGREE:
                        up_ref[x - layers + DEGREE, g, k, :, cols(t)] = half


def run_pack(start2, links2, layers, tiles):
    comps, rows, _ = start2.shape
    planes = tiles * LANES
    groups = rows // (VB * layers * tiles)
    link = jax.ShapeDtypeStruct((DEGREE, LINK_ROWS, planes), jnp.bfloat16)
    halo = jax.ShapeDtypeStruct((DEGREE, groups, comps, VB, planes), jnp.bfloat16)
    return pl.pallas_call(
        functools.partial(pack_kernel, layers=layers, tiles=tiles),
        in_specs=[pl.BlockSpec(memory_space=pltpu.HBM)] * 2,
        out_specs=in_vmem(4),
        out_shape=[link, link, halo, halo],
        scratch_shapes=fetch_scratch(start2, links2),
        compiler_params=params(VMEM_LIMIT),
        cost_estimate=cost(2.5),
        name="pack",
    )(start2, links2)


def mat_mul(a, b, conj_b=False):
    out_re, out_im = [], []
    for i in range(3):
        for j in range(3):
            re = im = None
            for k in range(3):
                ar, ai = a[0][3 * i + k], a[1][3 * i + k]
                if conj_b:
                    br, bi = b[0][3 * j + k], b[1][3 * j + k]
                    r = ar * br + ai * bi
                    m = ai * br - ar * bi
                else:
                    br, bi = b[0][3 * k + j], b[1][3 * k + j]
                    r = ar * br - ai * bi
                    m = ar * bi + ai * br
                re = r if re is None else re + r
                im = m if im is None else im + m
            out_re.append(re)
            out_im.append(im)
    return out_re, out_im


def rot(v, steps):
    return pltpu.roll(v, steps % LANES, 1)


def shifts(value, masks):
    z_last, z_first, y_low, y_high = masks
    tiles = len(value)
    up = [rot(v, LZ) for v in value]
    down = [rot(v, -LZ) for v in value]
    return (
        [jnp.where(y_low, down[t], down[(t + 1) % tiles]) for t in range(tiles)],
        [jnp.where(y_high, up[t], up[(t - 1) % tiles]) for t in range(tiles)],
        [rot(jnp.where(z_first, up[t], value[t]), -1) for t in range(tiles)],
        [rot(jnp.where(z_last, down[t], value[t]), 1) for t in range(tiles)],
    )


def lane_masks(rows):
    lane = lax.broadcasted_iota(jnp.int32, (rows, LANES), 1)
    return lane % LZ == LZ - 1, lane % LZ == 0, lane < LANES - LZ, lane >= LZ


def cols(t):
    return slice(t * LANES, (t + 1) * LANES)


def rows_at(ref, t, first):
    return (
        [ref[t, pl.ds(first + k, 1), :] for k in range(9)],
        [ref[t, pl.ds(first + 9 + k, 1), :] for k in range(9)],
    )


def put_rows(ref, t, first, g):
    for k in range(9):
        ref[t, pl.ds(first + k, 1), :] = g[0][k]
        ref[t, pl.ds(first + 9 + k, 1), :] = g[1][k]


def unit_rows():
    one = jnp.ones((1, LANES), jnp.float32)
    zero = jnp.zeros((1, LANES), jnp.float32)
    return [one if k % 4 == 0 else zero for k in range(9)], [zero] * 9


def fill_tables(ext_ref, g_ref, t_ref, table_ref, gauge_ref, places):
    tiles = ext_ref.shape[0]
    total = len(places)
    masks = lane_masks(total)

    def column(ref, k, stride):
        return [ref[t, pl.ds(k, total, stride=stride), :] for t in range(tiles)]

    gauge = [column(g_ref, k, GAUGE_ROWS) for k in range(18)]
    for d in (1, 2):
        link = [column(ext_ref, 18 * d + k, LINK_PAD) for k in range(18)]
        ahead = [shifts(v, masks)[2 * (d - 1)] for v in gauge]
        turned = []
        for t in range(tiles):
            here, there, mid = (
                ([v[t] for v in field[:9]], [v[t] for v in field[9:]])
                for field in (gauge, ahead, link)
            )
            turned.append(mat_mul(mat_mul(here, mid), there, conj_b=True))
        base = 54 * (d - 1)
        for k in range(9):
            re, im = [turned[t][0][k] for t in range(tiles)], [turned[t][1][k] for t in range(tiles)]
            back_re, back_im = shifts(re, masks)[2 * d - 1], shifts(im, masks)[2 * d - 1]
            for t in range(tiles):
                for at, value in (
                    (0, re[t]),
                    (9, re[t] + im[t]),
                    (18, im[t] - re[t]),
                    (27, back_re[t]),
                    (36, back_re[t] + back_im[t]),
                    (45, back_im[t] - back_re[t]),
                ):
                    t_ref[t, pl.ds(base + at + k, total, stride=TABLE_ROWS), :] = value
    for n, x in enumerate(places):
        for t in range(tiles):
            table_ref[x, 0:108, cols(t)] = t_ref[t, pl.ds(n * TABLE_ROWS, 108), :]
            gauge_ref[x, 0:18, cols(t)] = g_ref[t, pl.ds(n * GAUGE_ROWS, 18), :]


def gauge_own(links_ref, table_ref, gauge_ref, ext_ref, g_ref, t_ref, layers):
    tiles = ext_ref.shape[0]
    for t in range(tiles):
        for x in range(layers):
            ext_ref[t, pl.ds(x * LINK_PAD, LINK_ROWS), :] = links_ref[
                pl.ds(t * layers + x, LINK_ROWS, stride=tiles * layers), :
            ]
    for t in range(tiles):
        g = unit_rows()
        put_rows(g_ref, t, 0, g)
        for x in range(layers - 1):
            g = mat_mul(g, rows_at(ext_ref, t, x * LINK_PAD))
            put_rows(g_ref, t, (x + 1) * GAUGE_ROWS, g)
    fill_tables(
        ext_ref, g_ref, t_ref, table_ref, gauge_ref, [DEGREE + x for x in range(layers)]
    )


def gauge_halo_kernel(
    top_ref, lo_ref, hi_ref, table_in, gauge_in, table_ref, gauge_ref, ext_ref, g_ref, t_ref
):
    layers = table_ref.shape[0] - 2 * DEGREE
    for x in range(DEGREE, DEGREE + layers):
        table_ref[x] = table_in[x]
        gauge_ref[x] = gauge_in[x]
    tiles = ext_ref.shape[0]
    for t in range(tiles):
        for x in range(DEGREE):
            ext_ref[t, pl.ds(x * LINK_PAD, LINK_ROWS), :] = lo_ref[x, :, cols(t)].astype(jnp.float32)
            ext_ref[t, pl.ds((DEGREE + x) * LINK_PAD, LINK_ROWS), :] = hi_ref[x, :, cols(t)].astype(
                jnp.float32
            )
    for t in range(tiles):
        g = unit_rows()
        for x in range(DEGREE - 1, -1, -1):
            g = mat_mul(g, rows_at(ext_ref, t, x * LINK_PAD), conj_b=True)
            put_rows(g_ref, t, x * GAUGE_ROWS, g)
        top = DEGREE + layers - 1
        g = tuple(
            [gauge_in[top, pl.ds(first + k, 1), cols(t)] for k in range(9)] for first in (0, 9)
        )
        link = tuple(
            [top_ref[pl.ds(first + k, 1), cols(t)] for k in range(9)]
            for first in (0, 9)
        )
        for x in range(DEGREE):
            g = mat_mul(g, link)
            put_rows(g_ref, t, (DEGREE + x) * GAUGE_ROWS, g)
            if x < DEGREE - 1:
                link = rows_at(ext_ref, t, (DEGREE + x) * LINK_PAD)
    places = list(range(DEGREE)) + [DEGREE + layers + x for x in range(DEGREE)]
    fill_tables(ext_ref, g_ref, t_ref, table_ref, gauge_ref, places)


def gauge_scratch(count, tiles):
    return [
        pltpu.VMEM((tiles, count * LINK_PAD, LANES), jnp.float32),
        pltpu.VMEM((tiles, count * GAUGE_ROWS, LANES), jnp.float32),
        pltpu.VMEM((tiles, count * TABLE_ROWS, LANES), jnp.float32),
    ]


def gauge_shapes(layers, planes):
    total = layers + 2 * DEGREE
    return [
        jax.ShapeDtypeStruct((total, TABLE_ROWS, planes), jnp.float32),
        jax.ShapeDtypeStruct((total, GAUGE_ROWS, planes), jnp.float32),
    ]


def gauge_halo(top, lo, hi, table, gauge):
    total, _, planes = table.shape
    return pl.pallas_call(
        gauge_halo_kernel,
        in_specs=in_vmem(5),
        out_specs=in_vmem(2),
        out_shape=gauge_shapes(total - 2 * DEGREE, planes),
        scratch_shapes=gauge_scratch(2 * DEGREE, planes // LANES),
        compiler_params=params(),
        cost_estimate=cost(1.5),
        name="gauge_halo",
    )(top, lo, hi, table, gauge)


def turn(gauge_ref, x, source, adjoint, tiles):
    out = {}
    for t in range(tiles):
        v = [source(k, t) for k in range(6)]
        for i in range(3):
            re = im = None
            for j in range(3):
                k = 3 * j + i if adjoint else 3 * i + j
                a = gauge_ref[x, pl.ds(k, 1), cols(t)]
                b = gauge_ref[x, pl.ds(9 + k, 1), cols(t)]
                if adjoint:
                    r, m = a * v[j] + b * v[3 + j], a * v[3 + j] - b * v[j]
                else:
                    r, m = a * v[j] - b * v[3 + j], a * v[3 + j] + b * v[j]
                re = r if re is None else re + r
                im = m if im is None else im + m
            out[i, t], out[3 + i, t] = re, im
    return out


def layer(table_ref, g, x, src, prev, first, tiles):
    z_last, z_first, y_low, y_high = lane_masks(VB)
    sums = {}

    def add(key, value, minus=False):
        have = sums.get(key)
        if have is None:
            sums[key] = -value if minus else value
        else:
            sums[key] = have - value if minus else have + value

    def hop(t, base, v, adjoint):
        both = [v[j] + v[3 + j] for j in range(3)]
        for j in range(3):
            for i in range(3):
                k = base + (3 * j + i if adjoint else 3 * i + j)
                a = table_ref[x, pl.ds(k, 1), cols(t)]
                p = table_ref[x, pl.ds(k + 9, 1), cols(t)]
                q = table_ref[x, pl.ds(k + 18, 1), cols(t)]
                add((t, 0, i), a * both[j])
                if adjoint:
                    add((t, 1, i), q * v[3 + j], True)
                    add((t, 2, i), p * v[j], True)
                else:
                    add((t, 1, i), p * v[3 + j])
                    add((t, 2, i), q * v[j])

    out = {}
    for t in range(tiles):
        c = {(k, u): src[g, x, k, :, cols(u)] for k in range(6) for u in range(tiles)}
        after, before = (t + 1) % tiles, (t - 1) % tiles
        hop(t, 0, [rot(jnp.where(y_high, c[k, t], c[k, after]), -LZ) for k in range(6)], False)
        hop(t, 27, [rot(jnp.where(y_low, c[k, t], c[k, before]), LZ) for k in range(6)], True)
        hop(
            t, 54,
            [jnp.where(z_last, rot(c[k, t], LZ - 1), rot(c[k, t], -1)) for k in range(6)],
            False,
        )
        hop(
            t, 81,
            [jnp.where(z_first, rot(c[k, t], 1 - LZ), rot(c[k, t], 1)) for k in range(6)],
            True,
        )
        for i in range(3):
            re = sums[t, 0, i] - sums[t, 1, i]
            im = sums[t, 0, i] + sums[t, 2, i]
            for k, h in ((i, re), (3 + i, im)):
                h = h + (src[g, x + 1, k, :, cols(t)] + src[g, x - 1, k, :, cols(t)])
                if first:
                    out[k, t] = (6.0 * SCALE - OFFSET) * c[k, t] - SCALE * h
                else:
                    out[k, t] = (
                        (12.0 * SCALE - 2.0 * OFFSET) * c[k, t]
                        - (2.0 * SCALE) * h
                        - prev[g, x, k, :, cols(t)]
                    )
    return out


def put(ref, g, x, values):
    for (k, t), value in values.items():
        ref[g, x, k, :, cols(t)] = value


def inner_kernel(
    start_hbm, links_hbm, a_ref, b_ref, table_ref, gauge_ref, top_ref,
    start_ref, links_ref, sems, ext_ref, g_ref, t_ref, *, layers
):
    groups = a_ref.shape[0]
    tiles = table_ref.shape[-1] // LANES
    cells = VB * layers * tiles
    copies = fetch(start_hbm, links_hbm, start_ref, links_ref, sems)
    copies[0].wait()
    gauge_own(links_ref, table_ref, gauge_ref, ext_ref, g_ref, t_ref, layers)
    for t in range(tiles):
        top_ref[0:18, cols(t)] = ext_ref[t, pl.ds((layers - 1) * LINK_PAD, 18), :]
    for copy in copies[1:]:
        copy.wait()

    def init(n, _):
        g, x = n // layers, n % layers

        def source(k, t):
            at = g * cells + t * layers + x
            return start_ref[k, pl.ds(at, VB, stride=tiles * layers), :]

        put(a_ref, g, x + DEGREE, turn(gauge_ref, x + DEGREE, source, False, tiles))
        return 0

    lax.fori_loop(0, groups * layers, init, 0)
    for level in range(1, DEGREE):
        src, dst = (a_ref, b_ref) if level % 2 else (b_ref, a_ref)
        pairs = (layers - 2 * level) // 2

        def body(n, _, src=src, dst=dst, level=level, pairs=pairs):
            g, at = n // pairs, n % pairs
            for u in range(2):
                x = DEGREE + level + 2 * at + u
                put(dst, g, x, layer(table_ref, g, x, src, dst, level == 1, tiles))
            return 0

        if pairs > 0:
            lax.fori_loop(0, groups * pairs, body, 0)


def run_inner(start2, links2, layers, tiles):
    comps, rows, _ = start2.shape
    planes = tiles * LANES
    groups = rows // (VB * layers * tiles)
    state = jax.ShapeDtypeStruct((groups, layers + 2 * DEGREE, comps, VB, planes), jnp.float32)
    top = jax.ShapeDtypeStruct((GAUGE_ROWS, planes), jnp.float32)
    return pl.pallas_call(
        functools.partial(inner_kernel, layers=layers),
        in_specs=[pl.BlockSpec(memory_space=pltpu.HBM)] * 2,
        out_specs=in_vmem(5),
        out_shape=[state, state] + gauge_shapes(layers, planes) + [top],
        scratch_shapes=fetch_scratch(start2, links2) + gauge_scratch(layers, tiles),
        compiler_params=params(),
        cost_estimate=cost(8),
        name="inner",
    )(start2, links2)


def outer_kernel(
    place_ref, lo_ref, hi_ref, table_ref, gauge_ref, a_in, b_in,
    half_ref, keep_ref, give_ref, a_ref, b_ref, pack_ref, *, layers, parts
):
    groups = a_ref.shape[0]
    total = layers + 2 * DEGREE
    planes = table_ref.shape[-1]
    tiles = planes // LANES

    def init(n, _):
        g, x = n // DEGREE, n % DEGREE
        for ref, at in ((lo_ref, x), (hi_ref, x + DEGREE + layers)):

            def source(k, t, ref=ref):
                return ref[x, g, k, :, cols(t)].astype(jnp.float32)

            put(a_ref, g, at, turn(gauge_ref, at, source, False, tiles))
        for at in (x + DEGREE, total - 2 * DEGREE + x):
            a_ref[g, at] = a_in[g, at]
            b_ref[g, at] = b_in[g, at]
        return 0

    lax.fori_loop(0, groups * DEGREE, init, 0)
    for level in range(1, DEGREE):
        src, dst = (a_ref, b_ref) if level % 2 else (b_ref, a_ref)

        def body(n, _, src=src, dst=dst, level=level):
            g, at = n // DEGREE, n % DEGREE
            for x in (level + at, total - DEGREE - level + at):
                put(dst, g, x, layer(table_ref, g, x, src, dst, level == 1, tiles))
            return 0

        lax.fori_loop(0, groups * DEGREE, body, 0)
    src, prev = (a_ref, b_ref) if DEGREE % 2 else (b_ref, a_ref)

    def last(n, _):
        g, at = n // (layers // 2), n % (layers // 2)
        for u in range(2):
            x = 2 * at + u
            value = layer(table_ref, g, x + DEGREE, src, prev, False, tiles)
            value = turn(gauge_ref, x + DEGREE, lambda k, t: value[k, t], True, tiles)
            for (k, t), v in value.items():
                rounded = v.astype(jnp.bfloat16)
                half_ref[g, x, k, :, cols(t)] = rounded
                pack_ref[g, k, pl.ds(pl.multiple_of(x * VB, VB), VB), cols(t)] = rounded.astype(
                    jnp.float32
                )
        return 0

    lax.fori_loop(0, groups * (layers // 2), last, 0)

    me, shift = place_ref[0], place_ref[1]
    pairs = parts // 2
    width = planes // parts
    for g in range(groups):
        for k in range(6):
            turned = jnp.concatenate([pack_ref[g, k, :, cols(t)].T for t in range(tiles)], axis=0)
            for m in range(pairs):
                even = turned[2 * m * width : (2 * m + 1) * width].astype(jnp.bfloat16)
                odd = turned[(2 * m + 1) * width : (2 * m + 2) * width].astype(jnp.bfloat16)
                at = lax.rem(m - shift + pairs, pairs)
                keep_ref[at, g, k] = jnp.where(me == 0, even, odd)
                give_ref[at, g, k] = jnp.where(me == 0, odd, even)


def run_outer(place, lo, hi, table, gauge, a, b, layers, parts):
    groups, total, comps, _, planes = a.shape
    width = planes // parts
    cells = layers * VB
    block = jax.ShapeDtypeStruct((parts // 2, groups, comps, width, cells), jnp.bfloat16)
    half = jax.ShapeDtypeStruct((groups, layers, comps, VB, planes), jnp.bfloat16)
    return pl.pallas_call(
        functools.partial(outer_kernel, layers=layers, parts=parts),
        in_specs=[in_smem()] + in_vmem(6),
        out_specs=in_vmem(3),
        out_shape=[half, block, block],
        scratch_shapes=[
            pltpu.VMEM(a.shape, jnp.float32),
            pltpu.VMEM(a.shape, jnp.float32),
            pltpu.VMEM((groups, comps, cells, planes), jnp.float32),
        ],
        compiler_params=params(),
        cost_estimate=cost(16),
        name="outer",
    )(place, lo, hi, table, gauge, a, b)


def weight_kernel(half_ref, weight_ref):
    groups, layers, _, _, planes = half_ref.shape
    vectors = groups * VB
    for g in range(groups):
        for x in range(layers):
            for part in range(2):
                for c in range(3):
                    for p in range(2):
                        value = half_ref[g, x, (part ^ p) * 3 + c]
                        if p == 1 and part == 1:
                            value = -value
                        weight_ref[
                            pl.ds((x * 2 + p) * vectors + g * VB, VB),
                            pl.ds((part * 3 + c) * planes, planes),
                        ] = value


def run_weights(half):
    groups, layers, comps, _, planes = half.shape
    return pl.pallas_call(
        weight_kernel,
        in_specs=in_vmem(1),
        out_specs=in_vmem(1)[0],
        out_shape=jax.ShapeDtypeStruct((layers * 2 * groups * VB, comps * planes), jnp.bfloat16),
        compiler_params=params(),
        cost_estimate=cost(0.7),
        name="weights",
    )(half)


def corr_kernel(place_ref, stored_ref, weight_ref, out_ref, *, layers):
    span, block = out_ref.shape
    _, comps, _, planes = stored_ref.shape
    rows = jnp.concatenate(
        [stored_ref[:, k].reshape(block * layers, planes) for k in range(comps)], axis=1
    )
    full = lax.dot_general(
        rows, weight_ref[...], (((1,), (1,)), ((), ())), preferred_element_type=jnp.float32
    )
    layer_of_row = lax.broadcasted_iota(jnp.int32, (block * layers, span), 0) % layers
    kept = jnp.zeros((block * layers, span), jnp.float32)
    for x in range(layers):
        kept = jnp.where(layer_of_row == x, full[:, x * span : (x + 1) * span], kept)
    out_ref[...] = jnp.sum(kept.reshape(block, layers, span), axis=1).T


def run_corr(place, stored, weights, owners):
    count, comps, layers, planes = stored.shape
    block = count // owners
    span = weights.shape[0] // layers
    grid_spec = pltpu.PrefetchScalarGridSpec(
        num_scalar_prefetch=1,
        grid=(owners,),
        in_specs=[
            pl.BlockSpec((block, comps, layers, planes), lambda g, s: (g, 0, 0, 0)),
            pl.BlockSpec(memory_space=pltpu.VMEM),
        ],
        out_specs=pl.BlockSpec((pl.Squeezed(), span, block), lambda g, s: (g ^ s[2], 0, 0)),
    )
    return pl.pallas_call(
        functools.partial(corr_kernel, layers=layers),
        grid_spec=grid_spec,
        out_shape=jax.ShapeDtypeStruct((owners, span, block), jnp.float32),
        compiler_params=params(40 * 2**20),
        cost_estimate=cost(11),
        name="correlate",
    )(place, stored, weights)


def merge_kernel(keep_ref, got_ref, *out_refs):
    for step, ref in enumerate(out_refs):
        ref[0] = keep_ref[step]
        ref[1] = got_ref[step]


def run_merge(keep, got):
    shape = jax.ShapeDtypeStruct((2,) + keep.shape[1:], keep.dtype)
    return pl.pallas_call(
        merge_kernel,
        in_specs=in_vmem(2),
        out_specs=in_vmem(keep.shape[0]),
        out_shape=[shape] * keep.shape[0],
        compiler_params=params(),
        cost_estimate=cost(0.7),
        name="merge",
    )(keep, got)


def order_kernel(order_ref, *, layers, groups):
    depth = order_ref.shape[0]
    cells = layers * VB
    vectors = groups * VB
    row = lax.broadcasted_iota(jnp.int32, (depth, depth), 0)
    col = lax.broadcasted_iota(jnp.int32, (depth, depth), 1)
    bit, rest = row // (groups * cells), row % (groups * cells)
    group, cell = rest // cells, rest % cells
    wanted = ((cell // VB) * 2 + bit) * vectors + group * VB + cell % VB
    order_ref[...] = (wanted == col).astype(jnp.bfloat16)


def run_order(groups, layers):
    depth = 2 * groups * layers * VB
    return pl.pallas_call(
        functools.partial(order_kernel, layers=layers, groups=groups),
        out_specs=in_vmem(1)[0],
        out_shape=jax.ShapeDtypeStruct((depth, depth), jnp.bfloat16),
        compiler_params=params(),
        cost_estimate=cost(2),
        name="order",
    )()


def arrange_kernel(place_ref, order_ref, *refs, layers):
    out_ref = refs[-1]
    groups, comps, width = refs[0].shape[1:4]
    span = 2 * groups * VB
    side = place_ref[4]

    def move(block_ref):
        for h in range(2):
            core = side if h == 0 else 1 - side
            pieces = []
            for pair in range(comps // 2):
                lanes = [
                    block_ref[h, g, 2 * pair + bit] for bit in range(2) for g in range(groups)
                ]
                pieces.append(jnp.concatenate(lanes, axis=1))
            moved = jnp.dot(
                jnp.concatenate(pieces, axis=0), order_ref[...], preferred_element_type=jnp.float32
            )
            for x in range(layers):
                out_ref[core * layers + x] = jnp.concatenate(
                    [
                        moved[p * width : (p + 1) * width, x * span : (x + 1) * span]
                        for p in range(comps // 2)
                    ],
                    axis=1,
                ).astype(jnp.bfloat16)

    for step, ref in enumerate(refs[:-1]):
        pl.when(pl.program_id(0) == step)(functools.partial(move, ref))


def run_arrange(place, order, blocks, shape, layers, near):
    pairs = len(blocks)

    def where(g, s):
        source = lax.rem(s[3] - g + pairs, pairs)
        return source // near, lax.rem(source, near), 0, 0

    grid_spec = pltpu.PrefetchScalarGridSpec(
        num_scalar_prefetch=1,
        grid=(pairs,),
        in_specs=in_vmem(1 + pairs),
        out_specs=pl.BlockSpec((pl.Squeezed(), 2 * layers) + shape[2:], where),
    )
    return pl.pallas_call(
        functools.partial(arrange_kernel, layers=layers),
        grid_spec=grid_spec,
        out_shape=jax.ShapeDtypeStruct(shape, jnp.bfloat16),
        compiler_params=params(),
        cost_estimate=cost(3),
        name="arrange",
    )(place, order, *blocks)


def shards(start_block, gauge_links, stored_vectors, *, n_tm, n_space):
    _, parts, colours, vectors, layers, planes = start_block.shape
    comps = parts * colours
    tm, space = lax.axis_index("tm"), lax.axis_index("space")
    per = n_tm // n_space
    near = n_space // 2
    pairs = n_tm // 2
    groups = vectors // VB
    core = lax.rem(space, 2)
    place = jnp.stack(
        [core, lax.rem(tm, per) * near + space // 2, space, tm // 2, lax.rem(tm, 2)]
    ).astype(jnp.int32)

    tiles = planes // LANES

    def by_tile(value, *lead):
        value = value.reshape(-1, layers, tiles, LANES)
        return jnp.transpose(value, (0, 2, 1, 3)).reshape(*lead, LANES)

    start2 = by_tile(start_block, comps, vectors * tiles * layers)
    links2 = by_tile(gauge_links, LINK_ROWS * tiles * layers)
    up = [(i, (i + 1) % n_space) for i in range(n_space)]
    down = [((i + 1) % n_space, i) for i in range(n_space)]

    up_links, down_links, up_halo, down_halo = run_pack(start2, links2, layers, tiles)
    lo_links = lax.ppermute(up_links, "space", up)
    hi_links = lax.ppermute(down_links, "space", down)
    lo = lax.ppermute(up_halo, "space", up)
    hi = lax.ppermute(down_halo, "space", down)
    order = run_order(groups, layers)

    a, b, table, gauge, top = run_inner(start2, links2, layers, tiles)
    table, gauge = gauge_halo(top, lo_links, hi_links, table, gauge)
    half, keep, give = run_outer(place, lo, hi, table, gauge, a, b, layers, n_tm)

    weights = run_weights(half)
    got = lax.ppermute(give, "space", [(i, i ^ 1) for i in range(n_space)])
    blocks = run_merge(keep, got)
    stored = stored_vectors.reshape(stored_vectors.shape[1], comps, layers, planes)
    sent = []
    for step, block in enumerate(blocks):
        table_of = []
        for i in range(n_tm):
            for j in range(n_space):
                m = ((i % per) * near + j // 2 + step) % pairs
                table_of.append((i * n_space + j, (2 * m + j % 2) * n_space + i // per))
        sent.append(lax.ppermute(block, ("tm", "space"), table_of))
    partial = run_corr(place, stored, weights, n_space)
    sums = {d: partial[d] for d in range(n_space)}

    bit = 1
    while bit < n_space:
        going = [d for d in sums if d & bit]
        partner = [(i, i ^ bit) for i in range(n_space)]
        came = lax.ppermute(jnp.stack([sums[d] for d in going]), "space", partner)
        for n, d in enumerate(going):
            sums[d ^ bit] = sums[d ^ bit] + came[n]
            del sums[d]
        bit *= 2
    correlations = sums[0].T[None]

    shape = (per, n_space * layers, planes // n_tm, comps * vectors)
    return correlations, run_arrange(place, order, sent, shape, layers, near)


def solution(mesh):
    in_specs = (
        P("tm", None, None, None, "space", None),
        P("tm", None, None, None, None, "space", None),
        P("tm", None, None, None, "space", None),
    )
    out_specs = (P("tm", "space", None), P("space", None, "tm", None))
    body = functools.partial(shards, n_tm=mesh.shape["tm"], n_space=mesh.shape["space"])
    return jax.shard_map(body, mesh=mesh, in_specs=in_specs, out_specs=out_specs, check_vma=False)
```

```python
import functools

import jax
import jax.numpy as jnp
from jax import lax
from jax.experimental import pallas as pl
from jax.experimental.pallas import tpu as pltpu
from jax.sharding import PartitionSpec as P

DEGREE = 4
LZ = 16
LANES = 128
VB = 16

lower_edge = 0.5
upper_edge = 12.5
SCALE = 2.0 / (upper_edge - lower_edge)
OFFSET = (upper_edge + lower_edge) / (upper_edge - lower_edge)

VMEM_LIMIT = 60 * 2**20
LINK_ROWS = 54
LINK_PAD = 56
TABLE_ROWS = 112
GAUGE_ROWS = 24


def params(limit=24 * 2**20):
    return pltpu.CompilerParams(vmem_limit_bytes=limit)


def in_vmem(count):
    return [pl.BlockSpec(memory_space=pltpu.VMEM)] * count


def in_smem():
    return pl.BlockSpec(memory_space=pltpu.SMEM)


def cost(microseconds):
    return pl.CostEstimate(
        flops=1_000_000, bytes_accessed=int(microseconds * 3_000_000), transcendentals=0
    )


def fetch(start_hbm, links_hbm, start_ref, links_ref, sems):
    comps = start_ref.shape[0]
    copies = [pltpu.make_async_copy(links_hbm, links_ref, sems.at[comps])] + [
        pltpu.make_async_copy(start_hbm.at[k], start_ref.at[k], sems.at[k]) for k in range(comps)
    ]
    for copy in copies:
        copy.start()
    return copies


def fetch_scratch(start2, links2):
    return [
        pltpu.VMEM(start2.shape, jnp.float32),
        pltpu.VMEM(links2.shape, jnp.float32),
        pltpu.SemaphoreType.DMA((start2.shape[0] + 1,)),
    ]


def pack_kernel(
    start_hbm, links_hbm, up_links_ref, down_links_ref, up_ref, down_ref,
    start_ref, links_ref, sems, *, layers, tiles
):
    comps, groups = up_ref.shape[2], up_ref.shape[1]
    cells = VB * layers * tiles
    copies = fetch(start_hbm, links_hbm, start_ref, links_ref, sems)
    copies[0].wait()
    for x in range(layers):
        for t in range(tiles):
            rows = links_ref[pl.ds(t * layers + x, LINK_ROWS, stride=tiles * layers), :]
            if x < DEGREE:
                down_links_ref[x, :, cols(t)] = rows.astype(jnp.bfloat16)
            if x >= layers - DEGREE:
                up_links_ref[x - layers + DEGREE, :, cols(t)] = rows.astype(jnp.bfloat16)
    for k in range(comps):
        copies[1 + k].wait()
        for x in range(layers):
            for t in range(tiles):
                for g in range(groups):
                    half = start_ref[
                        k, pl.ds(g * cells + t * layers + x, VB, stride=tiles * layers), :
                    ].astype(jnp.bfloat16)
                    if x < DEGREE:
                        down_ref[x, g, k, :, cols(t)] = half
                    if x >= layers - DEGREE:
                        up_ref[x - layers + DEGREE, g, k, :, cols(t)] = half


def run_pack(start2, links2, layers, tiles):
    comps, rows, _ = start2.shape
    planes = tiles * LANES
    groups = rows // (VB * layers * tiles)
    link = jax.ShapeDtypeStruct((DEGREE, LINK_ROWS, planes), jnp.bfloat16)
    halo = jax.ShapeDtypeStruct((DEGREE, groups, comps, VB, planes), jnp.bfloat16)
    return pl.pallas_call(
        functools.partial(pack_kernel, layers=layers, tiles=tiles),
        in_specs=[pl.BlockSpec(memory_space=pltpu.HBM)] * 2,
        out_specs=in_vmem(4),
        out_shape=[link, link, halo, halo],
        scratch_shapes=fetch_scratch(start2, links2),
        compiler_params=params(VMEM_LIMIT),
        cost_estimate=cost(2.5),
        name="pack",
    )(start2, links2)


def mat_mul(a, b, conj_b=False):
    out_re, out_im = [], []
    for i in range(3):
        for j in range(3):
            re = im = None
            for k in range(3):
                ar, ai = a[0][3 * i + k], a[1][3 * i + k]
                if conj_b:
                    br, bi = b[0][3 * j + k], b[1][3 * j + k]
                    r = ar * br + ai * bi
                    m = ai * br - ar * bi
                else:
                    br, bi = b[0][3 * k + j], b[1][3 * k + j]
                    r = ar * br - ai * bi
                    m = ar * bi + ai * br
                re = r if re is None else re + r
                im = m if im is None else im + m
            out_re.append(re)
            out_im.append(im)
    return out_re, out_im


def rot(v, steps):
    return pltpu.roll(v, steps % LANES, 1)


def shifts(value, masks):
    z_last, z_first, y_low, y_high = masks
    tiles = len(value)
    up = [rot(v, LZ) for v in value]
    down = [rot(v, -LZ) for v in value]
    return (
        [jnp.where(y_low, down[t], down[(t + 1) % tiles]) for t in range(tiles)],
        [jnp.where(y_high, up[t], up[(t - 1) % tiles]) for t in range(tiles)],
        [rot(jnp.where(z_first, up[t], value[t]), -1) for t in range(tiles)],
        [rot(jnp.where(z_last, down[t], value[t]), 1) for t in range(tiles)],
    )


def lane_masks(rows):
    lane = lax.broadcasted_iota(jnp.int32, (rows, LANES), 1)
    return lane % LZ == LZ - 1, lane % LZ == 0, lane < LANES - LZ, lane >= LZ


def cols(t):
    return slice(t * LANES, (t + 1) * LANES)


def rows_at(ref, t, first):
    return (
        [ref[t, pl.ds(first + k, 1), :] for k in range(9)],
        [ref[t, pl.ds(first + 9 + k, 1), :] for k in range(9)],
    )


def put_rows(ref, t, first, g):
    for k in range(9):
        ref[t, pl.ds(first + k, 1), :] = g[0][k]
        ref[t, pl.ds(first + 9 + k, 1), :] = g[1][k]


def unit_rows():
    one = jnp.ones((1, LANES), jnp.float32)
    zero = jnp.zeros((1, LANES), jnp.float32)
    return [one if k % 4 == 0 else zero for k in range(9)], [zero] * 9


def fill_tables(ext_ref, g_ref, t_ref, table_ref, gauge_ref, places):
    tiles = ext_ref.shape[0]
    total = len(places)
    masks = lane_masks(total)

    def column(ref, k, stride):
        return [ref[t, pl.ds(k, total, stride=stride), :] for t in range(tiles)]

    gauge = [column(g_ref, k, GAUGE_ROWS) for k in range(18)]
    for d in (1, 2):
        link = [column(ext_ref, 18 * d + k, LINK_PAD) for k in range(18)]
        ahead = [shifts(v, masks)[2 * (d - 1)] for v in gauge]
        turned = []
        for t in range(tiles):
            here, there, mid = (
                ([v[t] for v in field[:9]], [v[t] for v in field[9:]])
                for field in (gauge, ahead, link)
            )
            turned.append(mat_mul(mat_mul(here, mid), there, conj_b=True))
        base = 54 * (d - 1)
        for k in range(9):
            re, im = [turned[t][0][k] for t in range(tiles)], [turned[t][1][k] for t in range(tiles)]
            back_re, back_im = shifts(re, masks)[2 * d - 1], shifts(im, masks)[2 * d - 1]
            for t in range(tiles):
                for at, value in (
                    (0, re[t]),
                    (9, re[t] + im[t]),
                    (18, im[t] - re[t]),
                    (27, back_re[t]),
                    (36, back_re[t] + back_im[t]),
                    (45, back_im[t] - back_re[t]),
                ):
                    t_ref[t, pl.ds(base + at + k, total, stride=TABLE_ROWS), :] = value
    for n, x in enumerate(places):
        for t in range(tiles):
            table_ref[x, 0:108, cols(t)] = t_ref[t, pl.ds(n * TABLE_ROWS, 108), :]
            gauge_ref[x, 0:18, cols(t)] = g_ref[t, pl.ds(n * GAUGE_ROWS, 18), :]


def gauge_own(links_ref, table_ref, gauge_ref, ext_ref, g_ref, t_ref, layers):
    tiles = ext_ref.shape[0]
    for t in range(tiles):
        for x in range(layers):
            ext_ref[t, pl.ds(x * LINK_PAD, LINK_ROWS), :] = links_ref[
                pl.ds(t * layers + x, LINK_ROWS, stride=tiles * layers), :
            ]
    for t in range(tiles):
        g = unit_rows()
        put_rows(g_ref, t, 0, g)
        for x in range(layers - 1):
            g = mat_mul(g, rows_at(ext_ref, t, x * LINK_PAD))
            put_rows(g_ref, t, (x + 1) * GAUGE_ROWS, g)
    fill_tables(
        ext_ref, g_ref, t_ref, table_ref, gauge_ref, [DEGREE + x for x in range(layers)]
    )


def gauge_halo_kernel(
    top_ref, lo_ref, hi_ref, table_in, gauge_in, table_ref, gauge_ref, ext_ref, g_ref, t_ref
):
    layers = table_ref.shape[0] - 2 * DEGREE
    for x in range(DEGREE, DEGREE + layers):
        table_ref[x] = table_in[x]
        gauge_ref[x] = gauge_in[x]
    tiles = ext_ref.shape[0]
    for t in range(tiles):
        for x in range(DEGREE):
            ext_ref[t, pl.ds(x * LINK_PAD, LINK_ROWS), :] = lo_ref[x, :, cols(t)].astype(jnp.float32)
            ext_ref[t, pl.ds((DEGREE + x) * LINK_PAD, LINK_ROWS), :] = hi_ref[x, :, cols(t)].astype(
                jnp.float32
            )
    for t in range(tiles):
        g = unit_rows()
        for x in range(DEGREE - 1, -1, -1):
            g = mat_mul(g, rows_at(ext_ref, t, x * LINK_PAD), conj_b=True)
            put_rows(g_ref, t, x * GAUGE_ROWS, g)
        top = DEGREE + layers - 1
        g = tuple(
            [gauge_in[top, pl.ds(first + k, 1), cols(t)] for k in range(9)] for first in (0, 9)
        )
        link = tuple(
            [top_ref[pl.ds(first + k, 1), cols(t)] for k in range(9)]
            for first in (0, 9)
        )
        for x in range(DEGREE):
            g = mat_mul(g, link)
            put_rows(g_ref, t, (DEGREE + x) * GAUGE_ROWS, g)
            if x < DEGREE - 1:
                link = rows_at(ext_ref, t, (DEGREE + x) * LINK_PAD)
    places = list(range(DEGREE)) + [DEGREE + layers + x for x in range(DEGREE)]
    fill_tables(ext_ref, g_ref, t_ref, table_ref, gauge_ref, places)


def gauge_scratch(count, tiles):
    return [
        pltpu.VMEM((tiles, count * LINK_PAD, LANES), jnp.float32),
        pltpu.VMEM((tiles, count * GAUGE_ROWS, LANES), jnp.float32),
        pltpu.VMEM((tiles, count * TABLE_ROWS, LANES), jnp.float32),
    ]


def gauge_shapes(layers, planes):
    total = layers + 2 * DEGREE
    return [
        jax.ShapeDtypeStruct((total, TABLE_ROWS, planes), jnp.float32),
        jax.ShapeDtypeStruct((total, GAUGE_ROWS, planes), jnp.float32),
    ]


def gauge_halo(top, lo, hi, table, gauge):
    total, _, planes = table.shape
    return pl.pallas_call(
        gauge_halo_kernel,
        in_specs=in_vmem(5),
        out_specs=in_vmem(2),
        out_shape=gauge_shapes(total - 2 * DEGREE, planes),
        scratch_shapes=gauge_scratch(2 * DEGREE, planes // LANES),
        compiler_params=params(),
        cost_estimate=cost(1.5),
        name="gauge_halo",
    )(top, lo, hi, table, gauge)


def turn(gauge_ref, x, source, adjoint, tiles):
    out = {}
    for t in range(tiles):
        v = [source(k, t) for k in range(6)]
        for i in range(3):
            re = im = None
            for j in range(3):
                k = 3 * j + i if adjoint else 3 * i + j
                a = gauge_ref[x, pl.ds(k, 1), cols(t)]
                b = gauge_ref[x, pl.ds(9 + k, 1), cols(t)]
                if adjoint:
                    r, m = a * v[j] + b * v[3 + j], a * v[3 + j] - b * v[j]
                else:
                    r, m = a * v[j] - b * v[3 + j], a * v[3 + j] + b * v[j]
                re = r if re is None else re + r
                im = m if im is None else im + m
            out[i, t], out[3 + i, t] = re, im
    return out


def layer(table_ref, g, x, src, prev, first, tiles):
    z_last, z_first, y_low, y_high = lane_masks(VB)
    sums = {}

    def add(key, value, minus=False):
        have = sums.get(key)
        if have is None:
            sums[key] = -value if minus else value
        else:
            sums[key] = have - value if minus else have + value

    def hop(t, base, v, adjoint):
        both = [v[j] + v[3 + j] for j in range(3)]
        for j in range(3):
            for i in range(3):
                k = base + (3 * j + i if adjoint else 3 * i + j)
                a = table_ref[x, pl.ds(k, 1), cols(t)]
                p = table_ref[x, pl.ds(k + 9, 1), cols(t)]
                q = table_ref[x, pl.ds(k + 18, 1), cols(t)]
                add((t, 0, i), a * both[j])
                if adjoint:
                    add((t, 1, i), q * v[3 + j], True)
                    add((t, 2, i), p * v[j], True)
                else:
                    add((t, 1, i), p * v[3 + j])
                    add((t, 2, i), q * v[j])

    out = {}
    for t in range(tiles):
        c = {(k, u): src[g, x, k, :, cols(u)] for k in range(6) for u in range(tiles)}
        after, before = (t + 1) % tiles, (t - 1) % tiles
        hop(t, 0, [rot(jnp.where(y_high, c[k, t], c[k, after]), -LZ) for k in range(6)], False)
        hop(t, 27, [rot(jnp.where(y_low, c[k, t], c[k, before]), LZ) for k in range(6)], True)
        hop(
            t, 54,
            [jnp.where(z_last, rot(c[k, t], LZ - 1), rot(c[k, t], -1)) for k in range(6)],
            False,
        )
        hop(
            t, 81,
            [jnp.where(z_first, rot(c[k, t], 1 - LZ), rot(c[k, t], 1)) for k in range(6)],
            True,
        )
        for i in range(3):
            re = sums[t, 0, i] - sums[t, 1, i]
            im = sums[t, 0, i] + sums[t, 2, i]
            for k, h in ((i, re), (3 + i, im)):
                h = h + (src[g, x + 1, k, :, cols(t)] + src[g, x - 1, k, :, cols(t)])
                if first:
                    out[k, t] = (6.0 * SCALE - OFFSET) * c[k, t] - SCALE * h
                else:
                    out[k, t] = (
                        (12.0 * SCALE - 2.0 * OFFSET) * c[k, t]
                        - (2.0 * SCALE) * h
                        - prev[g, x, k, :, cols(t)]
                    )
    return out


def put(ref, g, x, values):
    for (k, t), value in values.items():
        ref[g, x, k, :, cols(t)] = value


def inner_kernel(
    start_hbm, links_hbm, a_ref, b_ref, table_ref, gauge_ref, top_ref,
    start_ref, links_ref, sems, ext_ref, g_ref, t_ref, *, layers
):
    groups = a_ref.shape[0]
    tiles = table_ref.shape[-1] // LANES
    cells = VB * layers * tiles
    copies = fetch(start_hbm, links_hbm, start_ref, links_ref, sems)
    copies[0].wait()
    gauge_own(links_ref, table_ref, gauge_ref, ext_ref, g_ref, t_ref, layers)
    for t in range(tiles):
        top_ref[0:18, cols(t)] = ext_ref[t, pl.ds((layers - 1) * LINK_PAD, 18), :]
    for copy in copies[1:]:
        copy.wait()

    def init(n, _):
        g, x = n // layers, n % layers

        def source(k, t):
            at = g * cells + t * layers + x
            return start_ref[k, pl.ds(at, VB, stride=tiles * layers), :]

        put(a_ref, g, x + DEGREE, turn(gauge_ref, x + DEGREE, source, False, tiles))
        return 0

    lax.fori_loop(0, groups * layers, init, 0)
    for level in range(1, DEGREE):
        src, dst = (a_ref, b_ref) if level % 2 else (b_ref, a_ref)
        pairs = (layers - 2 * level) // 2

        def body(n, _, src=src, dst=dst, level=level, pairs=pairs):
            g, at = n // pairs, n % pairs
            for u in range(2):
                x = DEGREE + level + 2 * at + u
                put(dst, g, x, layer(table_ref, g, x, src, dst, level == 1, tiles))
            return 0

        if pairs > 0:
            lax.fori_loop(0, groups * pairs, body, 0)


def run_inner(start2, links2, layers, tiles):
    comps, rows, _ = start2.shape
    planes = tiles * LANES
    groups = rows // (VB * layers * tiles)
    state = jax.ShapeDtypeStruct((groups, layers + 2 * DEGREE, comps, VB, planes), jnp.float32)
    top = jax.ShapeDtypeStruct((GAUGE_ROWS, planes), jnp.float32)
    return pl.pallas_call(
        functools.partial(inner_kernel, layers=layers),
        in_specs=[pl.BlockSpec(memory_space=pltpu.HBM)] * 2,
        out_specs=in_vmem(5),
        out_shape=[state, state] + gauge_shapes(layers, planes) + [top],
        scratch_shapes=fetch_scratch(start2, links2) + gauge_scratch(layers, tiles),
        compiler_params=params(),
        cost_estimate=cost(8),
        name="inner",
    )(start2, links2)


def outer_kernel(
    place_ref, lo_ref, hi_ref, table_ref, gauge_ref, a_in, b_in,
    half_ref, keep_ref, give_ref, a_ref, b_ref, pack_ref, *, layers, parts
):
    groups = a_ref.shape[0]
    total = layers + 2 * DEGREE
    planes = table_ref.shape[-1]
    tiles = planes // LANES

    def init(n, _):
        g, x = n // DEGREE, n % DEGREE
        for ref, at in ((lo_ref, x), (hi_ref, x + DEGREE + layers)):

            def source(k, t, ref=ref):
                return ref[x, g, k, :, cols(t)].astype(jnp.float32)

            put(a_ref, g, at, turn(gauge_ref, at, source, False, tiles))
        for at in (x + DEGREE, total - 2 * DEGREE + x):
            a_ref[g, at] = a_in[g, at]
            b_ref[g, at] = b_in[g, at]
        return 0

    lax.fori_loop(0, groups * DEGREE, init, 0)
    for level in range(1, DEGREE):
        src, dst = (a_ref, b_ref) if level % 2 else (b_ref, a_ref)

        def body(n, _, src=src, dst=dst, level=level):
            g, at = n // DEGREE, n % DEGREE
            for x in (level + at, total - DEGREE - level + at):
                put(dst, g, x, layer(table_ref, g, x, src, dst, level == 1, tiles))
            return 0

        lax.fori_loop(0, groups * DEGREE, body, 0)
    src, prev = (a_ref, b_ref) if DEGREE % 2 else (b_ref, a_ref)

    def last(n, _):
        g, at = n // (layers // 2), n % (layers // 2)
        for u in range(2):
            x = 2 * at + u
            value = layer(table_ref, g, x + DEGREE, src, prev, False, tiles)
            value = turn(gauge_ref, x + DEGREE, lambda k, t: value[k, t], True, tiles)
            for (k, t), v in value.items():
                rounded = v.astype(jnp.bfloat16)
                half_ref[g, x, k, :, cols(t)] = rounded
                pack_ref[g, k, pl.ds(pl.multiple_of(x * VB, VB), VB), cols(t)] = rounded.astype(
                    jnp.float32
                )
        return 0

    lax.fori_loop(0, groups * (layers // 2), last, 0)

    side, base = place_ref[0], place_ref[1]
    pairs = parts // 2
    width = planes // parts
    for g in range(groups):
        for k in range(6):
            turned = jnp.concatenate([pack_ref[g, k, :, cols(t)].T for t in range(tiles)], axis=0)
            for m in range(pairs):
                near = turned[m * width : (m + 1) * width].astype(jnp.bfloat16)
                far = turned[(pairs + m) * width : (pairs + m + 1) * width].astype(jnp.bfloat16)
                keep_ref[base ^ m, g, k] = jnp.where(side == 0, near, far)
                give_ref[base ^ m, g, k] = jnp.where(side == 0, far, near)


def run_outer(place, lo, hi, table, gauge, a, b, layers, parts):
    groups, total, comps, _, planes = a.shape
    width = planes // parts
    cells = layers * VB
    block = jax.ShapeDtypeStruct((parts // 2, groups, comps, width, cells), jnp.bfloat16)
    half = jax.ShapeDtypeStruct((groups, layers, comps, VB, planes), jnp.bfloat16)
    return pl.pallas_call(
        functools.partial(outer_kernel, layers=layers, parts=parts),
        in_specs=[in_smem()] + in_vmem(6),
        out_specs=in_vmem(3),
        out_shape=[half, block, block],
        scratch_shapes=[
            pltpu.VMEM(a.shape, jnp.float32),
            pltpu.VMEM(a.shape, jnp.float32),
            pltpu.VMEM((groups, comps, cells, planes), jnp.float32),
        ],
        compiler_params=params(),
        cost_estimate=cost(16),
        name="outer",
    )(place, lo, hi, table, gauge, a, b)


def weight_kernel(half_ref, weight_ref):
    groups, layers, _, _, planes = half_ref.shape
    vectors = groups * VB
    for g in range(groups):
        for x in range(layers):
            for part in range(2):
                for c in range(3):
                    for p in range(2):
                        value = half_ref[g, x, (part ^ p) * 3 + c]
                        if p == 1 and part == 1:
                            value = -value
                        weight_ref[
                            pl.ds((x * 2 + p) * vectors + g * VB, VB),
                            pl.ds((part * 3 + c) * planes, planes),
                        ] = value


def run_weights(half):
    groups, layers, comps, _, planes = half.shape
    return pl.pallas_call(
        weight_kernel,
        in_specs=in_vmem(1),
        out_specs=in_vmem(1)[0],
        out_shape=jax.ShapeDtypeStruct((layers * 2 * groups * VB, comps * planes), jnp.bfloat16),
        compiler_params=params(),
        cost_estimate=cost(0.7),
        name="weights",
    )(half)


def corr_kernel(place_ref, stored_ref, weight_ref, out_ref, *, layers):
    span, block = out_ref.shape
    _, comps, _, planes = stored_ref.shape
    rows = jnp.concatenate(
        [stored_ref[:, k].reshape(block * layers, planes) for k in range(comps)], axis=1
    )
    full = lax.dot_general(
        rows, weight_ref[...], (((1,), (1,)), ((), ())), preferred_element_type=jnp.float32
    )
    layer_of_row = lax.broadcasted_iota(jnp.int32, (block * layers, span), 0) % layers
    kept = jnp.zeros((block * layers, span), jnp.float32)
    for x in range(layers):
        kept = jnp.where(layer_of_row == x, full[:, x * span : (x + 1) * span], kept)
    out_ref[...] = jnp.sum(kept.reshape(block, layers, span), axis=1).T


def run_corr(place, stored, weights, owners):
    count, comps, layers, planes = stored.shape
    block = count // owners
    span = weights.shape[0] // layers
    grid_spec = pltpu.PrefetchScalarGridSpec(
        num_scalar_prefetch=1,
        grid=(owners,),
        in_specs=[
            pl.BlockSpec((block, comps, layers, planes), lambda g, s: (g, 0, 0, 0)),
            pl.BlockSpec(memory_space=pltpu.VMEM),
        ],
        out_specs=pl.BlockSpec((pl.Squeezed(), span, block), lambda g, s: (g ^ s[2], 0, 0)),
    )
    return pl.pallas_call(
        functools.partial(corr_kernel, layers=layers),
        grid_spec=grid_spec,
        out_shape=jax.ShapeDtypeStruct((owners, span, block), jnp.float32),
        compiler_params=params(40 * 2**20),
        cost_estimate=cost(11),
        name="correlate",
    )(place, stored, weights)


def merge_kernel(keep_ref, got_ref, *out_refs):
    for step, ref in enumerate(out_refs):
        ref[0] = keep_ref[step]
        ref[1] = got_ref[step]


def run_merge(keep, got):
    shape = jax.ShapeDtypeStruct((2,) + keep.shape[1:], keep.dtype)
    return pl.pallas_call(
        merge_kernel,
        in_specs=in_vmem(2),
        out_specs=in_vmem(keep.shape[0]),
        out_shape=[shape] * keep.shape[0],
        compiler_params=params(),
        cost_estimate=cost(0.7),
        name="merge",
    )(keep, got)


def order_kernel(order_ref, *, layers, groups):
    depth = order_ref.shape[0]
    cells = layers * VB
    vectors = groups * VB
    row = lax.broadcasted_iota(jnp.int32, (depth, depth), 0)
    col = lax.broadcasted_iota(jnp.int32, (depth, depth), 1)
    bit, rest = row // (groups * cells), row % (groups * cells)
    group, cell = rest // cells, rest % cells
    wanted = ((cell // VB) * 2 + bit) * vectors + group * VB + cell % VB
    order_ref[...] = (wanted == col).astype(jnp.bfloat16)


def run_order(groups, layers):
    depth = 2 * groups * layers * VB
    return pl.pallas_call(
        functools.partial(order_kernel, layers=layers, groups=groups),
        out_specs=in_vmem(1)[0],
        out_shape=jax.ShapeDtypeStruct((depth, depth), jnp.bfloat16),
        compiler_params=params(),
        cost_estimate=cost(2),
        name="order",
    )()


def arrange_kernel(place_ref, order_ref, *refs, layers, per):
    out_ref = refs[-1]
    groups, comps, width = refs[0].shape[1:4]
    span = 2 * groups * VB
    pieces = []
    for ref in refs[:-1]:
        for h in range(2):
            for pair in range(comps // 2):
                lanes = [ref[h, g, 2 * pair + bit] for bit in range(2) for g in range(groups)]
                pieces.append(jnp.concatenate(lanes, axis=1))
    moved = jnp.dot(
        jnp.concatenate(pieces, axis=0), order_ref[...], preferred_element_type=jnp.float32
    )
    for step in range(len(refs) - 1):
        source = place_ref[3] ^ step
        slice_at, chip = lax.rem(source, per), source // per
        for h in range(2):
            first = (2 * chip + (place_ref[4] ^ h)) * layers
            at = (2 * step + h) * (comps // 2) * width
            for x in range(layers):
                out_ref[slice_at, first + x] = jnp.concatenate(
                    [
                        moved[at + p * width : at + (p + 1) * width, x * span : (x + 1) * span]
                        for p in range(comps // 2)
                    ],
                    axis=1,
                ).astype(jnp.bfloat16)


def run_arrange(place, order, blocks, shape, layers, per):
    return pl.pallas_call(
        functools.partial(arrange_kernel, layers=layers, per=per),
        in_specs=[in_smem()] + in_vmem(1 + len(blocks)),
        out_specs=in_vmem(1)[0],
        out_shape=jax.ShapeDtypeStruct(shape, jnp.bfloat16),
        compiler_params=params(),
        cost_estimate=cost(3),
        name="arrange",
    )(place, order, *blocks)


def shards(start_block, gauge_links, stored_vectors, *, n_tm, n_space):
    _, parts, colours, vectors, layers, planes = start_block.shape
    comps = parts * colours
    tm, space = lax.axis_index("tm"), lax.axis_index("space")
    per = n_tm // n_space
    pairs = n_tm // 2
    groups = vectors // VB

    def base_of(i, j):
        return (j // 2 * per + i % per) ^ (i // per % 2 * per)

    place = jnp.stack(
        [
            space % 2 ^ tm // pairs,
            base_of(tm, space),
            space,
            tm % pairs ^ space % 2 * per,
            tm // pairs ^ space * per // pairs,
        ]
    ).astype(jnp.int32)

    tiles = planes // LANES

    def by_tile(value, *lead):
        value = value.reshape(-1, layers, tiles, LANES)
        return jnp.transpose(value, (0, 2, 1, 3)).reshape(*lead, LANES)

    start2 = by_tile(start_block, comps, vectors * tiles * layers)
    links2 = by_tile(gauge_links, LINK_ROWS * tiles * layers)
    up = [(i, (i + 1) % n_space) for i in range(n_space)]
    down = [((i + 1) % n_space, i) for i in range(n_space)]

    up_links, down_links, up_halo, down_halo = run_pack(start2, links2, layers, tiles)
    lo_links = lax.ppermute(up_links, "space", up)
    hi_links = lax.ppermute(down_links, "space", down)
    lo = lax.ppermute(up_halo, "space", up)
    hi = lax.ppermute(down_halo, "space", down)
    order = run_order(groups, layers)

    a, b, table, gauge, top = run_inner(start2, links2, layers, tiles)
    table, gauge = gauge_halo(top, lo_links, hi_links, table, gauge)
    half, keep, give = run_outer(place, lo, hi, table, gauge, a, b, layers, n_tm)

    weights = run_weights(half)
    got = lax.ppermute(give, "space", [(i, i ^ 1) for i in range(n_space)])
    blocks = run_merge(keep, got)
    stored = stored_vectors.reshape(stored_vectors.shape[1], comps, layers, planes)
    sent = [None] * pairs
    digits = pairs.bit_length() - 1
    for step in sorted(range(pairs), key=lambda n: f"{n:0{digits}b}"[::-1]):
        table_of = []
        for i in range(n_tm):
            for j in range(n_space):
                to = (j % 2 ^ i // pairs) * pairs + (base_of(i, j) ^ step)
                table_of.append((i * n_space + j, to * n_space + i // per))
        sent[step] = lax.ppermute(blocks[step], ("tm", "space"), table_of)
    partial = run_corr(place, stored, weights, n_space)
    partial, *sent = lax.optimization_barrier((partial, *sent))
    sums = {d: partial[d] for d in range(n_space)}

    bit = 1
    while bit < n_space:
        going = [d for d in sums if d & bit]
        partner = [(i, i ^ bit) for i in range(n_space)]
        came = lax.ppermute(jnp.stack([sums[d] for d in going]), "space", partner)
        for n, d in enumerate(going):
            sums[d ^ bit] = sums[d ^ bit] + came[n]
            del sums[d]
        bit *= 2
    correlations = sums[0].T[None]

    shape = (per, n_space * layers, planes // n_tm, comps * vectors)
    return correlations, run_arrange(place, order, sent, shape, layers, per)


def solution(mesh):
    in_specs = (
        P("tm", None, None, None, "space", None),
        P("tm", None, None, None, None, "space", None),
        P("tm", None, None, None, "space", None),
    )
    out_specs = (P("tm", "space", None), P("space", None, "tm", None))
    body = functools.partial(shards, n_tm=mesh.shape["tm"], n_space=mesh.shape["space"])
    return jax.shard_map(body, mesh=mesh, in_specs=in_specs, out_specs=out_specs, check_vma=False)
```

```python
import functools

import jax
import jax.numpy as jnp
from jax import lax
from jax.experimental import pallas as pl
from jax.experimental.pallas import tpu as pltpu
from jax.sharding import PartitionSpec as P

DEGREE = 4
LZ = 16
LANES = 128
VB = 16

lower_edge = 0.5
upper_edge = 12.5
SCALE = 2.0 / (upper_edge - lower_edge)
OFFSET = (upper_edge + lower_edge) / (upper_edge - lower_edge)

VMEM_LIMIT = 60 * 2**20
LINK_ROWS = 54
LINK_PAD = 56
TABLE_ROWS = 112
GAUGE_ROWS = 24


def params(limit=24 * 2**20):
    return pltpu.CompilerParams(vmem_limit_bytes=limit)


def in_vmem(count):
    return [pl.BlockSpec(memory_space=pltpu.VMEM)] * count


def in_smem():
    return pl.BlockSpec(memory_space=pltpu.SMEM)


def cost(microseconds):
    return pl.CostEstimate(
        flops=1_000_000, bytes_accessed=int(microseconds * 3_000_000), transcendentals=0
    )


def fetch(start_hbm, links_hbm, start_ref, links_ref, sems):
    comps = start_ref.shape[0]
    copies = [pltpu.make_async_copy(links_hbm, links_ref, sems.at[comps])] + [
        pltpu.make_async_copy(start_hbm.at[k], start_ref.at[k], sems.at[k]) for k in range(comps)
    ]
    for copy in copies:
        copy.start()
    return copies


def fetch_scratch(start2, links2):
    return [
        pltpu.VMEM(start2.shape, jnp.float32),
        pltpu.VMEM(links2.shape, jnp.float32),
        pltpu.SemaphoreType.DMA((start2.shape[0] + 1,)),
    ]


def pack_kernel(
    start_hbm, links_hbm, up_links_ref, down_links_ref, up_ref, down_ref,
    start_ref, links_ref, sems, *, layers, tiles
):
    comps, groups = up_ref.shape[2], up_ref.shape[1]
    cells = VB * layers * tiles
    copies = fetch(start_hbm, links_hbm, start_ref, links_ref, sems)
    copies[0].wait()
    for x in range(layers):
        for t in range(tiles):
            rows = links_ref[pl.ds(t * layers + x, LINK_ROWS, stride=tiles * layers), :]
            if x < DEGREE:
                down_links_ref[x, :, cols(t)] = rows.astype(jnp.bfloat16)
            if x >= layers - DEGREE:
                up_links_ref[x - layers + DEGREE, :, cols(t)] = rows.astype(jnp.bfloat16)
    for k in range(comps):
        copies[1 + k].wait()
        for x in range(layers):
            for t in range(tiles):
                for g in range(groups):
                    half = start_ref[
                        k, pl.ds(g * cells + t * layers + x, VB, stride=tiles * layers), :
                    ].astype(jnp.bfloat16)
                    if x < DEGREE:
                        down_ref[x, g, k, :, cols(t)] = half
                    if x >= layers - DEGREE:
                        up_ref[x - layers + DEGREE, g, k, :, cols(t)] = half


def run_pack(start2, links2, layers, tiles):
    comps, rows, _ = start2.shape
    planes = tiles * LANES
    groups = rows // (VB * layers * tiles)
    link = jax.ShapeDtypeStruct((DEGREE, LINK_ROWS, planes), jnp.bfloat16)
    halo = jax.ShapeDtypeStruct((DEGREE, groups, comps, VB, planes), jnp.bfloat16)
    return pl.pallas_call(
        functools.partial(pack_kernel, layers=layers, tiles=tiles),
        in_specs=[pl.BlockSpec(memory_space=pltpu.HBM)] * 2,
        out_specs=in_vmem(4),
        out_shape=[link, link, halo, halo],
        scratch_shapes=fetch_scratch(start2, links2),
        compiler_params=params(VMEM_LIMIT),
        cost_estimate=cost(2.5),
        name="pack",
    )(start2, links2)


def mat_mul(a, b, conj_b=False):
    out_re, out_im = [], []
    for i in range(3):
        for j in range(3):
            re = im = None
            for k in range(3):
                ar, ai = a[0][3 * i + k], a[1][3 * i + k]
                if conj_b:
                    br, bi = b[0][3 * j + k], b[1][3 * j + k]
                    r = ar * br + ai * bi
                    m = ai * br - ar * bi
                else:
                    br, bi = b[0][3 * k + j], b[1][3 * k + j]
                    r = ar * br - ai * bi
                    m = ar * bi + ai * br
                re = r if re is None else re + r
                im = m if im is None else im + m
            out_re.append(re)
            out_im.append(im)
    return out_re, out_im


def rot(v, steps):
    return pltpu.roll(v, steps % LANES, 1)


def shifts(value, masks):
    z_last, z_first, y_low, y_high = masks
    tiles = len(value)
    up = [rot(v, LZ) for v in value]
    down = [rot(v, -LZ) for v in value]
    return (
        [jnp.where(y_low, down[t], down[(t + 1) % tiles]) for t in range(tiles)],
        [jnp.where(y_high, up[t], up[(t - 1) % tiles]) for t in range(tiles)],
        [rot(jnp.where(z_first, up[t], value[t]), -1) for t in range(tiles)],
        [rot(jnp.where(z_last, down[t], value[t]), 1) for t in range(tiles)],
    )


def lane_masks(rows):
    lane = lax.broadcasted_iota(jnp.int32, (rows, LANES), 1)
    return lane % LZ == LZ - 1, lane % LZ == 0, lane < LANES - LZ, lane >= LZ


def cols(t):
    return slice(t * LANES, (t + 1) * LANES)


def rows_at(ref, t, first):
    return (
        [ref[t, pl.ds(first + k, 1), :] for k in range(9)],
        [ref[t, pl.ds(first + 9 + k, 1), :] for k in range(9)],
    )


def put_rows(ref, t, first, g):
    for k in range(9):
        ref[t, pl.ds(first + k, 1), :] = g[0][k]
        ref[t, pl.ds(first + 9 + k, 1), :] = g[1][k]


def unit_rows():
    one = jnp.ones((1, LANES), jnp.float32)
    zero = jnp.zeros((1, LANES), jnp.float32)
    return [one if k % 4 == 0 else zero for k in range(9)], [zero] * 9


def fill_tables(ext_ref, g_ref, t_ref, table_ref, gauge_ref, places):
    tiles = ext_ref.shape[0]
    total = len(places)
    masks = lane_masks(total)

    def column(ref, k, stride):
        return [ref[t, pl.ds(k, total, stride=stride), :] for t in range(tiles)]

    gauge = [column(g_ref, k, GAUGE_ROWS) for k in range(18)]
    for d in (1, 2):
        link = [column(ext_ref, 18 * d + k, LINK_PAD) for k in range(18)]
        ahead = [shifts(v, masks)[2 * (d - 1)] for v in gauge]
        turned = []
        for t in range(tiles):
            here, there, mid = (
                ([v[t] for v in field[:9]], [v[t] for v in field[9:]])
                for field in (gauge, ahead, link)
            )
            turned.append(mat_mul(mat_mul(here, mid), there, conj_b=True))
        base = 54 * (d - 1)
        for k in range(9):
            re, im = [turned[t][0][k] for t in range(tiles)], [turned[t][1][k] for t in range(tiles)]
            back_re, back_im = shifts(re, masks)[2 * d - 1], shifts(im, masks)[2 * d - 1]
            for t in range(tiles):
                for at, value in (
                    (0, re[t]),
                    (9, re[t] + im[t]),
                    (18, im[t] - re[t]),
                    (27, back_re[t]),
                    (36, back_re[t] + back_im[t]),
                    (45, back_im[t] - back_re[t]),
                ):
                    t_ref[t, pl.ds(base + at + k, total, stride=TABLE_ROWS), :] = value
    for n, x in enumerate(places):
        for t in range(tiles):
            table_ref[x, 0:108, cols(t)] = t_ref[t, pl.ds(n * TABLE_ROWS, 108), :]
            gauge_ref[x, 0:18, cols(t)] = g_ref[t, pl.ds(n * GAUGE_ROWS, 18), :]


def gauge_own(links_ref, table_ref, gauge_ref, ext_ref, g_ref, t_ref, layers):
    tiles = ext_ref.shape[0]
    for t in range(tiles):
        for x in range(layers):
            ext_ref[t, pl.ds(x * LINK_PAD, LINK_ROWS), :] = links_ref[
                pl.ds(t * layers + x, LINK_ROWS, stride=tiles * layers), :
            ]
    for t in range(tiles):
        g = unit_rows()
        put_rows(g_ref, t, 0, g)
        for x in range(layers - 1):
            g = mat_mul(g, rows_at(ext_ref, t, x * LINK_PAD))
            put_rows(g_ref, t, (x + 1) * GAUGE_ROWS, g)
    fill_tables(
        ext_ref, g_ref, t_ref, table_ref, gauge_ref, [DEGREE + x for x in range(layers)]
    )


def gauge_halo_kernel(
    top_ref, lo_ref, hi_ref, table_in, gauge_in, table_ref, gauge_ref, ext_ref, g_ref, t_ref
):
    layers = table_ref.shape[0] - 2 * DEGREE
    for x in range(DEGREE, DEGREE + layers):
        table_ref[x] = table_in[x]
        gauge_ref[x] = gauge_in[x]
    tiles = ext_ref.shape[0]
    for t in range(tiles):
        for x in range(DEGREE):
            ext_ref[t, pl.ds(x * LINK_PAD, LINK_ROWS), :] = lo_ref[x, :, cols(t)].astype(jnp.float32)
            ext_ref[t, pl.ds((DEGREE + x) * LINK_PAD, LINK_ROWS), :] = hi_ref[x, :, cols(t)].astype(
                jnp.float32
            )
    for t in range(tiles):
        g = unit_rows()
        for x in range(DEGREE - 1, -1, -1):
            g = mat_mul(g, rows_at(ext_ref, t, x * LINK_PAD), conj_b=True)
            put_rows(g_ref, t, x * GAUGE_ROWS, g)
        top = DEGREE + layers - 1
        g = tuple(
            [gauge_in[top, pl.ds(first + k, 1), cols(t)] for k in range(9)] for first in (0, 9)
        )
        link = tuple(
            [top_ref[pl.ds(first + k, 1), cols(t)] for k in range(9)]
            for first in (0, 9)
        )
        for x in range(DEGREE):
            g = mat_mul(g, link)
            put_rows(g_ref, t, (DEGREE + x) * GAUGE_ROWS, g)
            if x < DEGREE - 1:
                link = rows_at(ext_ref, t, (DEGREE + x) * LINK_PAD)
    places = list(range(DEGREE)) + [DEGREE + layers + x for x in range(DEGREE)]
    fill_tables(ext_ref, g_ref, t_ref, table_ref, gauge_ref, places)


def gauge_scratch(count, tiles):
    return [
        pltpu.VMEM((tiles, count * LINK_PAD, LANES), jnp.float32),
        pltpu.VMEM((tiles, count * GAUGE_ROWS, LANES), jnp.float32),
        pltpu.VMEM((tiles, count * TABLE_ROWS, LANES), jnp.float32),
    ]


def gauge_shapes(layers, planes):
    total = layers + 2 * DEGREE
    return [
        jax.ShapeDtypeStruct((total, TABLE_ROWS, planes), jnp.float32),
        jax.ShapeDtypeStruct((total, GAUGE_ROWS, planes), jnp.float32),
    ]


def gauge_halo(top, lo, hi, table, gauge):
    total, _, planes = table.shape
    return pl.pallas_call(
        gauge_halo_kernel,
        in_specs=in_vmem(5),
        out_specs=in_vmem(2),
        out_shape=gauge_shapes(total - 2 * DEGREE, planes),
        scratch_shapes=gauge_scratch(2 * DEGREE, planes // LANES),
        compiler_params=params(),
        cost_estimate=cost(1.5),
        name="gauge_halo",
    )(top, lo, hi, table, gauge)


def turn(gauge_ref, x, source, adjoint, tiles):
    out = {}
    for t in range(tiles):
        v = [source(k, t) for k in range(6)]
        for i in range(3):
            re = im = None
            for j in range(3):
                k = 3 * j + i if adjoint else 3 * i + j
                a = gauge_ref[x, pl.ds(k, 1), cols(t)]
                b = gauge_ref[x, pl.ds(9 + k, 1), cols(t)]
                if adjoint:
                    r, m = a * v[j] + b * v[3 + j], a * v[3 + j] - b * v[j]
                else:
                    r, m = a * v[j] - b * v[3 + j], a * v[3 + j] + b * v[j]
                re = r if re is None else re + r
                im = m if im is None else im + m
            out[i, t], out[3 + i, t] = re, im
    return out


def layer(table_ref, g, x, src, prev, first, tiles):
    z_last, z_first, y_low, y_high = lane_masks(VB)
    sums = {}

    def add(key, value, minus=False):
        have = sums.get(key)
        if have is None:
            sums[key] = -value if minus else value
        else:
            sums[key] = have - value if minus else have + value

    def hop(t, base, v, adjoint):
        both = [v[j] + v[3 + j] for j in range(3)]
        for j in range(3):
            for i in range(3):
                k = base + (3 * j + i if adjoint else 3 * i + j)
                a = table_ref[x, pl.ds(k, 1), cols(t)]
                p = table_ref[x, pl.ds(k + 9, 1), cols(t)]
                q = table_ref[x, pl.ds(k + 18, 1), cols(t)]
                add((t, 0, i), a * both[j])
                if adjoint:
                    add((t, 1, i), q * v[3 + j], True)
                    add((t, 2, i), p * v[j], True)
                else:
                    add((t, 1, i), p * v[3 + j])
                    add((t, 2, i), q * v[j])

    out = {}
    for t in range(tiles):
        c = {(k, u): src[g, x, k, :, cols(u)] for k in range(6) for u in range(tiles)}
        after, before = (t + 1) % tiles, (t - 1) % tiles
        hop(t, 0, [rot(jnp.where(y_high, c[k, t], c[k, after]), -LZ) for k in range(6)], False)
        hop(t, 27, [rot(jnp.where(y_low, c[k, t], c[k, before]), LZ) for k in range(6)], True)
        hop(
            t, 54,
            [jnp.where(z_last, rot(c[k, t], LZ - 1), rot(c[k, t], -1)) for k in range(6)],
            False,
        )
        hop(
            t, 81,
            [jnp.where(z_first, rot(c[k, t], 1 - LZ), rot(c[k, t], 1)) for k in range(6)],
            True,
        )
        for i in range(3):
            re = sums[t, 0, i] - sums[t, 1, i]
            im = sums[t, 0, i] + sums[t, 2, i]
            for k, h in ((i, re), (3 + i, im)):
                h = h + (src[g, x + 1, k, :, cols(t)] + src[g, x - 1, k, :, cols(t)])
                if first:
                    out[k, t] = (6.0 * SCALE - OFFSET) * c[k, t] - SCALE * h
                else:
                    out[k, t] = (
                        (12.0 * SCALE - 2.0 * OFFSET) * c[k, t]
                        - (2.0 * SCALE) * h
                        - prev[g, x, k, :, cols(t)]
                    )
    return out


def put(ref, g, x, values):
    for (k, t), value in values.items():
        ref[g, x, k, :, cols(t)] = value


def inner_kernel(
    start_hbm, links_hbm, a_ref, b_ref, table_ref, gauge_ref, top_ref,
    start_ref, links_ref, sems, ext_ref, g_ref, t_ref, *, layers
):
    groups = a_ref.shape[0]
    tiles = table_ref.shape[-1] // LANES
    cells = VB * layers * tiles
    copies = fetch(start_hbm, links_hbm, start_ref, links_ref, sems)
    copies[0].wait()
    gauge_own(links_ref, table_ref, gauge_ref, ext_ref, g_ref, t_ref, layers)
    for t in range(tiles):
        top_ref[0:18, cols(t)] = ext_ref[t, pl.ds((layers - 1) * LINK_PAD, 18), :]
    for copy in copies[1:]:
        copy.wait()

    def init(n, _):
        g, x = n // layers, n % layers

        def source(k, t):
            at = g * cells + t * layers + x
            return start_ref[k, pl.ds(at, VB, stride=tiles * layers), :]

        put(a_ref, g, x + DEGREE, turn(gauge_ref, x + DEGREE, source, False, tiles))
        return 0

    lax.fori_loop(0, groups * layers, init, 0)
    for level in range(1, DEGREE):
        src, dst = (a_ref, b_ref) if level % 2 else (b_ref, a_ref)
        pairs = (layers - 2 * level) // 2

        def body(n, _, src=src, dst=dst, level=level, pairs=pairs):
            g, at = n // pairs, n % pairs
            for u in range(2):
                x = DEGREE + level + 2 * at + u
                put(dst, g, x, layer(table_ref, g, x, src, dst, level == 1, tiles))
            return 0

        if pairs > 0:
            lax.fori_loop(0, groups * pairs, body, 0)


def run_inner(start2, links2, layers, tiles):
    comps, rows, _ = start2.shape
    planes = tiles * LANES
    groups = rows // (VB * layers * tiles)
    state = jax.ShapeDtypeStruct((groups, layers + 2 * DEGREE, comps, VB, planes), jnp.float32)
    top = jax.ShapeDtypeStruct((GAUGE_ROWS, planes), jnp.float32)
    return pl.pallas_call(
        functools.partial(inner_kernel, layers=layers),
        in_specs=[pl.BlockSpec(memory_space=pltpu.HBM)] * 2,
        out_specs=in_vmem(5),
        out_shape=[state, state] + gauge_shapes(layers, planes) + [top],
        scratch_shapes=fetch_scratch(start2, links2) + gauge_scratch(layers, tiles),
        compiler_params=params(),
        cost_estimate=cost(8),
        name="inner",
    )(start2, links2)


def outer_kernel(
    place_ref, lo_ref, hi_ref, table_ref, gauge_ref, a_in, b_in,
    half_ref, keep_ref, give_ref, a_ref, b_ref, pack_ref, *, layers, parts
):
    groups = a_ref.shape[0]
    total = layers + 2 * DEGREE
    planes = table_ref.shape[-1]
    tiles = planes // LANES

    def init(n, _):
        g, x = n // DEGREE, n % DEGREE
        for ref, at in ((lo_ref, x), (hi_ref, x + DEGREE + layers)):

            def source(k, t, ref=ref):
                return ref[x, g, k, :, cols(t)].astype(jnp.float32)

            put(a_ref, g, at, turn(gauge_ref, at, source, False, tiles))
        for at in (x + DEGREE, total - 2 * DEGREE + x):
            a_ref[g, at] = a_in[g, at]
            b_ref[g, at] = b_in[g, at]
        return 0

    lax.fori_loop(0, groups * DEGREE, init, 0)
    for level in range(1, DEGREE):
        src, dst = (a_ref, b_ref) if level % 2 else (b_ref, a_ref)

        def body(n, _, src=src, dst=dst, level=level):
            g, at = n // DEGREE, n % DEGREE
            for x in (level + at, total - DEGREE - level + at):
                put(dst, g, x, layer(table_ref, g, x, src, dst, level == 1, tiles))
            return 0

        lax.fori_loop(0, groups * DEGREE, body, 0)
    src, prev = (a_ref, b_ref) if DEGREE % 2 else (b_ref, a_ref)

    def last(n, _):
        g, at = n // (layers // 2), n % (layers // 2)
        for u in range(2):
            x = 2 * at + u
            value = layer(table_ref, g, x + DEGREE, src, prev, False, tiles)
            value = turn(gauge_ref, x + DEGREE, lambda k, t: value[k, t], True, tiles)
            for (k, t), v in value.items():
                rounded = v.astype(jnp.bfloat16)
                half_ref[g, x, k, :, cols(t)] = rounded
                pack_ref[g, k, pl.ds(pl.multiple_of(x * VB, VB), VB), cols(t)] = rounded.astype(
                    jnp.float32
                )
        return 0

    lax.fori_loop(0, groups * (layers // 2), last, 0)

    side, base = place_ref[0], place_ref[1]
    pairs = parts // 2
    width = planes // parts
    for g in range(groups):
        for k in range(6):
            turned = jnp.concatenate([pack_ref[g, k, :, cols(t)].T for t in range(tiles)], axis=0)
            for m in range(pairs):
                near = turned[m * width : (m + 1) * width].astype(jnp.bfloat16)
                far = turned[(pairs + m) * width : (pairs + m + 1) * width].astype(jnp.bfloat16)
                keep_ref[base ^ m, g, k] = jnp.where(side == 0, near, far)
                give_ref[base ^ m, g, k] = jnp.where(side == 0, far, near)


def run_outer(place, lo, hi, table, gauge, a, b, layers, parts):
    groups, total, comps, _, planes = a.shape
    width = planes // parts
    cells = layers * VB
    block = jax.ShapeDtypeStruct((parts // 2, groups, comps, width, cells), jnp.bfloat16)
    half = jax.ShapeDtypeStruct((groups, layers, comps, VB, planes), jnp.bfloat16)
    return pl.pallas_call(
        functools.partial(outer_kernel, layers=layers, parts=parts),
        in_specs=[in_smem()] + in_vmem(6),
        out_specs=in_vmem(3),
        out_shape=[half, block, block],
        scratch_shapes=[
            pltpu.VMEM(a.shape, jnp.float32),
            pltpu.VMEM(a.shape, jnp.float32),
            pltpu.VMEM((groups, comps, cells, planes), jnp.float32),
        ],
        compiler_params=params(),
        cost_estimate=cost(16),
        name="outer",
    )(place, lo, hi, table, gauge, a, b)


def weight_kernel(half_ref, weight_ref):
    groups, layers, _, _, planes = half_ref.shape
    vectors = groups * VB
    for g in range(groups):
        for x in range(layers):
            for part in range(2):
                for c in range(3):
                    for p in range(2):
                        value = half_ref[g, x, (part ^ p) * 3 + c]
                        if p == 1 and part == 1:
                            value = -value
                        weight_ref[
                            pl.ds((x * 2 + p) * vectors + g * VB, VB),
                            pl.ds((part * 3 + c) * planes, planes),
                        ] = value


def run_weights(half):
    groups, layers, comps, _, planes = half.shape
    return pl.pallas_call(
        weight_kernel,
        in_specs=in_vmem(1),
        out_specs=in_vmem(1)[0],
        out_shape=jax.ShapeDtypeStruct((layers * 2 * groups * VB, comps * planes), jnp.bfloat16),
        compiler_params=params(),
        cost_estimate=cost(0.7),
        name="weights",
    )(half)


def corr_kernel(place_ref, stored_ref, weight_ref, out_ref, *, layers):
    span, block = out_ref.shape
    _, comps, _, planes = stored_ref.shape
    rows = jnp.concatenate(
        [stored_ref[:, k].reshape(block * layers, planes) for k in range(comps)], axis=1
    )
    layer_of_row = lax.broadcasted_iota(jnp.int32, (block * layers, LANES), 0) % layers
    layer_of_lane = lax.broadcasted_iota(jnp.int32, (block * layers, LANES), 1) // span
    kept = jnp.zeros((block * layers, LANES), jnp.float32)
    width = min(2 * LANES, weight_ref.shape[0])
    for first in range(0, weight_ref.shape[0], width):
        full = lax.dot_general(
            rows,
            weight_ref[first : first + width, :],
            (((1,), (1,)), ((), ())),
            preferred_element_type=jnp.float32,
        )
        for at in range(0, width, LANES):
            here = layer_of_row == (first + at) // span + layer_of_lane
            kept = jnp.where(here, full[:, at : at + LANES], kept)
    summed = jnp.sum(kept.reshape(block, layers, LANES), axis=1)
    total = summed[:, :span]
    for at in range(span, LANES, span):
        total = total + summed[:, at : at + span]
    out_ref[...] = total.T


def run_corr(place, stored, weights, owners):
    count, comps, layers, planes = stored.shape
    block = count // owners
    span = weights.shape[0] // layers
    grid_spec = pltpu.PrefetchScalarGridSpec(
        num_scalar_prefetch=1,
        grid=(owners,),
        in_specs=[
            pl.BlockSpec((block, comps, layers, planes), lambda g, s: (g, 0, 0, 0)),
            pl.BlockSpec(memory_space=pltpu.VMEM),
        ],
        out_specs=pl.BlockSpec((pl.Squeezed(), span, block), lambda g, s: (g ^ s[2], 0, 0)),
    )
    return pl.pallas_call(
        functools.partial(corr_kernel, layers=layers),
        grid_spec=grid_spec,
        out_shape=jax.ShapeDtypeStruct((owners, span, block), jnp.float32),
        compiler_params=params(40 * 2**20),
        cost_estimate=cost(8),
        name="correlate",
    )(place, stored, weights)


def merge_kernel(keep_ref, got_ref, *out_refs):
    for step, ref in enumerate(out_refs):
        ref[0] = keep_ref[step]
        ref[1] = got_ref[step]


def run_merge(keep, got):
    shape = jax.ShapeDtypeStruct((2,) + keep.shape[1:], keep.dtype)
    return pl.pallas_call(
        merge_kernel,
        in_specs=in_vmem(2),
        out_specs=in_vmem(keep.shape[0]),
        out_shape=[shape] * keep.shape[0],
        compiler_params=params(),
        cost_estimate=cost(0.7),
        name="merge",
    )(keep, got)


def order_kernel(order_ref, *, layers, groups):
    depth = order_ref.shape[0]
    cells = layers * VB
    vectors = groups * VB
    row = lax.broadcasted_iota(jnp.int32, (depth, depth), 0)
    col = lax.broadcasted_iota(jnp.int32, (depth, depth), 1)
    bit, rest = row // (groups * cells), row % (groups * cells)
    group, cell = rest // cells, rest % cells
    wanted = ((cell // VB) * 2 + bit) * vectors + group * VB + cell % VB
    order_ref[...] = (wanted == col).astype(jnp.bfloat16)


def run_order(groups, layers):
    depth = 2 * groups * layers * VB
    return pl.pallas_call(
        functools.partial(order_kernel, layers=layers, groups=groups),
        out_specs=in_vmem(1)[0],
        out_shape=jax.ShapeDtypeStruct((depth, depth), jnp.bfloat16),
        compiler_params=params(),
        cost_estimate=cost(2),
        name="order",
    )()


def arrange_kernel(place_ref, order_ref, *refs, layers, per):
    out_ref = refs[-1]
    groups, comps, width = refs[0].shape[1:4]
    span = 2 * groups * VB
    pieces = []
    for ref in refs[:-1]:
        for h in range(2):
            for pair in range(comps // 2):
                lanes = [ref[h, g, 2 * pair + bit] for bit in range(2) for g in range(groups)]
                pieces.append(jnp.concatenate(lanes, axis=1))
    moved = jnp.dot(
        jnp.concatenate(pieces, axis=0), order_ref[...], preferred_element_type=jnp.float32
    )
    for step in range(len(refs) - 1):
        source = place_ref[3] ^ step
        slice_at, chip = lax.rem(source, per), source // per
        for h in range(2):
            first = (2 * chip + (place_ref[4] ^ h)) * layers
            at = (2 * step + h) * (comps // 2) * width
            for x in range(layers):
                out_ref[slice_at, first + x] = jnp.concatenate(
                    [
                        moved[at + p * width : at + (p + 1) * width, x * span : (x + 1) * span]
                        for p in range(comps // 2)
                    ],
                    axis=1,
                ).astype(jnp.bfloat16)


def run_arrange(place, order, blocks, shape, layers, per):
    return pl.pallas_call(
        functools.partial(arrange_kernel, layers=layers, per=per),
        in_specs=[in_smem()] + in_vmem(1 + len(blocks)),
        out_specs=in_vmem(1)[0],
        out_shape=jax.ShapeDtypeStruct(shape, jnp.bfloat16),
        compiler_params=params(),
        cost_estimate=cost(3),
        name="arrange",
    )(place, order, *blocks)


def shards(start_block, gauge_links, stored_vectors, *, n_tm, n_space):
    _, parts, colours, vectors, layers, planes = start_block.shape
    comps = parts * colours
    tm, space = lax.axis_index("tm"), lax.axis_index("space")
    per = n_tm // n_space
    pairs = n_tm // 2
    groups = vectors // VB

    def base_of(i, j):
        return (j // 2 * per + i % per) ^ (i // per % 2 * per)

    place = jnp.stack(
        [
            space % 2 ^ tm // pairs,
            base_of(tm, space),
            space,
            tm % pairs ^ space % 2 * per,
            tm // pairs ^ space * per // pairs,
        ]
    ).astype(jnp.int32)

    tiles = planes // LANES

    def by_tile(value, *lead):
        value = value.reshape(-1, layers, tiles, LANES)
        return jnp.transpose(value, (0, 2, 1, 3)).reshape(*lead, LANES)

    start2 = by_tile(start_block, comps, vectors * tiles * layers)
    links2 = by_tile(gauge_links, LINK_ROWS * tiles * layers)
    up = [(i, (i + 1) % n_space) for i in range(n_space)]
    down = [((i + 1) % n_space, i) for i in range(n_space)]

    up_links, down_links, up_halo, down_halo = run_pack(start2, links2, layers, tiles)
    lo_links = lax.ppermute(up_links, "space", up)
    hi_links = lax.ppermute(down_links, "space", down)
    lo = lax.ppermute(up_halo, "space", up)
    hi = lax.ppermute(down_halo, "space", down)
    order = run_order(groups, layers)

    a, b, table, gauge, top = run_inner(start2, links2, layers, tiles)
    table, gauge = gauge_halo(top, lo_links, hi_links, table, gauge)
    half, keep, give = run_outer(place, lo, hi, table, gauge, a, b, layers, n_tm)

    weights = run_weights(half)
    got = lax.ppermute(give, "space", [(i, i ^ 1) for i in range(n_space)])
    blocks = run_merge(keep, got)
    stored = stored_vectors.reshape(stored_vectors.shape[1], comps, layers, planes)
    sent = [None] * pairs
    digits = pairs.bit_length() - 1
    for step in sorted(range(pairs), key=lambda n: f"{n:0{digits}b}"[::-1]):
        table_of = []
        for i in range(n_tm):
            for j in range(n_space):
                to = (j % 2 ^ i // pairs) * pairs + (base_of(i, j) ^ step)
                table_of.append((i * n_space + j, to * n_space + i // per))
        sent[step] = lax.ppermute(blocks[step], ("tm", "space"), table_of)
    partial = run_corr(place, stored, weights, n_space)
    partial, *sent[:-1] = lax.optimization_barrier((partial, *sent[:-1]))
    total = partial[0]
    for distance in range(1, n_space):
        partner = [(i, i ^ distance) for i in range(n_space)]
        total = total + lax.ppermute(partial[distance], "space", partner)
    correlations = total.T[None]

    shape = (per, n_space * layers, planes // n_tm, comps * vectors)
    return correlations, run_arrange(place, order, sent, shape, layers, per)


def solution(mesh):
    in_specs = (
        P("tm", None, None, None, "space", None),
        P("tm", None, None, None, None, "space", None),
        P("tm", None, None, None, "space", None),
    )
    out_specs = (P("tm", "space", None), P("space", None, "tm", None))
    body = functools.partial(shards, n_tm=mesh.shape["tm"], n_space=mesh.shape["space"])
    return jax.shard_map(body, mesh=mesh, in_specs=in_specs, out_specs=out_specs, check_vma=False)
```

```python
import functools

import jax
import jax.numpy as jnp
from jax import lax
from jax.experimental import pallas as pl
from jax.experimental.pallas import tpu as pltpu
from jax.sharding import PartitionSpec as P

DEGREE = 4
LZ = 16
LANES = 128
VB = 16

lower_edge = 0.5
upper_edge = 12.5
SCALE = 2.0 / (upper_edge - lower_edge)
OFFSET = (upper_edge + lower_edge) / (upper_edge - lower_edge)

VMEM_LIMIT = 60 * 2**20
LINK_ROWS = 54
LINK_PAD = 56
TABLE_ROWS = 112
GAUGE_ROWS = 24


def params(limit=24 * 2**20):
    return pltpu.CompilerParams(vmem_limit_bytes=limit)


def in_vmem(count):
    return [pl.BlockSpec(memory_space=pltpu.VMEM)] * count


def in_smem():
    return pl.BlockSpec(memory_space=pltpu.SMEM)


def cost(microseconds):
    return pl.CostEstimate(
        flops=1_000_000, bytes_accessed=int(microseconds * 3_000_000), transcendentals=0
    )


def fetch(start_hbm, links_hbm, start_ref, links_ref, sems):
    comps = start_ref.shape[0]
    copies = [pltpu.make_async_copy(links_hbm, links_ref, sems.at[comps])] + [
        pltpu.make_async_copy(start_hbm.at[k], start_ref.at[k], sems.at[k]) for k in range(comps)
    ]
    for copy in copies:
        copy.start()
    return copies


def fetch_scratch(start2, links2):
    return [
        pltpu.VMEM(start2.shape, jnp.float32),
        pltpu.VMEM(links2.shape, jnp.float32),
        pltpu.SemaphoreType.DMA((start2.shape[0] + 1,)),
    ]


def pack_kernel(
    start_hbm, links_hbm, up_links_ref, down_links_ref, up_ref, down_ref,
    start_ref, links_ref, sems, *, layers, tiles
):
    comps, groups = up_ref.shape[2], up_ref.shape[1]
    cells = VB * layers * tiles
    copies = fetch(start_hbm, links_hbm, start_ref, links_ref, sems)
    copies[0].wait()
    for x in range(layers):
        for t in range(tiles):
            rows = links_ref[pl.ds(t * layers + x, LINK_ROWS, stride=tiles * layers), :]
            if x < DEGREE:
                down_links_ref[x, :, cols(t)] = rows.astype(jnp.bfloat16)
            if x >= layers - DEGREE:
                up_links_ref[x - layers + DEGREE, :, cols(t)] = rows.astype(jnp.bfloat16)
    for k in range(comps):
        copies[1 + k].wait()
        for x in range(layers):
            for t in range(tiles):
                for g in range(groups):
                    half = start_ref[
                        k, pl.ds(g * cells + t * layers + x, VB, stride=tiles * layers), :
                    ].astype(jnp.bfloat16)
                    if x < DEGREE:
                        down_ref[x, g, k, :, cols(t)] = half
                    if x >= layers - DEGREE:
                        up_ref[x - layers + DEGREE, g, k, :, cols(t)] = half


def run_pack(start2, links2, layers, tiles):
    comps, rows, _ = start2.shape
    planes = tiles * LANES
    groups = rows // (VB * layers * tiles)
    link = jax.ShapeDtypeStruct((DEGREE, LINK_ROWS, planes), jnp.bfloat16)
    halo = jax.ShapeDtypeStruct((DEGREE, groups, comps, VB, planes), jnp.bfloat16)
    return pl.pallas_call(
        functools.partial(pack_kernel, layers=layers, tiles=tiles),
        in_specs=[pl.BlockSpec(memory_space=pltpu.HBM)] * 2,
        out_specs=in_vmem(4),
        out_shape=[link, link, halo, halo],
        scratch_shapes=fetch_scratch(start2, links2),
        compiler_params=params(VMEM_LIMIT),
        cost_estimate=cost(2.5),
        name="pack",
    )(start2, links2)


def mat_mul(a, b, conj_b=False):
    out_re, out_im = [], []
    for i in range(3):
        for j in range(3):
            re = im = None
            for k in range(3):
                ar, ai = a[0][3 * i + k], a[1][3 * i + k]
                if conj_b:
                    br, bi = b[0][3 * j + k], b[1][3 * j + k]
                    r = ar * br + ai * bi
                    m = ai * br - ar * bi
                else:
                    br, bi = b[0][3 * k + j], b[1][3 * k + j]
                    r = ar * br - ai * bi
                    m = ar * bi + ai * br
                re = r if re is None else re + r
                im = m if im is None else im + m
            out_re.append(re)
            out_im.append(im)
    return out_re, out_im


def rot(v, steps):
    return pltpu.roll(v, steps % LANES, 1)


def shifts(value, masks):
    z_last, z_first, y_low, y_high = masks
    tiles = len(value)
    up = [rot(v, LZ) for v in value]
    down = [rot(v, -LZ) for v in value]
    return (
        [jnp.where(y_low, down[t], down[(t + 1) % tiles]) for t in range(tiles)],
        [jnp.where(y_high, up[t], up[(t - 1) % tiles]) for t in range(tiles)],
        [rot(jnp.where(z_first, up[t], value[t]), -1) for t in range(tiles)],
        [rot(jnp.where(z_last, down[t], value[t]), 1) for t in range(tiles)],
    )


def lane_masks(rows):
    lane = lax.broadcasted_iota(jnp.int32, (rows, LANES), 1)
    return lane % LZ == LZ - 1, lane % LZ == 0, lane < LANES - LZ, lane >= LZ


def cols(t):
    return slice(t * LANES, (t + 1) * LANES)


def rows_at(ref, t, first):
    return (
        [ref[t, pl.ds(first + k, 1), :] for k in range(9)],
        [ref[t, pl.ds(first + 9 + k, 1), :] for k in range(9)],
    )


def put_rows(ref, t, first, g):
    for k in range(9):
        ref[t, pl.ds(first + k, 1), :] = g[0][k]
        ref[t, pl.ds(first + 9 + k, 1), :] = g[1][k]


def unit_rows():
    one = jnp.ones((1, LANES), jnp.float32)
    zero = jnp.zeros((1, LANES), jnp.float32)
    return [one if k % 4 == 0 else zero for k in range(9)], [zero] * 9


def fill_tables(ext_ref, g_ref, t_ref, table_ref, gauge_ref, places):
    tiles = ext_ref.shape[0]
    total = len(places)
    masks = lane_masks(total)

    def column(ref, k, stride):
        return [ref[t, pl.ds(k, total, stride=stride), :] for t in range(tiles)]

    gauge = [column(g_ref, k, GAUGE_ROWS) for k in range(18)]
    for d in (1, 2):
        link = [column(ext_ref, 18 * d + k, LINK_PAD) for k in range(18)]
        ahead = [shifts(v, masks)[2 * (d - 1)] for v in gauge]
        turned = []
        for t in range(tiles):
            here, there, mid = (
                ([v[t] for v in field[:9]], [v[t] for v in field[9:]])
                for field in (gauge, ahead, link)
            )
            turned.append(mat_mul(mat_mul(here, mid), there, conj_b=True))
        base = 54 * (d - 1)
        for k in range(9):
            re, im = [turned[t][0][k] for t in range(tiles)], [turned[t][1][k] for t in range(tiles)]
            back_re, back_im = shifts(re, masks)[2 * d - 1], shifts(im, masks)[2 * d - 1]
            for t in range(tiles):
                for at, value in (
                    (0, re[t]),
                    (9, re[t] + im[t]),
                    (18, im[t] - re[t]),
                    (27, back_re[t]),
                    (36, back_re[t] + back_im[t]),
                    (45, back_im[t] - back_re[t]),
                ):
                    t_ref[t, pl.ds(base + at + k, total, stride=TABLE_ROWS), :] = value
    for n, x in enumerate(places):
        for t in range(tiles):
            table_ref[x, 0:108, cols(t)] = t_ref[t, pl.ds(n * TABLE_ROWS, 108), :]
            gauge_ref[x, 0:18, cols(t)] = g_ref[t, pl.ds(n * GAUGE_ROWS, 18), :]


def gauge_own(links_ref, table_ref, gauge_ref, ext_ref, g_ref, t_ref, layers):
    tiles = ext_ref.shape[0]
    for t in range(tiles):
        for x in range(layers):
            ext_ref[t, pl.ds(x * LINK_PAD, LINK_ROWS), :] = links_ref[
                pl.ds(t * layers + x, LINK_ROWS, stride=tiles * layers), :
            ]
    for t in range(tiles):
        g = unit_rows()
        put_rows(g_ref, t, 0, g)
        for x in range(layers - 1):
            g = mat_mul(g, rows_at(ext_ref, t, x * LINK_PAD))
            put_rows(g_ref, t, (x + 1) * GAUGE_ROWS, g)
    fill_tables(
        ext_ref, g_ref, t_ref, table_ref, gauge_ref, [DEGREE + x for x in range(layers)]
    )


def gauge_halo_kernel(
    top_ref, lo_ref, hi_ref, table_in, gauge_in, table_ref, gauge_ref, ext_ref, g_ref, t_ref
):
    layers = table_ref.shape[0] - 2 * DEGREE
    for x in range(DEGREE, DEGREE + layers):
        table_ref[x] = table_in[x]
        gauge_ref[x] = gauge_in[x]
    tiles = ext_ref.shape[0]
    for t in range(tiles):
        for x in range(DEGREE):
            ext_ref[t, pl.ds(x * LINK_PAD, LINK_ROWS), :] = lo_ref[x, :, cols(t)].astype(jnp.float32)
            ext_ref[t, pl.ds((DEGREE + x) * LINK_PAD, LINK_ROWS), :] = hi_ref[x, :, cols(t)].astype(
                jnp.float32
            )
    for t in range(tiles):
        g = unit_rows()
        for x in range(DEGREE - 1, -1, -1):
            g = mat_mul(g, rows_at(ext_ref, t, x * LINK_PAD), conj_b=True)
            put_rows(g_ref, t, x * GAUGE_ROWS, g)
        top = DEGREE + layers - 1
        g = tuple(
            [gauge_in[top, pl.ds(first + k, 1), cols(t)] for k in range(9)] for first in (0, 9)
        )
        link = tuple(
            [top_ref[pl.ds(first + k, 1), cols(t)] for k in range(9)]
            for first in (0, 9)
        )
        for x in range(DEGREE):
            g = mat_mul(g, link)
            put_rows(g_ref, t, (DEGREE + x) * GAUGE_ROWS, g)
            if x < DEGREE - 1:
                link = rows_at(ext_ref, t, (DEGREE + x) * LINK_PAD)
    places = list(range(DEGREE)) + [DEGREE + layers + x for x in range(DEGREE)]
    fill_tables(ext_ref, g_ref, t_ref, table_ref, gauge_ref, places)


def gauge_scratch(count, tiles):
    return [
        pltpu.VMEM((tiles, count * LINK_PAD, LANES), jnp.float32),
        pltpu.VMEM((tiles, count * GAUGE_ROWS, LANES), jnp.float32),
        pltpu.VMEM((tiles, count * TABLE_ROWS, LANES), jnp.float32),
    ]


def gauge_shapes(layers, planes):
    total = layers + 2 * DEGREE
    return [
        jax.ShapeDtypeStruct((total, TABLE_ROWS, planes), jnp.float32),
        jax.ShapeDtypeStruct((total, GAUGE_ROWS, planes), jnp.float32),
    ]


def gauge_halo(top, lo, hi, table, gauge):
    total, _, planes = table.shape
    return pl.pallas_call(
        gauge_halo_kernel,
        in_specs=in_vmem(5),
        out_specs=in_vmem(2),
        out_shape=gauge_shapes(total - 2 * DEGREE, planes),
        scratch_shapes=gauge_scratch(2 * DEGREE, planes // LANES),
        compiler_params=params(),
        cost_estimate=cost(1.5),
        name="gauge_halo",
    )(top, lo, hi, table, gauge)


def turn(gauge_ref, x, source, adjoint, tiles):
    out = {}
    for t in range(tiles):
        v = [source(k, t) for k in range(6)]
        for i in range(3):
            re = im = None
            for j in range(3):
                k = 3 * j + i if adjoint else 3 * i + j
                a = gauge_ref[x, pl.ds(k, 1), cols(t)]
                b = gauge_ref[x, pl.ds(9 + k, 1), cols(t)]
                if adjoint:
                    r, m = a * v[j] + b * v[3 + j], a * v[3 + j] - b * v[j]
                else:
                    r, m = a * v[j] - b * v[3 + j], a * v[3 + j] + b * v[j]
                re = r if re is None else re + r
                im = m if im is None else im + m
            out[i, t], out[3 + i, t] = re, im
    return out


def layer(table_ref, g, x, src, prev, first, tiles):
    z_last, z_first, y_low, y_high = lane_masks(VB)
    sums = {}

    def add(key, value, minus=False):
        have = sums.get(key)
        if have is None:
            sums[key] = -value if minus else value
        else:
            sums[key] = have - value if minus else have + value

    def hop(t, base, v, adjoint):
        both = [v[j] + v[3 + j] for j in range(3)]
        for j in range(3):
            for i in range(3):
                k = base + (3 * j + i if adjoint else 3 * i + j)
                a = table_ref[x, pl.ds(k, 1), cols(t)]
                p = table_ref[x, pl.ds(k + 9, 1), cols(t)]
                q = table_ref[x, pl.ds(k + 18, 1), cols(t)]
                add((t, 0, i), a * both[j])
                if adjoint:
                    add((t, 1, i), q * v[3 + j], True)
                    add((t, 2, i), p * v[j], True)
                else:
                    add((t, 1, i), p * v[3 + j])
                    add((t, 2, i), q * v[j])

    out = {}
    for t in range(tiles):
        c = {(k, u): src[g, x, k, :, cols(u)] for k in range(6) for u in range(tiles)}
        after, before = (t + 1) % tiles, (t - 1) % tiles
        hop(t, 0, [rot(jnp.where(y_high, c[k, t], c[k, after]), -LZ) for k in range(6)], False)
        hop(t, 27, [rot(jnp.where(y_low, c[k, t], c[k, before]), LZ) for k in range(6)], True)
        hop(
            t, 54,
            [jnp.where(z_last, rot(c[k, t], LZ - 1), rot(c[k, t], -1)) for k in range(6)],
            False,
        )
        hop(
            t, 81,
            [jnp.where(z_first, rot(c[k, t], 1 - LZ), rot(c[k, t], 1)) for k in range(6)],
            True,
        )
        for i in range(3):
            re = sums[t, 0, i] - sums[t, 1, i]
            im = sums[t, 0, i] + sums[t, 2, i]
            for k, h in ((i, re), (3 + i, im)):
                h = h + (src[g, x + 1, k, :, cols(t)] + src[g, x - 1, k, :, cols(t)])
                if first:
                    out[k, t] = (6.0 * SCALE - OFFSET) * c[k, t] - SCALE * h
                else:
                    out[k, t] = (
                        (12.0 * SCALE - 2.0 * OFFSET) * c[k, t]
                        - (2.0 * SCALE) * h
                        - prev[g, x, k, :, cols(t)]
                    )
    return out


def put(ref, g, x, values):
    for (k, t), value in values.items():
        ref[g, x, k, :, cols(t)] = value


def inner_kernel(
    start_hbm, links_hbm, a_ref, b_ref, table_ref, gauge_ref, top_ref,
    start_ref, links_ref, sems, ext_ref, g_ref, t_ref, *, layers
):
    groups = a_ref.shape[0]
    tiles = table_ref.shape[-1] // LANES
    cells = VB * layers * tiles
    copies = fetch(start_hbm, links_hbm, start_ref, links_ref, sems)
    copies[0].wait()
    gauge_own(links_ref, table_ref, gauge_ref, ext_ref, g_ref, t_ref, layers)
    for t in range(tiles):
        top_ref[0:18, cols(t)] = ext_ref[t, pl.ds((layers - 1) * LINK_PAD, 18), :]
    for copy in copies[1:]:
        copy.wait()

    def init(n, _):
        g, x = n // layers, n % layers

        def source(k, t):
            at = g * cells + t * layers + x
            return start_ref[k, pl.ds(at, VB, stride=tiles * layers), :]

        put(a_ref, g, x + DEGREE, turn(gauge_ref, x + DEGREE, source, False, tiles))
        return 0

    lax.fori_loop(0, groups * layers, init, 0)
    for level in range(1, DEGREE):
        src, dst = (a_ref, b_ref) if level % 2 else (b_ref, a_ref)
        pairs = (layers - 2 * level) // 2

        def body(n, _, src=src, dst=dst, level=level, pairs=pairs):
            g, at = n // pairs, n % pairs
            for u in range(2):
                x = DEGREE + level + 2 * at + u
                put(dst, g, x, layer(table_ref, g, x, src, dst, level == 1, tiles))
            return 0

        if pairs > 0:
            lax.fori_loop(0, groups * pairs, body, 0)


def run_inner(start2, links2, layers, tiles):
    comps, rows, _ = start2.shape
    planes = tiles * LANES
    groups = rows // (VB * layers * tiles)
    state = jax.ShapeDtypeStruct((groups, layers + 2 * DEGREE, comps, VB, planes), jnp.float32)
    top = jax.ShapeDtypeStruct((GAUGE_ROWS, planes), jnp.float32)
    return pl.pallas_call(
        functools.partial(inner_kernel, layers=layers),
        in_specs=[pl.BlockSpec(memory_space=pltpu.HBM)] * 2,
        out_specs=in_vmem(5),
        out_shape=[state, state] + gauge_shapes(layers, planes) + [top],
        scratch_shapes=fetch_scratch(start2, links2) + gauge_scratch(layers, tiles),
        compiler_params=params(),
        cost_estimate=cost(8),
        name="inner",
    )(start2, links2)


def outer_kernel(
    place_ref, lo_ref, hi_ref, table_ref, gauge_ref, a_in, b_in,
    half_ref, keep_ref, give_ref, a_ref, b_ref, pack_ref, *, layers, parts
):
    groups = a_ref.shape[0]
    total = layers + 2 * DEGREE
    planes = table_ref.shape[-1]
    tiles = planes // LANES

    def init(n, _):
        g, x = n // DEGREE, n % DEGREE
        for ref, at in ((lo_ref, x), (hi_ref, x + DEGREE + layers)):

            def source(k, t, ref=ref):
                return ref[x, g, k, :, cols(t)].astype(jnp.float32)

            put(a_ref, g, at, turn(gauge_ref, at, source, False, tiles))
        for at in (x + DEGREE, total - 2 * DEGREE + x):
            a_ref[g, at] = a_in[g, at]
            b_ref[g, at] = b_in[g, at]
        return 0

    lax.fori_loop(0, groups * DEGREE, init, 0)
    for level in range(1, DEGREE):
        src, dst = (a_ref, b_ref) if level % 2 else (b_ref, a_ref)

        def body(n, _, src=src, dst=dst, level=level):
            steps = DEGREE // 2
            g, at = n // steps, 2 * (n % steps)
            for first in (level + at, total - DEGREE - level + at):
                for x in (first, first + 1):
                    put(dst, g, x, layer(table_ref, g, x, src, dst, level == 1, tiles))
            return 0

        lax.fori_loop(0, groups * (DEGREE // 2), body, 0)
    src, prev = (a_ref, b_ref) if DEGREE % 2 else (b_ref, a_ref)

    def last(n, _):
        g, at = n // (layers // 4), n % (layers // 4)
        for u in range(4):
            x = 4 * at + u
            value = layer(table_ref, g, x + DEGREE, src, prev, False, tiles)
            value = turn(gauge_ref, x + DEGREE, lambda k, t: value[k, t], True, tiles)
            for (k, t), v in value.items():
                rounded = v.astype(jnp.bfloat16)
                half_ref[g, x, k, :, cols(t)] = rounded
                pack_ref[g, k, pl.ds(pl.multiple_of(x * VB, VB), VB), cols(t)] = rounded.astype(
                    jnp.float32
                )
        return 0

    lax.fori_loop(0, groups * (layers // 4), last, 0)

    side, base = place_ref[0], place_ref[1]
    pairs = parts // 2
    width = planes // parts
    for g in range(groups):
        for k in range(6):
            turned = jnp.concatenate([pack_ref[g, k, :, cols(t)].T for t in range(tiles)], axis=0)
            for m in range(pairs):
                near = turned[m * width : (m + 1) * width].astype(jnp.bfloat16)
                far = turned[(pairs + m) * width : (pairs + m + 1) * width].astype(jnp.bfloat16)
                keep_ref[base ^ m, g, k] = jnp.where(side == 0, near, far)
                give_ref[base ^ m, g, k] = jnp.where(side == 0, far, near)


def run_outer(place, lo, hi, table, gauge, a, b, layers, parts):
    groups, total, comps, _, planes = a.shape
    width = planes // parts
    cells = layers * VB
    block = jax.ShapeDtypeStruct((parts // 2, groups, comps, width, cells), jnp.bfloat16)
    half = jax.ShapeDtypeStruct((groups, layers, comps, VB, planes), jnp.bfloat16)
    return pl.pallas_call(
        functools.partial(outer_kernel, layers=layers, parts=parts),
        in_specs=[in_smem()] + in_vmem(6),
        out_specs=in_vmem(3),
        out_shape=[half, block, block],
        scratch_shapes=[
            pltpu.VMEM(a.shape, jnp.float32),
            pltpu.VMEM(a.shape, jnp.float32),
            pltpu.VMEM((groups, comps, cells, planes), jnp.float32),
        ],
        compiler_params=params(),
        cost_estimate=cost(16),
        name="outer",
    )(place, lo, hi, table, gauge, a, b)


def weight_kernel(half_ref, weight_ref):
    groups, layers, _, _, planes = half_ref.shape
    vectors = groups * VB
    for g in range(groups):
        for x in range(layers):
            for part in range(2):
                for c in range(3):
                    for p in range(2):
                        value = half_ref[g, x, (part ^ p) * 3 + c]
                        if p == 1 and part == 1:
                            value = -value
                        weight_ref[
                            pl.ds((x * 2 + p) * vectors + g * VB, VB),
                            pl.ds((part * 3 + c) * planes, planes),
                        ] = value


def run_weights(half):
    groups, layers, comps, _, planes = half.shape
    return pl.pallas_call(
        weight_kernel,
        in_specs=in_vmem(1),
        out_specs=in_vmem(1)[0],
        out_shape=jax.ShapeDtypeStruct((layers * 2 * groups * VB, comps * planes), jnp.bfloat16),
        compiler_params=params(),
        cost_estimate=cost(0.7),
        name="weights",
    )(half)


def corr_kernel(place_ref, stored_ref, weight_ref, out_ref, *, layers):
    span, block = out_ref.shape
    _, comps, _, planes = stored_ref.shape
    rows = jnp.concatenate(
        [stored_ref[:, k].reshape(block * layers, planes) for k in range(comps)], axis=1
    )
    layer_of_row = lax.broadcasted_iota(jnp.int32, (block * layers, LANES), 0) % layers
    layer_of_lane = lax.broadcasted_iota(jnp.int32, (block * layers, LANES), 1) // span
    kept = jnp.zeros((block * layers, LANES), jnp.float32)
    width = min(2 * LANES, weight_ref.shape[0])
    for first in range(0, weight_ref.shape[0], width):
        full = lax.dot_general(
            rows,
            weight_ref[first : first + width, :],
            (((1,), (1,)), ((), ())),
            preferred_element_type=jnp.float32,
        )
        for at in range(0, width, LANES):
            here = layer_of_row == (first + at) // span + layer_of_lane
            kept = jnp.where(here, full[:, at : at + LANES], kept)
    summed = jnp.sum(kept.reshape(block, layers, LANES), axis=1)
    total = summed[:, :span]
    for at in range(span, LANES, span):
        total = total + summed[:, at : at + span]
    out_ref[...] = total.T


def run_corr(place, stored, weights, owners):
    count, comps, layers, planes = stored.shape
    block = count // owners
    span = weights.shape[0] // layers
    grid_spec = pltpu.PrefetchScalarGridSpec(
        num_scalar_prefetch=1,
        grid=(owners,),
        in_specs=[
            pl.BlockSpec((block, comps, layers, planes), lambda g, s: (g, 0, 0, 0)),
            pl.BlockSpec(memory_space=pltpu.VMEM),
        ],
        out_specs=pl.BlockSpec((pl.Squeezed(), span, block), lambda g, s: (g ^ s[2], 0, 0)),
    )
    return pl.pallas_call(
        functools.partial(corr_kernel, layers=layers),
        grid_spec=grid_spec,
        out_shape=jax.ShapeDtypeStruct((owners, span, block), jnp.float32),
        compiler_params=params(40 * 2**20),
        cost_estimate=cost(8),
        name="correlate",
    )(place, stored, weights)


def merge_kernel(keep_ref, got_ref, *out_refs):
    for step, ref in enumerate(out_refs):
        ref[0] = keep_ref[step]
        ref[1] = got_ref[step]


def run_merge(keep, got):
    shape = jax.ShapeDtypeStruct((2,) + keep.shape[1:], keep.dtype)
    return pl.pallas_call(
        merge_kernel,
        in_specs=in_vmem(2),
        out_specs=in_vmem(keep.shape[0]),
        out_shape=[shape] * keep.shape[0],
        compiler_params=params(),
        cost_estimate=cost(0.7),
        name="merge",
    )(keep, got)


def order_kernel(order_ref, *, layers, groups):
    depth = order_ref.shape[0]
    cells = layers * VB
    vectors = groups * VB
    row = lax.broadcasted_iota(jnp.int32, (depth, depth), 0)
    col = lax.broadcasted_iota(jnp.int32, (depth, depth), 1)
    bit, rest = row // (groups * cells), row % (groups * cells)
    group, cell = rest // cells, rest % cells
    wanted = ((cell // VB) * 2 + bit) * vectors + group * VB + cell % VB
    order_ref[...] = (wanted == col).astype(jnp.bfloat16)


def run_order(groups, layers):
    depth = 2 * groups * layers * VB
    return pl.pallas_call(
        functools.partial(order_kernel, layers=layers, groups=groups),
        out_specs=in_vmem(1)[0],
        out_shape=jax.ShapeDtypeStruct((depth, depth), jnp.bfloat16),
        compiler_params=params(),
        cost_estimate=cost(2),
        name="order",
    )()


def arrange_kernel(place_ref, order_ref, *refs, layers, per):
    out_ref = refs[-1]
    groups, comps, width = refs[0].shape[1:4]
    span = 2 * groups * VB
    pieces = []
    for ref in refs[:-1]:
        for h in range(2):
            for pair in range(comps // 2):
                lanes = [ref[h, g, 2 * pair + bit] for bit in range(2) for g in range(groups)]
                pieces.append(jnp.concatenate(lanes, axis=1))
    moved = jnp.dot(
        jnp.concatenate(pieces, axis=0), order_ref[...], preferred_element_type=jnp.float32
    )
    for step in range(len(refs) - 1):
        source = place_ref[3] ^ step
        slice_at, chip = lax.rem(source, per), source // per
        for h in range(2):
            first = (2 * chip + (place_ref[4] ^ h)) * layers
            at = (2 * step + h) * (comps // 2) * width
            for x in range(layers):
                out_ref[slice_at, first + x] = jnp.concatenate(
                    [
                        moved[at + p * width : at + (p + 1) * width, x * span : (x + 1) * span]
                        for p in range(comps // 2)
                    ],
                    axis=1,
                ).astype(jnp.bfloat16)


def run_arrange(place, order, blocks, shape, layers, per):
    return pl.pallas_call(
        functools.partial(arrange_kernel, layers=layers, per=per),
        in_specs=[in_smem()] + in_vmem(1 + len(blocks)),
        out_specs=in_vmem(1)[0],
        out_shape=jax.ShapeDtypeStruct(shape, jnp.bfloat16),
        compiler_params=params(),
        cost_estimate=cost(3),
        name="arrange",
    )(place, order, *blocks)


def shards(start_block, gauge_links, stored_vectors, *, n_tm, n_space):
    _, parts, colours, vectors, layers, planes = start_block.shape
    comps = parts * colours
    tm, space = lax.axis_index("tm"), lax.axis_index("space")
    per = n_tm // n_space
    pairs = n_tm // 2
    groups = vectors // VB

    def base_of(i, j):
        return (j // 2 * per + i % per) ^ (i // per % 2 * per)

    place = jnp.stack(
        [
            space % 2 ^ tm // pairs,
            base_of(tm, space),
            space,
            tm % pairs ^ space % 2 * per,
            tm // pairs ^ space * per // pairs,
        ]
    ).astype(jnp.int32)

    tiles = planes // LANES

    def by_tile(value, *lead):
        value = value.reshape(-1, layers, tiles, LANES)
        return jnp.transpose(value, (0, 2, 1, 3)).reshape(*lead, LANES)

    start2 = by_tile(start_block, comps, vectors * tiles * layers)
    links2 = by_tile(gauge_links, LINK_ROWS * tiles * layers)
    up = [(i, (i + 1) % n_space) for i in range(n_space)]
    down = [((i + 1) % n_space, i) for i in range(n_space)]

    up_links, down_links, up_halo, down_halo = run_pack(start2, links2, layers, tiles)
    lo_links = lax.ppermute(up_links, "space", up)
    hi_links = lax.ppermute(down_links, "space", down)
    lo = lax.ppermute(up_halo, "space", up)
    hi = lax.ppermute(down_halo, "space", down)
    order = run_order(groups, layers)

    a, b, table, gauge, top = run_inner(start2, links2, layers, tiles)
    table, gauge = gauge_halo(top, lo_links, hi_links, table, gauge)
    half, keep, give = run_outer(place, lo, hi, table, gauge, a, b, layers, n_tm)

    weights = run_weights(half)
    got = lax.ppermute(give, "space", [(i, i ^ 1) for i in range(n_space)])
    blocks = run_merge(keep, got)
    stored = stored_vectors.reshape(stored_vectors.shape[1], comps, layers, planes)
    sent = [None] * pairs
    digits = pairs.bit_length() - 1
    for step in sorted(range(pairs), key=lambda n: f"{n:0{digits}b}"[::-1]):
        table_of = []
        for i in range(n_tm):
            for j in range(n_space):
                to = (j % 2 ^ i // pairs) * pairs + (base_of(i, j) ^ step)
                table_of.append((i * n_space + j, to * n_space + i // per))
        sent[step] = lax.ppermute(blocks[step], ("tm", "space"), table_of)
    partial = run_corr(place, stored, weights, n_space)
    partial, *sent[:-1] = lax.optimization_barrier((partial, *sent[:-1]))
    total = partial[0]
    for distance in range(1, n_space):
        partner = [(i, i ^ distance) for i in range(n_space)]
        total = total + lax.ppermute(partial[distance], "space", partner)
    correlations = total.T[None]

    shape = (per, n_space * layers, planes // n_tm, comps * vectors)
    return correlations, run_arrange(place, order, sent, shape, layers, per)


def solution(mesh):
    in_specs = (
        P("tm", None, None, None, "space", None),
        P("tm", None, None, None, None, "space", None),
        P("tm", None, None, None, "space", None),
    )
    out_specs = (P("tm", "space", None), P("space", None, "tm", None))
    body = functools.partial(shards, n_tm=mesh.shape["tm"], n_space=mesh.shape["space"])
    return jax.shard_map(body, mesh=mesh, in_specs=in_specs, out_specs=out_specs, check_vma=False)
```

```python
import functools

import jax
import jax.numpy as jnp
from jax import lax
from jax.experimental import pallas as pl
from jax.experimental.pallas import tpu as pltpu
from jax.sharding import PartitionSpec as P

DEGREE = 4
LZ = 16
LANES = 128
VB = 16

lower_edge = 0.5
upper_edge = 12.5
SCALE = 2.0 / (upper_edge - lower_edge)
OFFSET = (upper_edge + lower_edge) / (upper_edge - lower_edge)

VMEM_LIMIT = 60 * 2**20
LINK_ROWS = 54
LINK_PAD = 56
TABLE_ROWS = 112
GAUGE_ROWS = 24


def params(limit=24 * 2**20):
    return pltpu.CompilerParams(vmem_limit_bytes=limit)


def in_vmem(count):
    return [pl.BlockSpec(memory_space=pltpu.VMEM)] * count


def in_smem():
    return pl.BlockSpec(memory_space=pltpu.SMEM)


def cost(microseconds):
    return pl.CostEstimate(
        flops=1_000_000, bytes_accessed=int(microseconds * 3_000_000), transcendentals=0
    )


def fetch(start_hbm, links_hbm, start_ref, links_ref, sems):
    comps = start_ref.shape[0]
    copies = [pltpu.make_async_copy(links_hbm, links_ref, sems.at[comps])] + [
        pltpu.make_async_copy(start_hbm.at[k], start_ref.at[k], sems.at[k]) for k in range(comps)
    ]
    for copy in copies:
        copy.start()
    return copies


def fetch_scratch(start2, links2):
    return [
        pltpu.VMEM(start2.shape, jnp.float32),
        pltpu.VMEM(links2.shape, jnp.float32),
        pltpu.SemaphoreType.DMA((start2.shape[0] + 1,)),
    ]


def pack_kernel(
    start_hbm, links_hbm, up_links_ref, down_links_ref, up_ref, down_ref,
    start_ref, links_ref, sems, *, layers, tiles
):
    comps, groups = up_ref.shape[2], up_ref.shape[1]
    cells = VB * layers * tiles
    copies = fetch(start_hbm, links_hbm, start_ref, links_ref, sems)
    copies[0].wait()
    for x in range(layers):
        for t in range(tiles):
            rows = links_ref[pl.ds(t * layers + x, LINK_ROWS, stride=tiles * layers), :]
            if x < DEGREE:
                down_links_ref[x, :, cols(t)] = rows.astype(jnp.bfloat16)
            if x >= layers - DEGREE:
                up_links_ref[x - layers + DEGREE, :, cols(t)] = rows.astype(jnp.bfloat16)
    for k in range(comps):
        copies[1 + k].wait()
        for x in range(layers):
            for t in range(tiles):
                for g in range(groups):
                    half = start_ref[
                        k, pl.ds(g * cells + t * layers + x, VB, stride=tiles * layers), :
                    ].astype(jnp.bfloat16)
                    if x < DEGREE:
                        down_ref[x, g, k, :, cols(t)] = half
                    if x >= layers - DEGREE:
                        up_ref[x - layers + DEGREE, g, k, :, cols(t)] = half


def run_pack(start2, links2, layers, tiles):
    comps, rows, _ = start2.shape
    planes = tiles * LANES
    groups = rows // (VB * layers * tiles)
    link = jax.ShapeDtypeStruct((DEGREE, LINK_ROWS, planes), jnp.bfloat16)
    halo = jax.ShapeDtypeStruct((DEGREE, groups, comps, VB, planes), jnp.bfloat16)
    return pl.pallas_call(
        functools.partial(pack_kernel, layers=layers, tiles=tiles),
        in_specs=[pl.BlockSpec(memory_space=pltpu.HBM)] * 2,
        out_specs=in_vmem(4),
        out_shape=[link, link, halo, halo],
        scratch_shapes=fetch_scratch(start2, links2),
        compiler_params=params(VMEM_LIMIT),
        cost_estimate=cost(2.5),
        name="pack",
    )(start2, links2)


def mat_mul(a, b, conj_b=False):
    out_re, out_im = [], []
    for i in range(3):
        for j in range(3):
            re = im = None
            for k in range(3):
                ar, ai = a[0][3 * i + k], a[1][3 * i + k]
                if conj_b:
                    br, bi = b[0][3 * j + k], b[1][3 * j + k]
                    r = ar * br + ai * bi
                    m = ai * br - ar * bi
                else:
                    br, bi = b[0][3 * k + j], b[1][3 * k + j]
                    r = ar * br - ai * bi
                    m = ar * bi + ai * br
                re = r if re is None else re + r
                im = m if im is None else im + m
            out_re.append(re)
            out_im.append(im)
    return out_re, out_im


def rot(v, steps):
    return pltpu.roll(v, steps % LANES, 1)


def shifts(value, masks):
    z_last, z_first, y_low, y_high = masks
    tiles = len(value)
    up = [rot(v, LZ) for v in value]
    down = [rot(v, -LZ) for v in value]
    return (
        [jnp.where(y_low, down[t], down[(t + 1) % tiles]) for t in range(tiles)],
        [jnp.where(y_high, up[t], up[(t - 1) % tiles]) for t in range(tiles)],
        [rot(jnp.where(z_first, up[t], value[t]), -1) for t in range(tiles)],
        [rot(jnp.where(z_last, down[t], value[t]), 1) for t in range(tiles)],
    )


def lane_masks(rows):
    lane = lax.broadcasted_iota(jnp.int32, (rows, LANES), 1)
    return lane % LZ == LZ - 1, lane % LZ == 0, lane < LANES - LZ, lane >= LZ


def cols(t):
    return slice(t * LANES, (t + 1) * LANES)


def rows_at(ref, t, first):
    return (
        [ref[t, pl.ds(first + k, 1), :] for k in range(9)],
        [ref[t, pl.ds(first + 9 + k, 1), :] for k in range(9)],
    )


def put_rows(ref, t, first, g):
    for k in range(9):
        ref[t, pl.ds(first + k, 1), :] = g[0][k]
        ref[t, pl.ds(first + 9 + k, 1), :] = g[1][k]


def unit_rows():
    one = jnp.ones((1, LANES), jnp.float32)
    zero = jnp.zeros((1, LANES), jnp.float32)
    return [one if k % 4 == 0 else zero for k in range(9)], [zero] * 9


def fill_tables(ext_ref, g_ref, t_ref, table_ref, gauge_ref, places):
    tiles = ext_ref.shape[0]
    total = len(places)
    masks = lane_masks(total)

    def column(ref, k, stride):
        return [ref[t, pl.ds(k, total, stride=stride), :] for t in range(tiles)]

    gauge = [column(g_ref, k, GAUGE_ROWS) for k in range(18)]
    for d in (1, 2):
        link = [column(ext_ref, 18 * d + k, LINK_PAD) for k in range(18)]
        ahead = [shifts(v, masks)[2 * (d - 1)] for v in gauge]
        turned = []
        for t in range(tiles):
            here, there, mid = (
                ([v[t] for v in field[:9]], [v[t] for v in field[9:]])
                for field in (gauge, ahead, link)
            )
            turned.append(mat_mul(mat_mul(here, mid), there, conj_b=True))
        base = 54 * (d - 1)
        for k in range(9):
            re, im = [turned[t][0][k] for t in range(tiles)], [turned[t][1][k] for t in range(tiles)]
            back_re, back_im = shifts(re, masks)[2 * d - 1], shifts(im, masks)[2 * d - 1]
            for t in range(tiles):
                for at, value in (
                    (0, re[t]),
                    (9, re[t] + im[t]),
                    (18, im[t] - re[t]),
                    (27, back_re[t]),
                    (36, back_re[t] + back_im[t]),
                    (45, back_im[t] - back_re[t]),
                ):
                    t_ref[t, pl.ds(base + at + k, total, stride=TABLE_ROWS), :] = value
    for n, x in enumerate(places):
        for t in range(tiles):
            table_ref[x, 0:108, cols(t)] = t_ref[t, pl.ds(n * TABLE_ROWS, 108), :]
            gauge_ref[x, 0:18, cols(t)] = g_ref[t, pl.ds(n * GAUGE_ROWS, 18), :]


def gauge_own(links_ref, table_ref, gauge_ref, ext_ref, g_ref, t_ref, layers):
    tiles = ext_ref.shape[0]
    for t in range(tiles):
        for x in range(layers):
            ext_ref[t, pl.ds(x * LINK_PAD, LINK_ROWS), :] = links_ref[
                pl.ds(t * layers + x, LINK_ROWS, stride=tiles * layers), :
            ]
    for t in range(tiles):
        g = unit_rows()
        put_rows(g_ref, t, 0, g)
        for x in range(layers - 1):
            g = mat_mul(g, rows_at(ext_ref, t, x * LINK_PAD))
            put_rows(g_ref, t, (x + 1) * GAUGE_ROWS, g)
    fill_tables(
        ext_ref, g_ref, t_ref, table_ref, gauge_ref, [DEGREE + x for x in range(layers)]
    )


def gauge_halo_kernel(
    top_ref, lo_ref, hi_ref, table_in, gauge_in, table_ref, gauge_ref, ext_ref, g_ref, t_ref
):
    layers = table_ref.shape[0] - 2 * DEGREE
    for x in range(DEGREE, DEGREE + layers):
        table_ref[x] = table_in[x]
        gauge_ref[x] = gauge_in[x]
    tiles = ext_ref.shape[0]
    for t in range(tiles):
        for x in range(DEGREE):
            ext_ref[t, pl.ds(x * LINK_PAD, LINK_ROWS), :] = lo_ref[x, :, cols(t)].astype(jnp.float32)
            ext_ref[t, pl.ds((DEGREE + x) * LINK_PAD, LINK_ROWS), :] = hi_ref[x, :, cols(t)].astype(
                jnp.float32
            )
    for t in range(tiles):
        g = unit_rows()
        for x in range(DEGREE - 1, -1, -1):
            g = mat_mul(g, rows_at(ext_ref, t, x * LINK_PAD), conj_b=True)
            put_rows(g_ref, t, x * GAUGE_ROWS, g)
        top = DEGREE + layers - 1
        g = tuple(
            [gauge_in[top, pl.ds(first + k, 1), cols(t)] for k in range(9)] for first in (0, 9)
        )
        link = tuple(
            [top_ref[pl.ds(first + k, 1), cols(t)] for k in range(9)]
            for first in (0, 9)
        )
        for x in range(DEGREE):
            g = mat_mul(g, link)
            put_rows(g_ref, t, (DEGREE + x) * GAUGE_ROWS, g)
            if x < DEGREE - 1:
                link = rows_at(ext_ref, t, (DEGREE + x) * LINK_PAD)
    places = list(range(DEGREE)) + [DEGREE + layers + x for x in range(DEGREE)]
    fill_tables(ext_ref, g_ref, t_ref, table_ref, gauge_ref, places)


def gauge_scratch(count, tiles):
    return [
        pltpu.VMEM((tiles, count * LINK_PAD, LANES), jnp.float32),
        pltpu.VMEM((tiles, count * GAUGE_ROWS, LANES), jnp.float32),
        pltpu.VMEM((tiles, count * TABLE_ROWS, LANES), jnp.float32),
    ]


def gauge_shapes(layers, planes):
    total = layers + 2 * DEGREE
    return [
        jax.ShapeDtypeStruct((total, TABLE_ROWS, planes), jnp.float32),
        jax.ShapeDtypeStruct((total, GAUGE_ROWS, planes), jnp.float32),
    ]


def gauge_halo(top, lo, hi, table, gauge):
    total, _, planes = table.shape
    return pl.pallas_call(
        gauge_halo_kernel,
        in_specs=in_vmem(5),
        out_specs=in_vmem(2),
        out_shape=gauge_shapes(total - 2 * DEGREE, planes),
        scratch_shapes=gauge_scratch(2 * DEGREE, planes // LANES),
        compiler_params=params(),
        cost_estimate=cost(1.5),
        name="gauge_halo",
    )(top, lo, hi, table, gauge)


def turn(gauge_ref, x, source, adjoint, tiles):
    out = {}
    for t in range(tiles):
        v = [source(k, t) for k in range(6)]
        for i in range(3):
            re = im = None
            for j in range(3):
                k = 3 * j + i if adjoint else 3 * i + j
                a = gauge_ref[x, pl.ds(k, 1), cols(t)]
                b = gauge_ref[x, pl.ds(9 + k, 1), cols(t)]
                if adjoint:
                    r, m = a * v[j] + b * v[3 + j], a * v[3 + j] - b * v[j]
                else:
                    r, m = a * v[j] - b * v[3 + j], a * v[3 + j] + b * v[j]
                re = r if re is None else re + r
                im = m if im is None else im + m
            out[i, t], out[3 + i, t] = re, im
    return out


def layer(table_ref, g, x, src, prev, first, tiles):
    z_last, z_first, y_low, y_high = lane_masks(VB)
    sums = {}

    def add(key, value, minus=False):
        have = sums.get(key)
        if have is None:
            sums[key] = -value if minus else value
        else:
            sums[key] = have - value if minus else have + value

    def hop(t, base, v, adjoint):
        both = [v[j] + v[3 + j] for j in range(3)]
        for j in range(3):
            for i in range(3):
                k = base + (3 * j + i if adjoint else 3 * i + j)
                a = table_ref[x, pl.ds(k, 1), cols(t)]
                p = table_ref[x, pl.ds(k + 9, 1), cols(t)]
                q = table_ref[x, pl.ds(k + 18, 1), cols(t)]
                add((t, 0, i), a * both[j])
                if adjoint:
                    add((t, 1, i), q * v[3 + j], True)
                    add((t, 2, i), p * v[j], True)
                else:
                    add((t, 1, i), p * v[3 + j])
                    add((t, 2, i), q * v[j])

    out = {}
    for t in range(tiles):
        c = {(k, u): src[g, x, k, :, cols(u)] for k in range(6) for u in range(tiles)}
        after, before = (t + 1) % tiles, (t - 1) % tiles
        hop(t, 0, [rot(jnp.where(y_high, c[k, t], c[k, after]), -LZ) for k in range(6)], False)
        hop(t, 27, [rot(jnp.where(y_low, c[k, t], c[k, before]), LZ) for k in range(6)], True)
        hop(
            t, 54,
            [jnp.where(z_last, rot(c[k, t], LZ - 1), rot(c[k, t], -1)) for k in range(6)],
            False,
        )
        hop(
            t, 81,
            [jnp.where(z_first, rot(c[k, t], 1 - LZ), rot(c[k, t], 1)) for k in range(6)],
            True,
        )
        for i in range(3):
            re = sums[t, 0, i] - sums[t, 1, i]
            im = sums[t, 0, i] + sums[t, 2, i]
            for k, h in ((i, re), (3 + i, im)):
                h = h + (src[g, x + 1, k, :, cols(t)] + src[g, x - 1, k, :, cols(t)])
                if first:
                    out[k, t] = (6.0 * SCALE - OFFSET) * c[k, t] - SCALE * h
                else:
                    out[k, t] = (
                        (12.0 * SCALE - 2.0 * OFFSET) * c[k, t]
                        - (2.0 * SCALE) * h
                        - prev[g, x, k, :, cols(t)]
                    )
    return out


def put(ref, g, x, values):
    for (k, t), value in values.items():
        ref[g, x, k, :, cols(t)] = value


def inner_kernel(
    start_hbm, links_hbm, a_ref, b_ref, table_ref, gauge_ref, top_ref,
    start_ref, links_ref, sems, ext_ref, g_ref, t_ref, *, layers
):
    groups = a_ref.shape[0]
    tiles = table_ref.shape[-1] // LANES
    cells = VB * layers * tiles
    copies = fetch(start_hbm, links_hbm, start_ref, links_ref, sems)
    copies[0].wait()
    gauge_own(links_ref, table_ref, gauge_ref, ext_ref, g_ref, t_ref, layers)
    for t in range(tiles):
        top_ref[0:18, cols(t)] = ext_ref[t, pl.ds((layers - 1) * LINK_PAD, 18), :]
    for copy in copies[1:]:
        copy.wait()

    def init(n, _):
        g, x = n // layers, n % layers

        def source(k, t):
            at = g * cells + t * layers + x
            return start_ref[k, pl.ds(at, VB, stride=tiles * layers), :]

        put(a_ref, g, x + DEGREE, turn(gauge_ref, x + DEGREE, source, False, tiles))
        return 0

    lax.fori_loop(0, groups * layers, init, 0)
    for level in range(1, DEGREE):
        src, dst = (a_ref, b_ref) if level % 2 else (b_ref, a_ref)
        pairs = (layers - 2 * level) // 2

        def body(n, _, src=src, dst=dst, level=level, pairs=pairs):
            g, at = n // pairs, n % pairs
            for u in range(2):
                x = DEGREE + level + 2 * at + u
                put(dst, g, x, layer(table_ref, g, x, src, dst, level == 1, tiles))
            return 0

        if pairs > 0:
            lax.fori_loop(0, groups * pairs, body, 0)


def run_inner(start2, links2, layers, tiles):
    comps, rows, _ = start2.shape
    planes = tiles * LANES
    groups = rows // (VB * layers * tiles)
    state = jax.ShapeDtypeStruct((groups, layers + 2 * DEGREE, comps, VB, planes), jnp.float32)
    top = jax.ShapeDtypeStruct((GAUGE_ROWS, planes), jnp.float32)
    return pl.pallas_call(
        functools.partial(inner_kernel, layers=layers),
        in_specs=[pl.BlockSpec(memory_space=pltpu.HBM)] * 2,
        out_specs=in_vmem(5),
        out_shape=[state, state] + gauge_shapes(layers, planes) + [top],
        scratch_shapes=fetch_scratch(start2, links2) + gauge_scratch(layers, tiles),
        compiler_params=params(),
        cost_estimate=cost(8),
        name="inner",
    )(start2, links2)


def outer_kernel(
    place_ref, lo_ref, hi_ref, table_ref, gauge_ref, a_in, b_in,
    half_ref, keep_ref, give_ref, a_ref, b_ref, pack_ref, *, layers, parts
):
    groups = a_ref.shape[0]
    total = layers + 2 * DEGREE
    planes = table_ref.shape[-1]
    tiles = planes // LANES

    def init(n, _):
        g, x = n // DEGREE, n % DEGREE
        for ref, at in ((lo_ref, x), (hi_ref, x + DEGREE + layers)):

            def source(k, t, ref=ref):
                return ref[x, g, k, :, cols(t)].astype(jnp.float32)

            put(a_ref, g, at, turn(gauge_ref, at, source, False, tiles))
        for at in (x + DEGREE, total - 2 * DEGREE + x):
            a_ref[g, at] = a_in[g, at]
            b_ref[g, at] = b_in[g, at]
        return 0

    lax.fori_loop(0, groups * DEGREE, init, 0)
    for level in range(1, DEGREE):
        src, dst = (a_ref, b_ref) if level % 2 else (b_ref, a_ref)

        def body(n, _, src=src, dst=dst, level=level):
            for at in range(DEGREE):
                for x in (level + at, total - DEGREE - level + at):
                    put(dst, n, x, layer(table_ref, n, x, src, dst, level == 1, tiles))
            return 0

        lax.fori_loop(0, groups, body, 0)
    src, prev = (a_ref, b_ref) if DEGREE % 2 else (b_ref, a_ref)

    def last(n, _):
        g, at = n // (layers // 4), n % (layers // 4)
        for u in range(4):
            x = 4 * at + u
            value = layer(table_ref, g, x + DEGREE, src, prev, False, tiles)
            value = turn(gauge_ref, x + DEGREE, lambda k, t: value[k, t], True, tiles)
            for (k, t), v in value.items():
                rounded = v.astype(jnp.bfloat16)
                half_ref[g, x, k, :, cols(t)] = rounded
                pack_ref[g, k, pl.ds(pl.multiple_of(x * VB, VB), VB), cols(t)] = rounded.astype(
                    jnp.float32
                )
        return 0

    lax.fori_loop(0, groups * (layers // 4), last, 0)

    side, base = place_ref[0], place_ref[1]
    pairs = parts // 2
    width = planes // parts
    for g in range(groups):
        for k in range(6):
            turned = jnp.concatenate([pack_ref[g, k, :, cols(t)].T for t in range(tiles)], axis=0)
            for m in range(pairs):
                near = turned[m * width : (m + 1) * width].astype(jnp.bfloat16)
                far = turned[(pairs + m) * width : (pairs + m + 1) * width].astype(jnp.bfloat16)
                keep_ref[base ^ m, g, k] = jnp.where(side == 0, near, far)
                give_ref[base ^ m, g, k] = jnp.where(side == 0, far, near)


def run_outer(place, lo, hi, table, gauge, a, b, layers, parts):
    groups, total, comps, _, planes = a.shape
    width = planes // parts
    cells = layers * VB
    block = jax.ShapeDtypeStruct((parts // 2, groups, comps, width, cells), jnp.bfloat16)
    half = jax.ShapeDtypeStruct((groups, layers, comps, VB, planes), jnp.bfloat16)
    return pl.pallas_call(
        functools.partial(outer_kernel, layers=layers, parts=parts),
        in_specs=[in_smem()] + in_vmem(6),
        out_specs=in_vmem(3),
        out_shape=[half, block, block],
        scratch_shapes=[
            pltpu.VMEM(a.shape, jnp.float32),
            pltpu.VMEM(a.shape, jnp.float32),
            pltpu.VMEM((groups, comps, cells, planes), jnp.float32),
        ],
        compiler_params=params(),
        cost_estimate=cost(16),
        name="outer",
    )(place, lo, hi, table, gauge, a, b)


def weight_kernel(half_ref, weight_ref):
    groups, layers, _, _, planes = half_ref.shape
    vectors = groups * VB
    for g in range(groups):
        for x in range(layers):
            for part in range(2):
                for c in range(3):
                    for p in range(2):
                        value = half_ref[g, x, (part ^ p) * 3 + c]
                        if p == 1 and part == 1:
                            value = -value
                        weight_ref[
                            pl.ds((x * 2 + p) * vectors + g * VB, VB),
                            pl.ds((part * 3 + c) * planes, planes),
                        ] = value


def run_weights(half):
    groups, layers, comps, _, planes = half.shape
    return pl.pallas_call(
        weight_kernel,
        in_specs=in_vmem(1),
        out_specs=in_vmem(1)[0],
        out_shape=jax.ShapeDtypeStruct((layers * 2 * groups * VB, comps * planes), jnp.bfloat16),
        compiler_params=params(),
        cost_estimate=cost(0.7),
        name="weights",
    )(half)


def corr_kernel(place_ref, stored_ref, weight_ref, out_ref, *, layers):
    span, block = out_ref.shape
    _, comps, _, planes = stored_ref.shape
    rows = jnp.concatenate(
        [stored_ref[:, k].reshape(block * layers, planes) for k in range(comps)], axis=1
    )
    layer_of_row = lax.broadcasted_iota(jnp.int32, (block * layers, LANES), 0) % layers
    layer_of_lane = lax.broadcasted_iota(jnp.int32, (block * layers, LANES), 1) // span
    kept = jnp.zeros((block * layers, LANES), jnp.float32)
    width = min(2 * LANES, weight_ref.shape[0])
    for first in range(0, weight_ref.shape[0], width):
        full = lax.dot_general(
            rows,
            weight_ref[first : first + width, :],
            (((1,), (1,)), ((), ())),
            preferred_element_type=jnp.float32,
        )
        for at in range(0, width, LANES):
            here = layer_of_row == (first + at) // span + layer_of_lane
            kept = jnp.where(here, full[:, at : at + LANES], kept)
    summed = jnp.sum(kept.reshape(block, layers, LANES), axis=1)
    total = summed[:, :span]
    for at in range(span, LANES, span):
        total = total + summed[:, at : at + span]
    out_ref[...] = total.T


def run_corr(place, stored, weights, owners):
    count, comps, layers, planes = stored.shape
    block = count // owners
    span = weights.shape[0] // layers
    grid_spec = pltpu.PrefetchScalarGridSpec(
        num_scalar_prefetch=1,
        grid=(owners,),
        in_specs=[
            pl.BlockSpec((block, comps, layers, planes), lambda g, s: (g, 0, 0, 0)),
            pl.BlockSpec(memory_space=pltpu.VMEM),
        ],
        out_specs=pl.BlockSpec((pl.Squeezed(), span, block), lambda g, s: (g ^ s[2], 0, 0)),
    )
    return pl.pallas_call(
        functools.partial(corr_kernel, layers=layers),
        grid_spec=grid_spec,
        out_shape=jax.ShapeDtypeStruct((owners, span, block), jnp.float32),
        compiler_params=params(40 * 2**20),
        cost_estimate=cost(8),
        name="correlate",
    )(place, stored, weights)


def merge_kernel(keep_ref, got_ref, *out_refs):
    for step, ref in enumerate(out_refs):
        ref[0] = keep_ref[step]
        ref[1] = got_ref[step]


def run_merge(keep, got):
    shape = jax.ShapeDtypeStruct((2,) + keep.shape[1:], keep.dtype)
    return pl.pallas_call(
        merge_kernel,
        in_specs=in_vmem(2),
        out_specs=in_vmem(keep.shape[0]),
        out_shape=[shape] * keep.shape[0],
        compiler_params=params(),
        cost_estimate=cost(0.7),
        name="merge",
    )(keep, got)


def order_kernel(order_ref, *, layers, groups):
    depth = order_ref.shape[0]
    cells = layers * VB
    vectors = groups * VB
    row = lax.broadcasted_iota(jnp.int32, (depth, depth), 0)
    col = lax.broadcasted_iota(jnp.int32, (depth, depth), 1)
    bit, rest = row // (groups * cells), row % (groups * cells)
    group, cell = rest // cells, rest % cells
    wanted = ((cell // VB) * 2 + bit) * vectors + group * VB + cell % VB
    order_ref[...] = (wanted == col).astype(jnp.bfloat16)


def run_order(groups, layers):
    depth = 2 * groups * layers * VB
    return pl.pallas_call(
        functools.partial(order_kernel, layers=layers, groups=groups),
        out_specs=in_vmem(1)[0],
        out_shape=jax.ShapeDtypeStruct((depth, depth), jnp.bfloat16),
        compiler_params=params(),
        cost_estimate=cost(2),
        name="order",
    )()


def arrange_kernel(place_ref, order_ref, *refs, layers, per):
    out_ref = refs[-1]
    groups, comps, width = refs[0].shape[1:4]
    span = 2 * groups * VB
    pieces = []
    for ref in refs[:-1]:
        for h in range(2):
            for pair in range(comps // 2):
                lanes = [ref[h, g, 2 * pair + bit] for bit in range(2) for g in range(groups)]
                pieces.append(jnp.concatenate(lanes, axis=1))
    moved = jnp.dot(
        jnp.concatenate(pieces, axis=0), order_ref[...], preferred_element_type=jnp.float32
    )
    for step in range(len(refs) - 1):
        source = place_ref[3] ^ step
        slice_at, chip = lax.rem(source, per), source // per
        for h in range(2):
            first = (2 * chip + (place_ref[4] ^ h)) * layers
            at = (2 * step + h) * (comps // 2) * width
            for x in range(layers):
                out_ref[slice_at, first + x] = jnp.concatenate(
                    [
                        moved[at + p * width : at + (p + 1) * width, x * span : (x + 1) * span]
                        for p in range(comps // 2)
                    ],
                    axis=1,
                ).astype(jnp.bfloat16)


def run_arrange(place, order, blocks, shape, layers, per):
    return pl.pallas_call(
        functools.partial(arrange_kernel, layers=layers, per=per),
        in_specs=[in_smem()] + in_vmem(1 + len(blocks)),
        out_specs=in_vmem(1)[0],
        out_shape=jax.ShapeDtypeStruct(shape, jnp.bfloat16),
        compiler_params=params(),
        cost_estimate=cost(3),
        name="arrange",
    )(place, order, *blocks)


def shards(start_block, gauge_links, stored_vectors, *, n_tm, n_space):
    _, parts, colours, vectors, layers, planes = start_block.shape
    comps = parts * colours
    tm, space = lax.axis_index("tm"), lax.axis_index("space")
    per = n_tm // n_space
    pairs = n_tm // 2
    groups = vectors // VB

    def base_of(i, j):
        return (j // 2 * per + i % per) ^ (i // per % 2 * per)

    place = jnp.stack(
        [
            space % 2 ^ tm // pairs,
            base_of(tm, space),
            space,
            tm % pairs ^ space % 2 * per,
            tm // pairs ^ space * per // pairs,
        ]
    ).astype(jnp.int32)

    tiles = planes // LANES

    def by_tile(value, *lead):
        value = value.reshape(-1, layers, tiles, LANES)
        return jnp.transpose(value, (0, 2, 1, 3)).reshape(*lead, LANES)

    start2 = by_tile(start_block, comps, vectors * tiles * layers)
    links2 = by_tile(gauge_links, LINK_ROWS * tiles * layers)
    up = [(i, (i + 1) % n_space) for i in range(n_space)]
    down = [((i + 1) % n_space, i) for i in range(n_space)]

    up_links, down_links, up_halo, down_halo = run_pack(start2, links2, layers, tiles)
    lo_links = lax.ppermute(up_links, "space", up)
    hi_links = lax.ppermute(down_links, "space", down)
    lo = lax.ppermute(up_halo, "space", up)
    hi = lax.ppermute(down_halo, "space", down)
    order = run_order(groups, layers)

    a, b, table, gauge, top = run_inner(start2, links2, layers, tiles)
    table, gauge = gauge_halo(top, lo_links, hi_links, table, gauge)
    half, keep, give = run_outer(place, lo, hi, table, gauge, a, b, layers, n_tm)

    weights = run_weights(half)
    got = lax.ppermute(give, "space", [(i, i ^ 1) for i in range(n_space)])
    blocks = run_merge(keep, got)
    stored = stored_vectors.reshape(stored_vectors.shape[1], comps, layers, planes)
    sent = [None] * pairs
    digits = pairs.bit_length() - 1
    for step in sorted(range(pairs), key=lambda n: f"{n:0{digits}b}"[::-1]):
        table_of = []
        for i in range(n_tm):
            for j in range(n_space):
                to = (j % 2 ^ i // pairs) * pairs + (base_of(i, j) ^ step)
                table_of.append((i * n_space + j, to * n_space + i // per))
        sent[step] = lax.ppermute(blocks[step], ("tm", "space"), table_of)
    partial = run_corr(place, stored, weights, n_space)
    partial, *sent[:-1] = lax.optimization_barrier((partial, *sent[:-1]))
    total = partial[0]
    for distance in range(1, n_space):
        partner = [(i, i ^ distance) for i in range(n_space)]
        total = total + lax.ppermute(partial[distance], "space", partner)
    correlations = total.T[None]

    shape = (per, n_space * layers, planes // n_tm, comps * vectors)
    return correlations, run_arrange(place, order, sent, shape, layers, per)


def solution(mesh):
    in_specs = (
        P("tm", None, None, None, "space", None),
        P("tm", None, None, None, None, "space", None),
        P("tm", None, None, None, "space", None),
    )
    out_specs = (P("tm", "space", None), P("space", None, "tm", None))
    body = functools.partial(shards, n_tm=mesh.shape["tm"], n_space=mesh.shape["space"])
    return jax.shard_map(body, mesh=mesh, in_specs=in_specs, out_specs=out_specs, check_vma=False)
```

```python
import functools

import jax
import jax.numpy as jnp
from jax import lax
from jax.experimental import pallas as pl
from jax.experimental.pallas import tpu as pltpu
from jax.sharding import PartitionSpec as P

DEGREE = 4
LZ = 16
LANES = 128
VB = 16

lower_edge = 0.5
upper_edge = 12.5
SCALE = 2.0 / (upper_edge - lower_edge)
OFFSET = (upper_edge + lower_edge) / (upper_edge - lower_edge)

VMEM_LIMIT = 60 * 2**20
LINK_ROWS = 54
LINK_PAD = 56
TABLE_ROWS = 112
GAUGE_ROWS = 24


def params(limit=24 * 2**20):
    return pltpu.CompilerParams(vmem_limit_bytes=limit)


def in_vmem(count):
    return [pl.BlockSpec(memory_space=pltpu.VMEM)] * count


def in_smem():
    return pl.BlockSpec(memory_space=pltpu.SMEM)


def cost(microseconds):
    return pl.CostEstimate(
        flops=1_000_000, bytes_accessed=int(microseconds * 3_000_000), transcendentals=0
    )


def fetch(start_hbm, links_hbm, start_ref, links_ref, sems):
    comps = start_ref.shape[0]
    copies = [pltpu.make_async_copy(links_hbm, links_ref, sems.at[comps])] + [
        pltpu.make_async_copy(start_hbm.at[k], start_ref.at[k], sems.at[k]) for k in range(comps)
    ]
    for copy in copies:
        copy.start()
    return copies


def fetch_scratch(start2, links2):
    return [
        pltpu.VMEM(start2.shape, jnp.float32),
        pltpu.VMEM(links2.shape, jnp.float32),
        pltpu.SemaphoreType.DMA((start2.shape[0] + 1,)),
    ]


def pack_kernel(
    start_hbm, links_hbm, up_links_ref, down_links_ref, up_ref, down_ref,
    start_ref, links_ref, sems, *, layers, tiles
):
    comps, groups = up_ref.shape[2], up_ref.shape[1]
    cells = VB * layers * tiles
    copies = fetch(start_hbm, links_hbm, start_ref, links_ref, sems)
    copies[0].wait()
    for x in range(layers):
        for t in range(tiles):
            rows = links_ref[pl.ds(t * layers + x, LINK_ROWS, stride=tiles * layers), :]
            if x < DEGREE:
                down_links_ref[x, :, cols(t)] = rows.astype(jnp.bfloat16)
            if x >= layers - DEGREE:
                up_links_ref[x - layers + DEGREE, :, cols(t)] = rows.astype(jnp.bfloat16)
    for k in range(comps):
        copies[1 + k].wait()
        for x in range(layers):
            for t in range(tiles):
                for g in range(groups):
                    half = start_ref[
                        k, pl.ds(g * cells + t * layers + x, VB, stride=tiles * layers), :
                    ].astype(jnp.bfloat16)
                    if x < DEGREE:
                        down_ref[x, g, k, :, cols(t)] = half
                    if x >= layers - DEGREE:
                        up_ref[x - layers + DEGREE, g, k, :, cols(t)] = half


def run_pack(start2, links2, layers, tiles):
    comps, rows, _ = start2.shape
    planes = tiles * LANES
    groups = rows // (VB * layers * tiles)
    link = jax.ShapeDtypeStruct((DEGREE, LINK_ROWS, planes), jnp.bfloat16)
    halo = jax.ShapeDtypeStruct((DEGREE, groups, comps, VB, planes), jnp.bfloat16)
    return pl.pallas_call(
        functools.partial(pack_kernel, layers=layers, tiles=tiles),
        in_specs=[pl.BlockSpec(memory_space=pltpu.HBM)] * 2,
        out_specs=in_vmem(4),
        out_shape=[link, link, halo, halo],
        scratch_shapes=fetch_scratch(start2, links2),
        compiler_params=params(VMEM_LIMIT),
        cost_estimate=cost(2.5),
        name="pack",
    )(start2, links2)


def mat_mul(a, b, conj_b=False):
    out_re, out_im = [], []
    for i in range(3):
        for j in range(3):
            re = im = None
            for k in range(3):
                ar, ai = a[0][3 * i + k], a[1][3 * i + k]
                if conj_b:
                    br, bi = b[0][3 * j + k], b[1][3 * j + k]
                    r = ar * br + ai * bi
                    m = ai * br - ar * bi
                else:
                    br, bi = b[0][3 * k + j], b[1][3 * k + j]
                    r = ar * br - ai * bi
                    m = ar * bi + ai * br
                re = r if re is None else re + r
                im = m if im is None else im + m
            out_re.append(re)
            out_im.append(im)
    return out_re, out_im


def rot(v, steps):
    return pltpu.roll(v, steps % LANES, 1)


def shifts(value, masks):
    z_last, z_first, y_low, y_high = masks
    tiles = len(value)
    up = [rot(v, LZ) for v in value]
    down = [rot(v, -LZ) for v in value]
    return (
        [jnp.where(y_low, down[t], down[(t + 1) % tiles]) for t in range(tiles)],
        [jnp.where(y_high, up[t], up[(t - 1) % tiles]) for t in range(tiles)],
        [rot(jnp.where(z_first, up[t], value[t]), -1) for t in range(tiles)],
        [rot(jnp.where(z_last, down[t], value[t]), 1) for t in range(tiles)],
    )


def lane_masks(rows):
    lane = lax.broadcasted_iota(jnp.int32, (rows, LANES), 1)
    return lane % LZ == LZ - 1, lane % LZ == 0, lane < LANES - LZ, lane >= LZ


def cols(t):
    return slice(t * LANES, (t + 1) * LANES)


def rows_at(ref, t, first):
    return (
        [ref[t, pl.ds(first + k, 1), :] for k in range(9)],
        [ref[t, pl.ds(first + 9 + k, 1), :] for k in range(9)],
    )


def put_rows(ref, t, first, g):
    for k in range(9):
        ref[t, pl.ds(first + k, 1), :] = g[0][k]
        ref[t, pl.ds(first + 9 + k, 1), :] = g[1][k]


def unit_rows():
    one = jnp.ones((1, LANES), jnp.float32)
    zero = jnp.zeros((1, LANES), jnp.float32)
    return [one if k % 4 == 0 else zero for k in range(9)], [zero] * 9


def fill_tables(ext_ref, g_ref, t_ref, table_ref, gauge_ref, places):
    tiles = ext_ref.shape[0]
    total = len(places)
    masks = lane_masks(total)

    def column(ref, k, stride):
        return [ref[t, pl.ds(k, total, stride=stride), :] for t in range(tiles)]

    gauge = [column(g_ref, k, GAUGE_ROWS) for k in range(18)]
    for d in (1, 2):
        link = [column(ext_ref, 18 * d + k, LINK_PAD) for k in range(18)]
        ahead = [shifts(v, masks)[2 * (d - 1)] for v in gauge]
        turned = []
        for t in range(tiles):
            here, there, mid = (
                ([v[t] for v in field[:9]], [v[t] for v in field[9:]])
                for field in (gauge, ahead, link)
            )
            turned.append(mat_mul(mat_mul(here, mid), there, conj_b=True))
        base = 54 * (d - 1)
        for k in range(9):
            re, im = [turned[t][0][k] for t in range(tiles)], [turned[t][1][k] for t in range(tiles)]
            back_re, back_im = shifts(re, masks)[2 * d - 1], shifts(im, masks)[2 * d - 1]
            for t in range(tiles):
                for at, value in (
                    (0, re[t]),
                    (9, re[t] + im[t]),
                    (18, im[t] - re[t]),
                    (27, back_re[t]),
                    (36, back_re[t] + back_im[t]),
                    (45, back_im[t] - back_re[t]),
                ):
                    t_ref[t, pl.ds(base + at + k, total, stride=TABLE_ROWS), :] = value
    for n, x in enumerate(places):
        for t in range(tiles):
            table_ref[x, 0:108, cols(t)] = t_ref[t, pl.ds(n * TABLE_ROWS, 108), :]
            gauge_ref[x, 0:18, cols(t)] = g_ref[t, pl.ds(n * GAUGE_ROWS, 18), :]


def gauge_own(links_ref, table_ref, gauge_ref, ext_ref, g_ref, t_ref, layers):
    tiles = ext_ref.shape[0]
    for t in range(tiles):
        for x in range(layers):
            ext_ref[t, pl.ds(x * LINK_PAD, LINK_ROWS), :] = links_ref[
                pl.ds(t * layers + x, LINK_ROWS, stride=tiles * layers), :
            ]
    for t in range(tiles):
        g = unit_rows()
        put_rows(g_ref, t, 0, g)
        for x in range(layers - 1):
            g = mat_mul(g, rows_at(ext_ref, t, x * LINK_PAD))
            put_rows(g_ref, t, (x + 1) * GAUGE_ROWS, g)
    fill_tables(
        ext_ref, g_ref, t_ref, table_ref, gauge_ref, [DEGREE + x for x in range(layers)]
    )


def gauge_halo_kernel(
    top_ref, lo_ref, hi_ref, table_in, gauge_in, table_ref, gauge_ref, ext_ref, g_ref, t_ref
):
    layers = table_ref.shape[0] - 2 * DEGREE
    for x in range(DEGREE, DEGREE + layers):
        table_ref[x] = table_in[x]
        gauge_ref[x] = gauge_in[x]
    tiles = ext_ref.shape[0]
    for t in range(tiles):
        for x in range(DEGREE):
            ext_ref[t, pl.ds(x * LINK_PAD, LINK_ROWS), :] = lo_ref[x, :, cols(t)].astype(jnp.float32)
            ext_ref[t, pl.ds((DEGREE + x) * LINK_PAD, LINK_ROWS), :] = hi_ref[x, :, cols(t)].astype(
                jnp.float32
            )
    for t in range(tiles):
        g = unit_rows()
        for x in range(DEGREE - 1, -1, -1):
            g = mat_mul(g, rows_at(ext_ref, t, x * LINK_PAD), conj_b=True)
            put_rows(g_ref, t, x * GAUGE_ROWS, g)
        top = DEGREE + layers - 1
        g = tuple(
            [gauge_in[top, pl.ds(first + k, 1), cols(t)] for k in range(9)] for first in (0, 9)
        )
        link = tuple(
            [top_ref[pl.ds(first + k, 1), cols(t)] for k in range(9)]
            for first in (0, 9)
        )
        for x in range(DEGREE):
            g = mat_mul(g, link)
            put_rows(g_ref, t, (DEGREE + x) * GAUGE_ROWS, g)
            if x < DEGREE - 1:
                link = rows_at(ext_ref, t, (DEGREE + x) * LINK_PAD)
    places = list(range(DEGREE)) + [DEGREE + layers + x for x in range(DEGREE)]
    fill_tables(ext_ref, g_ref, t_ref, table_ref, gauge_ref, places)


def gauge_scratch(count, tiles):
    return [
        pltpu.VMEM((tiles, count * LINK_PAD, LANES), jnp.float32),
        pltpu.VMEM((tiles, count * GAUGE_ROWS, LANES), jnp.float32),
        pltpu.VMEM((tiles, count * TABLE_ROWS, LANES), jnp.float32),
    ]


def gauge_shapes(layers, planes):
    total = layers + 2 * DEGREE
    return [
        jax.ShapeDtypeStruct((total, TABLE_ROWS, planes), jnp.float32),
        jax.ShapeDtypeStruct((total, GAUGE_ROWS, planes), jnp.float32),
    ]


def gauge_halo(top, lo, hi, table, gauge):
    total, _, planes = table.shape
    return pl.pallas_call(
        gauge_halo_kernel,
        in_specs=in_vmem(5),
        out_specs=in_vmem(2),
        out_shape=gauge_shapes(total - 2 * DEGREE, planes),
        scratch_shapes=gauge_scratch(2 * DEGREE, planes // LANES),
        compiler_params=params(),
        cost_estimate=cost(1.5),
        name="gauge_halo",
    )(top, lo, hi, table, gauge)


def turn(gauge_ref, x, source, adjoint, tiles):
    out = {}
    for t in range(tiles):
        v = [source(k, t) for k in range(6)]
        for i in range(3):
            re = im = None
            for j in range(3):
                k = 3 * j + i if adjoint else 3 * i + j
                a = gauge_ref[x, pl.ds(k, 1), cols(t)]
                b = gauge_ref[x, pl.ds(9 + k, 1), cols(t)]
                if adjoint:
                    r, m = a * v[j] + b * v[3 + j], a * v[3 + j] - b * v[j]
                else:
                    r, m = a * v[j] - b * v[3 + j], a * v[3 + j] + b * v[j]
                re = r if re is None else re + r
                im = m if im is None else im + m
            out[i, t], out[3 + i, t] = re, im
    return out


def layer(table_ref, g, x, src, prev, first, tiles):
    z_last, z_first, y_low, y_high = lane_masks(VB)
    sums = {}

    def add(key, value, minus=False):
        have = sums.get(key)
        if have is None:
            sums[key] = -value if minus else value
        else:
            sums[key] = have - value if minus else have + value

    def hop(t, base, v, adjoint):
        both = [v[j] + v[3 + j] for j in range(3)]
        for j in range(3):
            for i in range(3):
                k = base + (3 * j + i if adjoint else 3 * i + j)
                a = table_ref[x, pl.ds(k, 1), cols(t)]
                p = table_ref[x, pl.ds(k + 9, 1), cols(t)]
                q = table_ref[x, pl.ds(k + 18, 1), cols(t)]
                add((t, 0, i), a * both[j])
                if adjoint:
                    add((t, 1, i), q * v[3 + j], True)
                    add((t, 2, i), p * v[j], True)
                else:
                    add((t, 1, i), p * v[3 + j])
                    add((t, 2, i), q * v[j])

    out = {}
    for t in range(tiles):
        c = {(k, u): src[g, x, k, :, cols(u)] for k in range(6) for u in range(tiles)}
        after, before = (t + 1) % tiles, (t - 1) % tiles
        hop(t, 0, [rot(jnp.where(y_high, c[k, t], c[k, after]), -LZ) for k in range(6)], False)
        hop(t, 27, [rot(jnp.where(y_low, c[k, t], c[k, before]), LZ) for k in range(6)], True)
        hop(
            t, 54,
            [jnp.where(z_last, rot(c[k, t], LZ - 1), rot(c[k, t], -1)) for k in range(6)],
            False,
        )
        hop(
            t, 81,
            [jnp.where(z_first, rot(c[k, t], 1 - LZ), rot(c[k, t], 1)) for k in range(6)],
            True,
        )
        for i in range(3):
            re = sums[t, 0, i] - sums[t, 1, i]
            im = sums[t, 0, i] + sums[t, 2, i]
            for k, h in ((i, re), (3 + i, im)):
                h = h + (src[g, x + 1, k, :, cols(t)] + src[g, x - 1, k, :, cols(t)])
                if first:
                    out[k, t] = (6.0 * SCALE - OFFSET) * c[k, t] - SCALE * h
                else:
                    out[k, t] = (
                        (12.0 * SCALE - 2.0 * OFFSET) * c[k, t]
                        - (2.0 * SCALE) * h
                        - prev[g, x, k, :, cols(t)]
                    )
    return out


def put(ref, g, x, values):
    for (k, t), value in values.items():
        ref[g, x, k, :, cols(t)] = value


def inner_kernel(
    start_hbm, links_hbm, a_ref, b_ref, table_ref, gauge_ref, top_ref,
    start_ref, links_ref, sems, ext_ref, g_ref, t_ref, *, layers
):
    groups = a_ref.shape[0]
    tiles = table_ref.shape[-1] // LANES
    cells = VB * layers * tiles
    copies = fetch(start_hbm, links_hbm, start_ref, links_ref, sems)
    copies[0].wait()
    gauge_own(links_ref, table_ref, gauge_ref, ext_ref, g_ref, t_ref, layers)
    for t in range(tiles):
        top_ref[0:18, cols(t)] = ext_ref[t, pl.ds((layers - 1) * LINK_PAD, 18), :]
    for copy in copies[1:]:
        copy.wait()

    def init(n, _):
        g, x = n // layers, n % layers

        def source(k, t):
            at = g * cells + t * layers + x
            return start_ref[k, pl.ds(at, VB, stride=tiles * layers), :]

        put(a_ref, g, x + DEGREE, turn(gauge_ref, x + DEGREE, source, False, tiles))
        return 0

    lax.fori_loop(0, groups * layers, init, 0)
    for level in range(1, DEGREE):
        src, dst = (a_ref, b_ref) if level % 2 else (b_ref, a_ref)
        pairs = (layers - 2 * level) // 2

        def body(n, _, src=src, dst=dst, level=level, pairs=pairs):
            g, at = n // pairs, n % pairs
            for u in range(2):
                x = DEGREE + level + 2 * at + u
                put(dst, g, x, layer(table_ref, g, x, src, dst, level == 1, tiles))
            return 0

        if pairs > 0:
            lax.fori_loop(0, groups * pairs, body, 0)


def run_inner(start2, links2, layers, tiles):
    comps, rows, _ = start2.shape
    planes = tiles * LANES
    groups = rows // (VB * layers * tiles)
    state = jax.ShapeDtypeStruct((groups, layers + 2 * DEGREE, comps, VB, planes), jnp.float32)
    top = jax.ShapeDtypeStruct((GAUGE_ROWS, planes), jnp.float32)
    return pl.pallas_call(
        functools.partial(inner_kernel, layers=layers),
        in_specs=[pl.BlockSpec(memory_space=pltpu.HBM)] * 2,
        out_specs=in_vmem(5),
        out_shape=[state, state] + gauge_shapes(layers, planes) + [top],
        scratch_shapes=fetch_scratch(start2, links2) + gauge_scratch(layers, tiles),
        compiler_params=params(),
        cost_estimate=cost(8),
        name="inner",
    )(start2, links2)


def outer_kernel(
    place_ref, lo_ref, hi_ref, table_ref, gauge_ref, a_in, b_in,
    half_ref, keep_ref, give_ref, a_ref, b_ref, pack_ref, *, layers, parts
):
    groups = a_ref.shape[0]
    total = layers + 2 * DEGREE
    planes = table_ref.shape[-1]
    tiles = planes // LANES

    def init(n, _):
        g, x = n // DEGREE, n % DEGREE
        for ref, at in ((lo_ref, x), (hi_ref, x + DEGREE + layers)):

            def source(k, t, ref=ref):
                return ref[x, g, k, :, cols(t)].astype(jnp.float32)

            put(a_ref, g, at, turn(gauge_ref, at, source, False, tiles))
        for at in (x + DEGREE, total - 2 * DEGREE + x):
            a_ref[g, at] = a_in[g, at]
            b_ref[g, at] = b_in[g, at]
        return 0

    lax.fori_loop(0, groups * DEGREE, init, 0)
    for level in range(1, DEGREE):
        src, dst = (a_ref, b_ref) if level % 2 else (b_ref, a_ref)

        def body(n, _, src=src, dst=dst, level=level):
            for at in range(DEGREE):
                for x in (level + at, total - DEGREE - level + at):
                    put(dst, n, x, layer(table_ref, n, x, src, dst, level == 1, tiles))
            return 0

        lax.fori_loop(0, groups, body, 0)
    src, prev = (a_ref, b_ref) if DEGREE % 2 else (b_ref, a_ref)

    def last(n, _):
        g = n
        for x in range(layers):
            value = layer(table_ref, g, x + DEGREE, src, prev, False, tiles)
            value = turn(gauge_ref, x + DEGREE, lambda k, t: value[k, t], True, tiles)
            for (k, t), v in value.items():
                rounded = v.astype(jnp.bfloat16)
                half_ref[g, x, k, :, cols(t)] = rounded
                pack_ref[g, k, pl.ds(x * VB, VB), cols(t)] = rounded.astype(
                    jnp.float32
                )
        return 0

    lax.fori_loop(0, groups, last, 0)

    side, base = place_ref[0], place_ref[1]
    pairs = parts // 2
    width = planes // parts
    for g in range(groups):
        for k in range(6):
            turned = jnp.concatenate([pack_ref[g, k, :, cols(t)].T for t in range(tiles)], axis=0)
            for m in range(pairs):
                near = turned[m * width : (m + 1) * width].astype(jnp.bfloat16)
                far = turned[(pairs + m) * width : (pairs + m + 1) * width].astype(jnp.bfloat16)
                keep_ref[base ^ m, g, k] = jnp.where(side == 0, near, far)
                give_ref[base ^ m, g, k] = jnp.where(side == 0, far, near)


def run_outer(place, lo, hi, table, gauge, a, b, layers, parts):
    groups, total, comps, _, planes = a.shape
    width = planes // parts
    cells = layers * VB
    block = jax.ShapeDtypeStruct((parts // 2, groups, comps, width, cells), jnp.bfloat16)
    half = jax.ShapeDtypeStruct((groups, layers, comps, VB, planes), jnp.bfloat16)
    return pl.pallas_call(
        functools.partial(outer_kernel, layers=layers, parts=parts),
        in_specs=[in_smem()] + in_vmem(6),
        out_specs=in_vmem(3),
        out_shape=[half, block, block],
        scratch_shapes=[
            pltpu.VMEM(a.shape, jnp.float32),
            pltpu.VMEM(a.shape, jnp.float32),
            pltpu.VMEM((groups, comps, cells, planes), jnp.float32),
        ],
        compiler_params=params(),
        cost_estimate=cost(16),
        name="outer",
    )(place, lo, hi, table, gauge, a, b)


def weight_kernel(half_ref, weight_ref):
    groups, layers, _, _, planes = half_ref.shape
    vectors = groups * VB
    for g in range(groups):
        for x in range(layers):
            for part in range(2):
                for c in range(3):
                    for p in range(2):
                        value = half_ref[g, x, (part ^ p) * 3 + c]
                        if p == 1 and part == 1:
                            value = -value
                        weight_ref[
                            pl.ds((x * 2 + p) * vectors + g * VB, VB),
                            pl.ds((part * 3 + c) * planes, planes),
                        ] = value


def run_weights(half):
    groups, layers, comps, _, planes = half.shape
    return pl.pallas_call(
        weight_kernel,
        in_specs=in_vmem(1),
        out_specs=in_vmem(1)[0],
        out_shape=jax.ShapeDtypeStruct((layers * 2 * groups * VB, comps * planes), jnp.bfloat16),
        compiler_params=params(),
        cost_estimate=cost(0.7),
        name="weights",
    )(half)


def corr_kernel(place_ref, stored_ref, weight_ref, out_ref, *, layers):
    span, block = out_ref.shape
    _, comps, _, planes = stored_ref.shape
    rows = jnp.concatenate(
        [stored_ref[:, k].reshape(block * layers, planes) for k in range(comps)], axis=1
    )
    layer_of_row = lax.broadcasted_iota(jnp.int32, (block * layers, LANES), 0) % layers
    layer_of_lane = lax.broadcasted_iota(jnp.int32, (block * layers, LANES), 1) // span
    kept = jnp.zeros((block * layers, LANES), jnp.float32)
    width = min(2 * LANES, weight_ref.shape[0])
    for first in range(0, weight_ref.shape[0], width):
        full = lax.dot_general(
            rows,
            weight_ref[first : first + width, :],
            (((1,), (1,)), ((), ())),
            preferred_element_type=jnp.float32,
        )
        for at in range(0, width, LANES):
            here = layer_of_row == (first + at) // span + layer_of_lane
            kept = jnp.where(here, full[:, at : at + LANES], kept)
    summed = jnp.sum(kept.reshape(block, layers, LANES), axis=1)
    total = summed[:, :span]
    for at in range(span, LANES, span):
        total = total + summed[:, at : at + span]
    out_ref[...] = total.T


def run_corr(place, stored, weights, owners):
    count, comps, layers, planes = stored.shape
    block = count // owners
    span = weights.shape[0] // layers
    grid_spec = pltpu.PrefetchScalarGridSpec(
        num_scalar_prefetch=1,
        grid=(owners,),
        in_specs=[
            pl.BlockSpec((block, comps, layers, planes), lambda g, s: (g, 0, 0, 0)),
            pl.BlockSpec(memory_space=pltpu.VMEM),
        ],
        out_specs=pl.BlockSpec((pl.Squeezed(), span, block), lambda g, s: (g ^ s[2], 0, 0)),
    )
    return pl.pallas_call(
        functools.partial(corr_kernel, layers=layers),
        grid_spec=grid_spec,
        out_shape=jax.ShapeDtypeStruct((owners, span, block), jnp.float32),
        compiler_params=params(40 * 2**20),
        cost_estimate=cost(8),
        name="correlate",
    )(place, stored, weights)


def merge_kernel(keep_ref, got_ref, *out_refs):
    for step, ref in enumerate(out_refs):
        ref[0] = keep_ref[step]
        ref[1] = got_ref[step]


def run_merge(keep, got):
    shape = jax.ShapeDtypeStruct((2,) + keep.shape[1:], keep.dtype)
    return pl.pallas_call(
        merge_kernel,
        in_specs=in_vmem(2),
        out_specs=in_vmem(keep.shape[0]),
        out_shape=[shape] * keep.shape[0],
        compiler_params=params(),
        cost_estimate=cost(0.7),
        name="merge",
    )(keep, got)


def order_kernel(order_ref, *, layers, groups):
    depth = order_ref.shape[0]
    cells = layers * VB
    vectors = groups * VB
    row = lax.broadcasted_iota(jnp.int32, (depth, depth), 0)
    col = lax.broadcasted_iota(jnp.int32, (depth, depth), 1)
    bit, rest = row // (groups * cells), row % (groups * cells)
    group, cell = rest // cells, rest % cells
    wanted = ((cell // VB) * 2 + bit) * vectors + group * VB + cell % VB
    order_ref[...] = (wanted == col).astype(jnp.bfloat16)


def run_order(groups, layers):
    depth = 2 * groups * layers * VB
    return pl.pallas_call(
        functools.partial(order_kernel, layers=layers, groups=groups),
        out_specs=in_vmem(1)[0],
        out_shape=jax.ShapeDtypeStruct((depth, depth), jnp.bfloat16),
        compiler_params=params(),
        cost_estimate=cost(2),
        name="order",
    )()


def arrange_kernel(place_ref, order_ref, *refs, layers, per):
    out_ref = refs[-1]
    groups, comps, width = refs[0].shape[1:4]
    span = 2 * groups * VB
    pieces = []
    for ref in refs[:-1]:
        for h in range(2):
            for pair in range(comps // 2):
                lanes = [ref[h, g, 2 * pair + bit] for bit in range(2) for g in range(groups)]
                pieces.append(jnp.concatenate(lanes, axis=1))
    moved = jnp.dot(
        jnp.concatenate(pieces, axis=0), order_ref[...], preferred_element_type=jnp.float32
    )
    for step in range(len(refs) - 1):
        source = place_ref[3] ^ step
        slice_at, chip = lax.rem(source, per), source // per
        for h in range(2):
            first = (2 * chip + (place_ref[4] ^ h)) * layers
            at = (2 * step + h) * (comps // 2) * width
            for x in range(layers):
                out_ref[slice_at, first + x] = jnp.concatenate(
                    [
                        moved[at + p * width : at + (p + 1) * width, x * span : (x + 1) * span]
                        for p in range(comps // 2)
                    ],
                    axis=1,
                ).astype(jnp.bfloat16)


def run_arrange(place, order, blocks, shape, layers, per):
    return pl.pallas_call(
        functools.partial(arrange_kernel, layers=layers, per=per),
        in_specs=[in_smem()] + in_vmem(1 + len(blocks)),
        out_specs=in_vmem(1)[0],
        out_shape=jax.ShapeDtypeStruct(shape, jnp.bfloat16),
        compiler_params=params(),
        cost_estimate=cost(3),
        name="arrange",
    )(place, order, *blocks)


def shards(start_block, gauge_links, stored_vectors, *, n_tm, n_space):
    _, parts, colours, vectors, layers, planes = start_block.shape
    comps = parts * colours
    tm, space = lax.axis_index("tm"), lax.axis_index("space")
    per = n_tm // n_space
    pairs = n_tm // 2
    groups = vectors // VB

    def base_of(i, j):
        return (j // 2 * per + i % per) ^ (i // per % 2 * per)

    place = jnp.stack(
        [
            space % 2 ^ tm // pairs,
            base_of(tm, space),
            space,
            tm % pairs ^ space % 2 * per,
            tm // pairs ^ space * per // pairs,
        ]
    ).astype(jnp.int32)

    tiles = planes // LANES

    def by_tile(value, *lead):
        value = value.reshape(-1, layers, tiles, LANES)
        return jnp.transpose(value, (0, 2, 1, 3)).reshape(*lead, LANES)

    start2 = by_tile(start_block, comps, vectors * tiles * layers)
    links2 = by_tile(gauge_links, LINK_ROWS * tiles * layers)
    up = [(i, (i + 1) % n_space) for i in range(n_space)]
    down = [((i + 1) % n_space, i) for i in range(n_space)]

    up_links, down_links, up_halo, down_halo = run_pack(start2, links2, layers, tiles)
    lo_links = lax.ppermute(up_links, "space", up)
    hi_links = lax.ppermute(down_links, "space", down)
    lo = lax.ppermute(up_halo, "space", up)
    hi = lax.ppermute(down_halo, "space", down)
    order = run_order(groups, layers)

    a, b, table, gauge, top = run_inner(start2, links2, layers, tiles)
    table, gauge = gauge_halo(top, lo_links, hi_links, table, gauge)
    half, keep, give = run_outer(place, lo, hi, table, gauge, a, b, layers, n_tm)

    weights = run_weights(half)
    got = lax.ppermute(give, "space", [(i, i ^ 1) for i in range(n_space)])
    blocks = run_merge(keep, got)
    stored = stored_vectors.reshape(stored_vectors.shape[1], comps, layers, planes)
    sent = [None] * pairs
    digits = pairs.bit_length() - 1
    for step in sorted(range(pairs), key=lambda n: f"{n:0{digits}b}"[::-1]):
        table_of = []
        for i in range(n_tm):
            for j in range(n_space):
                to = (j % 2 ^ i // pairs) * pairs + (base_of(i, j) ^ step)
                table_of.append((i * n_space + j, to * n_space + i // per))
        sent[step] = lax.ppermute(blocks[step], ("tm", "space"), table_of)
    partial = run_corr(place, stored, weights, n_space)
    partial, *sent[:-1] = lax.optimization_barrier((partial, *sent[:-1]))
    total = partial[0]
    for distance in range(1, n_space):
        partner = [(i, i ^ distance) for i in range(n_space)]
        total = total + lax.ppermute(partial[distance], "space", partner)
    correlations = total.T[None]

    shape = (per, n_space * layers, planes // n_tm, comps * vectors)
    return correlations, run_arrange(place, order, sent, shape, layers, per)


def solution(mesh):
    in_specs = (
        P("tm", None, None, None, "space", None),
        P("tm", None, None, None, None, "space", None),
        P("tm", None, None, None, "space", None),
    )
    out_specs = (P("tm", "space", None), P("space", None, "tm", None))
    body = functools.partial(shards, n_tm=mesh.shape["tm"], n_space=mesh.shape["space"])
    return jax.shard_map(body, mesh=mesh, in_specs=in_specs, out_specs=out_specs, check_vma=False)
```
